128 devices in a mesh: ctx: 16 (over z, x_lo, core), fsdp: 8 (over x_hi, y).
Axes of the slice: x: 4 (x_hi: 2, x_lo: 2; x = x_hi * 2 + x_lo), y: 4, z: 4, core: 2. Of those that a mesh axis runs over, the one named last changes fastest.
Arguments:
- inputs: bfloat16 [8192, 5376], P('ctx'), may hold values from -400 to 400
- output_cotangent: bfloat16 [8192, 4096], P('ctx', 'fsdp'), may hold values from -96 to 96
- w_query: bfloat16 [5376, 4096], P('ctx', 'fsdp'), may hold values from -0.078125 to 0.078125
- key_projection: bfloat16 [5376, 2048], P('ctx', 'fsdp'), may hold values from -0.078125 to 0.078125
- value_projection: bfloat16 [5376, 2048], P('ctx', 'fsdp'), may hold values from -0.078125 to 0.078125
- norm_gain: float32 [5376], replicated, may hold values from 0.25 to 1.75
- q_gain: float32 [128], replicated, may hold values from 0.25 to 1.75
- key_norm_gain: float32 [128], replicated, may hold values from 0.25 to 1.75
- half_lengths: int32 [4], replicated, may hold values from 1 to 6144, 8192 in all
Outputs:
- grad_inputs: bfloat16 [8192, 5376], P('ctx', 'fsdp')
- grad_w_query: bfloat16 [5376, 4096], P('ctx', 'fsdp')
- grad_w_key: bfloat16 [5376, 2048], P('ctx', 'fsdp')
- grad_w_value: bfloat16 [5376, 2048], P('ctx', 'fsdp')
- grad_norm_gain: float32 [5376], P(('fsdp', 'ctx'))
- grad_q_gain: float32 [128], replicated
- grad_k_gain: float32 [128], replicated
- norm_row_dots: float32 [8192], P('ctx')
The draws below stay inside these ranges and needn't reach their ends.
Inputs may be any that keep to these rules, and one draw needn't show every extreme that they name: `half_lengths`: the halves add up to 8192 tokens, and the longest holds exactly 6144.
All inputs are finite; a program needn't handle non-finite values.
Results may differ from the reference program's by a relative error of at most 0.035.
Values may be sent and summed in bfloat16 or wider, within the bound.
A program may use at most 128 MiB of HBM per device.

```python
import math
import jax
import jax.numpy as jnp
import numpy as np
from jax import lax

MODEL_DIMENSION = 5376
QUERY_HEADS = 32
KEY_VALUE_HEADS = 16
HEAD_SIZE = 128
WIN = 1024
TOK_DEV = 512
PACKED_TOKENS = 8192
SEGS = 4
LONGEST = 6144
REACH = 2
N_FSDP = 8


def draw_inputs(key, part):
    keys_list = jax.random.split(key, 3)
    row_scale = jnp.exp(jax.random.uniform(keys_list[0], (PACKED_TOKENS, 1), jnp.float32, 0.0, math.log(10.0)))
    rough_cols = jnp.exp(jax.random.uniform(keys_list[1], (1, MODEL_DIMENSION), jnp.float32, 0.0, math.log(3.0)))
    feature_frac = lax_free_ramp(MODEL_DIMENSION)
    low_end = 0.1
    gauss_base = jax.random.normal(keys_list[2], (PACKED_TOKENS, MODEL_DIMENSION), jnp.float32)
    rising = jnp.exp(math.log(low_end) + (math.log(3.0) - math.log(low_end)) * feature_frac)
    col_scale = rising * rough_cols
    gauss_base = jnp.clip(gauss_base, -4.0, 4.0)
    return (gauss_base * row_scale * col_scale).astype(jnp.bfloat16)


def lax_free_ramp(width_count):
    return (jnp.arange(width_count, dtype=jnp.float32) / float(max(width_count - 1, 1)))[None, :]


def shard_levels(key, shape, cuts, smallest, high):
    factor_of = 1.0
    for axis_at, blocks in cuts:
        draws = jax.random.uniform(jax.random.fold_in(jax.random.fold_in(key, 6), axis_at), (blocks,), jnp.float32, smallest / len(cuts), high / len(cuts))
        factor_of = factor_of * jnp.repeat(jnp.exp(draws), shape[axis_at] // blocks).reshape((-1,) + (1,) * (len(shape) - 1 - axis_at))
    return factor_of


def profile(count, total, most, lean):
    portions = [(1 << 20) // math.isqrt(rank ** lean) + 1 for rank in range(2, count + 1)]
    surplus, holding = total - most - (count - 1), [1] * (count - 1)
    while surplus > 0:
        candidates = [i for i in range(count - 1) if holding[i] < most]
        mass, budget = sum([portions[i] for i in candidates]), surplus
        for i in candidates:
            addition = min(most - holding[i], max(1, budget * portions[i] // mass), surplus)
            holding[i] = holding[i] + addition
            surplus = surplus - addition
    return np.array([most] + holding)


def uneven_parts(rng, count, total, reach, slope):
    if count == 2:
        one = jax.random.randint(rng, (), max(1, total - reach), min(reach, total - 1) + 1)
        return jnp.stack([one, total - one])
    sizes = jnp.asarray(profile(count, total, reach, slope), jnp.int32)
    couples = (count - 1) // 2
    source_of, sink = sizes[1:1 + 2 * couples:2], sizes[2:2 + 2 * couples:2]
    room = jnp.minimum(source_of - 1, reach - sink)
    shifted = jax.random.randint(jax.random.fold_in(rng, 1), (couples,), 0, 1 << 20) % (room + 1)
    sizes = sizes.at[1:1 + 2 * couples:2].set(source_of - shifted).at[2:2 + 2 * couples:2].set(sink + shifted)
    return sizes[jax.random.permutation(jax.random.fold_in(rng, 2), count)]


def centred(key, extent, spread, most, cuts=(), held_as=jnp.bfloat16):
    gain = shard_levels(key, extent, cuts, -0.22, 0.18) if cuts else 1.0
    result = jax.random.normal(key, extent, jnp.float32) * spread * gain
    return jnp.minimum(jnp.maximum(result, -most), most).astype(held_as)


def setup_inputs(seed: int = 0) -> dict:
    splits = jax.random.split(jax.random.key(seed), 10)
    inputs = draw_inputs(jax.random.fold_in(splits[9], 71), 0)
    output_cotangent = centred(splits[1], (PACKED_TOKENS, QUERY_HEADS * HEAD_SIZE), 16.0, 96.0, ((0, 16), (1, 8)))
    w_query = centred(splits[2], (MODEL_DIMENSION, QUERY_HEADS * HEAD_SIZE), MODEL_DIMENSION ** -0.5, 0.078125, ((0, 16), (1, 8)))
    key_projection = centred(splits[3], (MODEL_DIMENSION, KEY_VALUE_HEADS * HEAD_SIZE), MODEL_DIMENSION ** -0.5, 0.078125, ((0, 16), (1, 8)))
    value_projection = centred(splits[4], (MODEL_DIMENSION, KEY_VALUE_HEADS * HEAD_SIZE), MODEL_DIMENSION ** -0.5, 0.078125, ((0, 16), (1, 8)))
    norm_gain = jnp.clip(1.0 + 0.15 * jax.random.normal(splits[5], (MODEL_DIMENSION,), jnp.float32), 0.25, 1.75)
    q_gain = jnp.clip(1.0 + 0.15 * jax.random.normal(splits[6], (HEAD_SIZE,), jnp.float32), 0.25, 1.75)
    key_norm_gain = jnp.clip(1.0 + 0.15 * jax.random.normal(splits[7], (HEAD_SIZE,), jnp.float32), 0.25, 1.75)
    half_lengths = uneven_parts(splits[8], SEGS, PACKED_TOKENS, LONGEST, 2).astype(jnp.int32)
    return {"inputs": inputs, "output_cotangent": output_cotangent, "w_query": w_query, "key_projection": key_projection, "value_projection": value_projection, "norm_gain": norm_gain, "q_gain": q_gain, "key_norm_gain": key_norm_gain, "half_lengths": half_lengths}


epsilon = 1e-06
query_scale = 168.0 ** (-0.5)

def round_half(value_rows):
    return lax.optimization_barrier(value_rows.astype(jnp.bfloat16)).astype(jnp.float32)

def segment_of(half_lengths, positions):
    segment_ends = jnp.cumsum(half_lengths).astype(jnp.int32)
    return lax.optimization_barrier(jnp.sum((segment_ends[None, :] <= positions[:, None]).astype(jnp.int32), axis=1)).astype(jnp.int32)

def head_normalize(projected, head_count):
    shaped = projected.reshape(projected.shape[0], head_count, HEAD_SIZE)
    inverse = lax.rsqrt(lax.optimization_barrier(jnp.mean(shaped * shaped, axis=2, keepdims=True)) + epsilon)
    return (shaped * inverse, inverse)

def head_normalize_backward(upstream_grad, normal_part, inverse, gain_vector):
    upstream = upstream_grad * gain_vector
    return inverse * (upstream - normal_part * lax.optimization_barrier(jnp.mean(upstream * normal_part, axis=2, keepdims=True)))

def reference(inputs, output_cotangent, w_query, key_projection, value_projection, norm_gain, q_gain, key_norm_gain, half_lengths):
    queries_per_group = QUERY_HEADS // KEY_VALUE_HEADS
    window_reach_rows = REACH * TOK_DEV
    span_rows = window_reach_rows + TOK_DEV
    grad_scale = float(PACKED_TOKENS) ** (-0.5)
    widened = inputs.astype(jnp.float32)
    inv_rms = lax.rsqrt(lax.optimization_barrier(jnp.mean(widened * widened, axis=1, keepdims=True)) + epsilon)
    x_hat = widened * inv_rms
    normed = (x_hat * norm_gain).astype(jnp.bfloat16)
    q_raw = jnp.dot(normed, w_query, preferred_element_type=jnp.float32)
    key_unnormed = jnp.dot(normed, key_projection, preferred_element_type=jnp.float32)
    value_rows = jnp.dot(normed, value_projection, preferred_element_type=jnp.float32).astype(jnp.bfloat16)
    query_normalized, q_inverse = head_normalize(q_raw, QUERY_HEADS)
    key_normalized, key_inverse_rms = head_normalize(key_unnormed, KEY_VALUE_HEADS)
    query_multiplier = q_gain * query_scale
    query_rows = (query_normalized * query_multiplier).astype(jnp.bfloat16).reshape(PACKED_TOKENS, KEY_VALUE_HEADS, queries_per_group, HEAD_SIZE)
    key_rows = (key_normalized * key_norm_gain).astype(jnp.bfloat16)
    per_head_grads = output_cotangent.reshape(PACKED_TOKENS, KEY_VALUE_HEADS, queries_per_group, HEAD_SIZE)
    segments = segment_of(half_lengths, lax.iota(jnp.int32, PACKED_TOKENS))
    key_rows_padded = jnp.concatenate([jnp.zeros((window_reach_rows, KEY_VALUE_HEADS, HEAD_SIZE), jnp.bfloat16), key_rows], axis=0)
    value_rows_padded = jnp.concatenate([jnp.zeros((window_reach_rows, KEY_VALUE_HEADS, HEAD_SIZE), jnp.bfloat16), value_rows.reshape(PACKED_TOKENS, KEY_VALUE_HEADS, HEAD_SIZE)], axis=0)
    padded_segments = jnp.concatenate([jnp.zeros((window_reach_rows,), jnp.int32), segments], axis=0)

    def one_block(carry, block_index):
        acc_keys, acc_values = carry
        first_row = (block_index * TOK_DEV).astype(jnp.int32)
        block_q = lax.dynamic_slice_in_dim(query_rows, first_row, TOK_DEV, 0).astype(jnp.float32)
        block_grad = lax.dynamic_slice_in_dim(per_head_grads, first_row, TOK_DEV, 0).astype(jnp.float32)
        block_keys = lax.dynamic_slice_in_dim(key_rows_padded, first_row, span_rows, 0).astype(jnp.float32)
        block_values = lax.dynamic_slice_in_dim(value_rows_padded, first_row, span_rows, 0).astype(jnp.float32)
        query_pos = first_row + lax.iota(jnp.int32, TOK_DEV)
        key_pos = first_row - window_reach_rows + lax.iota(jnp.int32, span_rows)
        query_seg = lax.dynamic_slice_in_dim(segments, first_row, TOK_DEV, 0)
        key_seg = lax.dynamic_slice_in_dim(padded_segments, first_row, span_rows, 0)
        distance = query_pos[:, None] - key_pos[None, :]
        allowed = (query_seg[:, None] == key_seg[None, :]) & (distance >= 0) & (distance < WIN) & (key_pos[None, :] >= 0)
        scores = jnp.einsum('ikgd,jkd->kgij', block_q, block_keys)
        weights = jnp.where(allowed, jnp.exp(scores), 0.0)
        totals = lax.optimization_barrier(jnp.sum(weights, axis=3))
        numer = jnp.einsum('kgij,jkd->ikgd', round_half(weights), block_values)
        attn_out = numer / jnp.transpose(totals, (2, 0, 1))[..., None]
        delta = lax.optimization_barrier(jnp.sum(block_grad * attn_out, axis=3))
        probs = weights / totals[..., None]
        d_probs = jnp.einsum('ikgd,jkd->kgij', block_grad, block_values)
        d_scores = round_half(probs * (d_probs - jnp.transpose(delta, (1, 2, 0))[..., None]))
        d_query = jnp.einsum('kgij,jkd->ikgd', d_scores, block_keys)
        d_key = jnp.einsum('kgij,ikgd->jkd', d_scores, block_q)
        d_value = jnp.einsum('kgij,ikgd->jkd', round_half(probs), block_grad)
        acc_keys = lax.dynamic_update_slice_in_dim(acc_keys, lax.dynamic_slice_in_dim(acc_keys, first_row, span_rows, 0) + d_key, first_row, 0)
        acc_values = lax.dynamic_update_slice_in_dim(acc_values, lax.dynamic_slice_in_dim(acc_values, first_row, span_rows, 0) + d_value, first_row, 0)
        return ((acc_keys, acc_values), d_query)
    zeroed_accumulator = jnp.zeros((window_reach_rows + PACKED_TOKENS, KEY_VALUE_HEADS, HEAD_SIZE), jnp.float32)
    carried, d_query_blocks = lax.scan(one_block, (zeroed_accumulator, zeroed_accumulator), jnp.arange(PACKED_TOKENS // TOK_DEV, dtype=jnp.int32))
    d_queries = d_query_blocks.reshape(PACKED_TOKENS, QUERY_HEADS, HEAD_SIZE)
    key_grads = carried[0][window_reach_rows:]
    value_grads = carried[1][window_reach_rows:]
    dq16 = head_normalize_backward(d_queries, query_normalized, q_inverse, query_multiplier).reshape(PACKED_TOKENS, QUERY_HEADS * HEAD_SIZE).astype(jnp.bfloat16)
    key_grads_half16 = head_normalize_backward(key_grads, key_normalized, key_inverse_rms, key_norm_gain).reshape(PACKED_TOKENS, KEY_VALUE_HEADS * HEAD_SIZE).astype(jnp.bfloat16)
    value_grads_half16 = value_grads.reshape(PACKED_TOKENS, KEY_VALUE_HEADS * HEAD_SIZE).astype(jnp.bfloat16)
    q_group = QUERY_HEADS * HEAD_SIZE // N_FSDP
    key_value_group = KEY_VALUE_HEADS * HEAD_SIZE // N_FSDP
    d_normed = jnp.zeros((PACKED_TOKENS, MODEL_DIMENSION), jnp.float32)
    for group_index in range(N_FSDP):
        q_cols = slice(group_index * q_group, (group_index + 1) * q_group)
        kv_cols = slice(group_index * key_value_group, (group_index + 1) * key_value_group)
        term = jnp.dot(dq16[:, q_cols], w_query[:, q_cols].T, preferred_element_type=jnp.float32)
        term = term + jnp.dot(key_grads_half16[:, kv_cols], key_projection[:, kv_cols].T, preferred_element_type=jnp.float32)
        term = term + jnp.dot(value_grads_half16[:, kv_cols], value_projection[:, kv_cols].T, preferred_element_type=jnp.float32)
        d_normed = d_normed + round_half(term)
    upstream = d_normed * norm_gain
    row_dot = lax.optimization_barrier(jnp.sum(upstream * x_hat, axis=1, keepdims=True))
    grad_inputs = (inv_rms * (upstream - x_hat * row_dot / MODEL_DIMENSION)).astype(jnp.bfloat16)
    norm_row_dots = row_dot[:, 0] * float(MODEL_DIMENSION) ** (-0.5)

    def shard_grads(carry, shard_index):
        first_row = (shard_index * TOK_DEV).astype(jnp.int32)
        normed_block = lax.dynamic_slice_in_dim(normed, first_row, TOK_DEV, 0)
        query_term = round_half(grad_scale * jnp.dot(normed_block.T, lax.dynamic_slice_in_dim(dq16, first_row, TOK_DEV, 0), preferred_element_type=jnp.float32))
        key_term = round_half(grad_scale * jnp.dot(normed_block.T, lax.dynamic_slice_in_dim(key_grads_half16, first_row, TOK_DEV, 0), preferred_element_type=jnp.float32))
        value_term = round_half(grad_scale * jnp.dot(normed_block.T, lax.dynamic_slice_in_dim(value_grads_half16, first_row, TOK_DEV, 0), preferred_element_type=jnp.float32))
        gain_term = round_half(grad_scale * lax.optimization_barrier(jnp.sum(lax.dynamic_slice_in_dim(d_normed, first_row, TOK_DEV, 0) * lax.dynamic_slice_in_dim(x_hat, first_row, TOK_DEV, 0), axis=0)))
        return ((carry[0] + query_term, carry[1] + key_term, carry[2] + value_term, carry[3] + gain_term), None)
    initial_sums = (jnp.zeros((MODEL_DIMENSION, QUERY_HEADS * HEAD_SIZE), jnp.float32), jnp.zeros((MODEL_DIMENSION, KEY_VALUE_HEADS * HEAD_SIZE), jnp.float32), jnp.zeros((MODEL_DIMENSION, KEY_VALUE_HEADS * HEAD_SIZE), jnp.float32), jnp.zeros((MODEL_DIMENSION,), jnp.float32))
    sums, unused = lax.scan(shard_grads, initial_sums, jnp.arange(PACKED_TOKENS // TOK_DEV, dtype=jnp.int32))
    grad_q_gain = grad_scale * lax.optimization_barrier(jnp.sum(d_queries * query_normalized * query_scale, axis=(0, 1)))
    grad_k_gain = grad_scale * lax.optimization_barrier(jnp.sum(key_grads * key_normalized, axis=(0, 1)))
    return (grad_inputs, sums[0].astype(jnp.bfloat16), sums[1].astype(jnp.bfloat16), sums[2].astype(jnp.bfloat16), sums[3], grad_q_gain, grad_k_gain, norm_row_dots)
```

```python
import jax
import jax.numpy as jnp
from jax import lax
from jax.sharding import PartitionSpec as P

WIN = 1024
REACH = 2


epsilon = 1e-06
query_scale = 168.0 ** (-0.5)


def from_behind(value, axis, steps):
    count = lax.axis_size(axis)
    initial, last = (max(0, -steps), min(count, count - steps))
    return lax.ppermute(value, axis, [(source, source + steps) for source in range(initial, last)])


def head_normalize(projected, head_count, head_dim):
    shaped = projected.reshape(projected.shape[0], head_count, head_dim)
    inverse = lax.rsqrt(jnp.mean(shaped * shaped, axis=2, keepdims=True) + epsilon)
    return (shaped * inverse, inverse)


def head_normalize_backward(upstream_grad, normal_part, inverse, gain_vector):
    upstream = upstream_grad * gain_vector
    return inverse * (
        upstream - normal_part * jnp.mean(upstream * normal_part, axis=2, keepdims=True)
    )


def on_device(
    inputs,
    output_cotangent,
    w_query,
    key_projection,
    value_projection,
    norm_gain,
    q_gain,
    key_norm_gain,
    half_lengths,
):
    tokens = inputs.shape[0]
    model_width = inputs.shape[1]
    head_dim = q_gain.shape[0]
    q_cols = w_query.shape[1]
    kv_cols = key_projection.shape[1]
    q_heads = q_cols // head_dim
    kv_heads = kv_cols // head_dim
    queries_per_group = q_heads // kv_heads
    ctx_count = lax.axis_size("ctx")
    ctx_index = lax.axis_index("ctx")
    first_row = ctx_index * tokens
    grad_scale = float(tokens * ctx_count) ** (-0.5)
    contract_cols = (((1,), (1,)), ((), ()))
    contract_rows = (((0,), (0,)), ((), ()))
    widened = inputs.astype(jnp.float32)
    inv_rms = lax.rsqrt(jnp.mean(widened * widened, axis=1, keepdims=True) + epsilon)
    x_hat = widened * inv_rms
    normed = (x_hat * norm_gain).astype(jnp.bfloat16)
    stacked = jnp.concatenate([w_query, key_projection, value_projection], axis=1)
    projected = jnp.dot(
        normed,
        lax.all_gather(stacked, "ctx", axis=0, tiled=True),
        preferred_element_type=jnp.float32,
    )
    q_raw = projected[:, :q_cols]
    key_unnormed = projected[:, q_cols : q_cols + kv_cols]
    value_rows = projected[:, q_cols + kv_cols :].astype(jnp.bfloat16)
    query_normalized, q_inverse = head_normalize(q_raw, q_heads, head_dim)
    key_normalized, key_inverse_rms = head_normalize(key_unnormed, kv_heads, head_dim)
    query_multiplier = q_gain * query_scale
    query_rows = (
        (query_normalized * query_multiplier)
        .astype(jnp.bfloat16)
        .reshape(tokens, kv_heads, queries_per_group, head_dim)
    )
    key_rows = (key_normalized * key_norm_gain).astype(jnp.bfloat16)
    per_head_grads = output_cotangent.reshape(tokens, kv_heads, queries_per_group, head_dim)
    packed_kv = jnp.concatenate([key_rows.reshape(tokens, kv_cols), value_rows], axis=1)
    remote = [from_behind(packed_kv, "ctx", offset) for offset in range(1, REACH + 1)]
    key_tiles = [packed_kv] + remote
    halves = half_lengths.shape[0]
    upto = lax.iota(jnp.int32, halves)[None, :] <= lax.iota(jnp.int32, halves)[:, None]
    segment_ends = jnp.sum(jnp.where(upto, half_lengths[None, :], 0), axis=1)
    local_rows = lax.iota(jnp.int32, tokens)

    def segment_of(start_row):
        positions = start_row + local_rows
        return jnp.sum((segment_ends[None, :] <= positions[:, None]).astype(jnp.int32), axis=1)

    query_pos = first_row + local_rows
    query_seg = segment_of(first_row)

    def split_tile(key_tile):
        tile_keys = key_tile[:, :kv_cols].reshape(tokens, kv_heads, head_dim)
        tile_values = key_tile[:, kv_cols:].reshape(tokens, kv_heads, head_dim)
        return (tile_keys, tile_values)

    def first_pass(key_tile, allowed):
        tile_keys, tile_values = split_tile(key_tile)
        scores = jnp.einsum(
            "ikgd,jkd->kgij", query_rows, tile_keys, preferred_element_type=jnp.float32
        )
        weights = jnp.where(allowed, jnp.exp(scores), 0.0)
        numer = jnp.einsum(
            "kgij,jkd->ikgd",
            weights.astype(jnp.bfloat16),
            tile_values,
            preferred_element_type=jnp.float32,
        )
        return (jnp.sum(weights, axis=3), numer, weights)

    def skip_first(key_tile, allowed):
        return (
            jnp.zeros((kv_heads, queries_per_group, tokens), jnp.float32),
            jnp.zeros((tokens, kv_heads, queries_per_group, head_dim), jnp.float32),
            jnp.zeros((kv_heads, queries_per_group, tokens, tokens), jnp.float32),
        )

    totals = jnp.zeros((kv_heads, queries_per_group, tokens), jnp.float32)
    numer_sum = jnp.zeros((tokens, kv_heads, queries_per_group, head_dim), jnp.float32)
    tile_weights = []
    tile_active = []
    for offset, key_tile in enumerate(key_tiles):
        key_start = first_row - offset * tokens
        key_pos = key_start + local_rows
        key_seg = segment_of(key_start)
        distance = query_pos[:, None] - key_pos[None, :]
        allowed = (
            (query_seg[:, None] == key_seg[None, :])
            & (distance >= 0)
            & (distance < WIN)
            & (key_pos[None, :] >= 0)
        )
        active = (key_start + tokens > 0) & (key_seg[tokens - 1] >= query_seg[0])
        part_totals, part_numer, weights = lax.cond(
            active, first_pass, skip_first, key_tile, allowed
        )
        totals = totals + part_totals
        numer_sum = numer_sum + part_numer
        tile_weights.append(weights)
        tile_active.append(active)
    attn_out = numer_sum / jnp.transpose(totals, (2, 0, 1))[..., None]
    delta_rows = jnp.transpose(
        jnp.sum(per_head_grads.astype(jnp.float32) * attn_out, axis=3), (1, 2, 0)
    )

    def second_pass(key_tile, weights):
        tile_keys, tile_values = split_tile(key_tile)
        probs = weights / totals[..., None]
        d_probs = jnp.einsum(
            "ikgd,jkd->kgij", per_head_grads, tile_values, preferred_element_type=jnp.float32
        )
        d_scores = (probs * (d_probs - delta_rows[..., None])).astype(jnp.bfloat16)
        d_query = jnp.einsum(
            "kgij,jkd->ikgd", d_scores, tile_keys, preferred_element_type=jnp.float32
        )
        d_key = jnp.einsum(
            "kgij,ikgd->jkd", d_scores, query_rows, preferred_element_type=jnp.float32
        )
        d_value = jnp.einsum(
            "kgij,ikgd->jkd",
            probs.astype(jnp.bfloat16),
            per_head_grads,
            preferred_element_type=jnp.float32,
        )
        return (
            d_query,
            jnp.concatenate(
                [d_key.reshape(tokens, kv_cols), d_value.reshape(tokens, kv_cols)], axis=1
            ),
        )

    def skip_second(key_tile, weights):
        return (
            jnp.zeros((tokens, kv_heads, queries_per_group, head_dim), jnp.float32),
            jnp.zeros((tokens, 2 * kv_cols), jnp.float32),
        )

    d_query_sum = jnp.zeros((tokens, kv_heads, queries_per_group, head_dim), jnp.float32)
    kv_grad_parts = []
    for offset, key_tile in enumerate(key_tiles):
        d_query, kv_grad = lax.cond(
            tile_active[offset], second_pass, skip_second, key_tile, tile_weights[offset]
        )
        d_query_sum = d_query_sum + d_query
        kv_grad_parts.append(kv_grad)
    kv_grad_total = kv_grad_parts[0]
    for offset in range(1, REACH + 1):
        kv_grad_total = kv_grad_total + from_behind(
            kv_grad_parts[offset].astype(jnp.bfloat16), "ctx", -offset
        ).astype(jnp.float32)
    d_queries = d_query_sum.reshape(tokens, q_heads, head_dim)
    key_grads = kv_grad_total[:, :kv_cols].reshape(tokens, kv_heads, head_dim)
    dq16 = (
        head_normalize_backward(d_queries, query_normalized, q_inverse, query_multiplier)
        .reshape(tokens, q_cols)
        .astype(jnp.bfloat16)
    )
    key_grads_half16 = (
        head_normalize_backward(key_grads, key_normalized, key_inverse_rms, key_norm_gain)
        .reshape(tokens, kv_cols)
        .astype(jnp.bfloat16)
    )
    value_grads_half16 = kv_grad_total[:, kv_cols:].astype(jnp.bfloat16)
    d_stacked = jnp.concatenate([dq16, key_grads_half16, value_grads_half16], axis=1)
    head_part = lax.dot_general(
        d_stacked,
        lax.all_gather(stacked, "ctx", axis=0, tiled=True),
        contract_cols,
        preferred_element_type=jnp.float32,
    )
    fsdp_index = lax.axis_index("fsdp")
    features = model_width // lax.axis_size("fsdp")
    hat_mine = lax.dynamic_slice_in_dim(x_hat, fsdp_index * features, features, 1)
    gain_mine = lax.dynamic_slice_in_dim(norm_gain, fsdp_index * features, features, 0)
    d_mine = lax.psum_scatter(
        head_part.astype(jnp.bfloat16), "fsdp", scatter_dimension=1, tiled=True
    ).astype(jnp.float32)
    upstream = d_mine * gain_mine
    row_dot = lax.psum(jnp.sum(upstream * hat_mine, axis=1, keepdims=True), "fsdp")
    grad_inputs = (inv_rms * (upstream - hat_mine * row_dot / model_width)).astype(jnp.bfloat16)
    norm_row_dots = row_dot[:, 0] * float(model_width) ** (-0.5)
    gain_term = grad_scale * jnp.sum(d_mine * hat_mine, axis=0)
    weight_term = grad_scale * lax.dot_general(
        normed, d_stacked, contract_rows, preferred_element_type=jnp.float32
    )
    weight_sum, gain_sum = (
        lax.psum_scatter(
            weight_term.astype(jnp.bfloat16), "ctx", scatter_dimension=0, tiled=True
        ).astype(jnp.float32),
        lax.psum_scatter(
            gain_term.astype(jnp.bfloat16), "ctx", scatter_dimension=0, tiled=True
        ).astype(jnp.float32),
    )
    weight_sum = weight_sum.astype(jnp.bfloat16)
    q_term = grad_scale * jnp.sum(d_queries * query_normalized * query_scale, axis=(0, 1))
    k_term = grad_scale * jnp.sum(key_grads * key_normalized, axis=(0, 1))
    grad_q_gain, grad_k_gain = lax.psum((q_term, k_term), ("ctx", "fsdp"))
    return (
        grad_inputs,
        weight_sum[:, :q_cols],
        weight_sum[:, q_cols : q_cols + kv_cols],
        weight_sum[:, q_cols + kv_cols :],
        gain_sum,
        grad_q_gain,
        grad_k_gain,
        norm_row_dots,
    )


def solution(mesh):
    placed = (
        P("ctx", None),
        P("ctx", "fsdp"),
        P("ctx", "fsdp"),
        P("ctx", "fsdp"),
        P("ctx", "fsdp"),
        P(),
        P(),
        P(),
        P(),
    )
    return jax.shard_map(
        on_device,
        mesh=mesh,
        in_specs=placed,
        out_specs=(
            P("ctx", "fsdp"),
            P("ctx", "fsdp"),
            P("ctx", "fsdp"),
            P("ctx", "fsdp"),
            P(("fsdp", "ctx")),
            P(),
            P(),
            P("ctx"),
        ),
        check_vma=False,
    )
```

```python
import jax
import jax.numpy as jnp
from jax import lax
from jax.experimental import pallas as pl
from jax.experimental.pallas import tpu as pltpu
from jax.sharding import PartitionSpec as P

WIN = 1024
REACH = 2


epsilon = 1e-06
query_scale = 168.0 ** (-0.5)


F32, BF16 = jnp.float32, jnp.bfloat16
NT = (((1,), (1,)), ((), ()))
TN = (((0,), (0,)), ((), ()))
LOG2E = 1.4426950408889634


def attention_kernel(q_ref, kv_ref, do_ref, lo_ref, dq_ref, dkv_ref, v_one, e_all, mask, dkey, dval):
    tokens = q_ref.shape[0]
    half = tokens // 2
    span = 5 * half
    head = 128
    kvs = kv_ref.shape[1] // 2
    kv_heads = kvs // head
    group = q_ref.shape[1] // kvs
    ones = jnp.ones((kv_ref.shape[0], head), BF16)
    for g in range(kv_heads):
        v_one[g, :, :head] = kv_ref[:, kvs + g * head : kvs + (g + 1) * head]
        v_one[g, :, head:] = ones
    for t in range(2):
        col = lax.broadcasted_iota(jnp.int32, (half, span), 1) + t * half
        row = lax.broadcasted_iota(jnp.int32, (half, span), 0) + t * half
        low = lo_ref[t * half : (t + 1) * half, :]
        seen = (col >= low) & (col <= row + 2 * tokens)
        mask[t] = jnp.where(seen, 1.0, 0.0).astype(BF16)
    lane = lax.broadcasted_iota(jnp.int32, (half, head), 1)
    for g in range(kv_heads):
        dkey[...] = jnp.zeros_like(dkey)
        dval[...] = jnp.zeros_like(dval)
        for r in range(group):
            h = g * group + r
            hc = slice(h * head, (h + 1) * head)
            for t in range(2):
                qs = slice(t * half, (t + 1) * half)
                ks = slice(t * half, t * half + span)
                q = q_ref[qs, hc]
                keys = kv_ref[ks, g * head : (g + 1) * head]
                s = lax.dot_general(q, keys, NT, preferred_element_type=F32)
                e_all[...] = jnp.exp2(s).astype(BF16) * mask[t]
                out = jnp.dot(e_all[...], v_one[g, ks, :], preferred_element_type=F32)
                inv = 1.0 / out[:, head:]
                scaled = do_ref[qs, hc].astype(F32) * inv
                delta = jnp.sum(scaled * (out[:, :head] * inv), axis=1, keepdims=True)
                d_hi = delta.astype(BF16).astype(F32)
                tail = jnp.where(lane == 0, -d_hi, jnp.where(lane == 1, d_hi - delta, 0.0))
                scaled16 = scaled.astype(BF16)
                both = jnp.concatenate([scaled16, tail.astype(BF16)], axis=1)
                dp = lax.dot_general(both, v_one[g, ks, :], NT, preferred_element_type=F32)
                ds = dp.astype(BF16) * e_all[...]
                dq_ref[qs, hc] = jnp.dot(ds, keys, preferred_element_type=F32)
                dkey[ks, :] += lax.dot_general(ds, q, TN, preferred_element_type=F32)
                dval[ks, :] += lax.dot_general(e_all[...], scaled16, TN, preferred_element_type=F32)
        dkv_ref[:, g * head : (g + 1) * head] = dkey[...] * (1.0 / LOG2E)
        dkv_ref[:, kvs + g * head : kvs + (g + 1) * head] = dval[...]


def attention(q, kv, do, lo):
    tokens = q.shape[0]
    reach = kv.shape[0]
    half = tokens // 2
    vm = pl.BlockSpec(memory_space=pltpu.VMEM)
    return pl.pallas_call(
        attention_kernel,
        out_shape=(
            jax.ShapeDtypeStruct(q.shape, F32),
            jax.ShapeDtypeStruct(kv.shape, F32),
        ),
        in_specs=[vm] * 4,
        out_specs=(vm, vm),
        scratch_shapes=[
            pltpu.VMEM((kv.shape[1] // 256, reach, 256), BF16),
            pltpu.VMEM((half, 5 * half), BF16),
            pltpu.VMEM((2, half, 5 * half), BF16),
            pltpu.VMEM((reach, 128), F32),
            pltpu.VMEM((reach, 128), F32),
        ],
        compiler_params=pltpu.CompilerParams(vmem_limit_bytes=48 << 20),
        name="attention",
    )(q, kv, do, lo)


def from_behind(value, axis, steps):
    count = lax.axis_size(axis)
    initial, last = (max(0, -steps), min(count, count - steps))
    return lax.ppermute(value, axis, [(source, source + steps) for source in range(initial, last)])


def head_normalize(projected, head_count, head_dim):
    shaped = projected.reshape(projected.shape[0], head_count, head_dim)
    inverse = lax.rsqrt(jnp.mean(shaped * shaped, axis=2, keepdims=True) + epsilon)
    return (shaped * inverse, inverse)


def head_normalize_backward(upstream_grad, normal_part, inverse, gain_vector):
    upstream = upstream_grad * gain_vector
    return inverse * (
        upstream - normal_part * jnp.mean(upstream * normal_part, axis=2, keepdims=True)
    )


def on_device(
    inputs,
    output_cotangent,
    w_query,
    key_projection,
    value_projection,
    norm_gain,
    q_gain,
    key_norm_gain,
    half_lengths,
):
    tokens = inputs.shape[0]
    model_width = inputs.shape[1]
    head_dim = q_gain.shape[0]
    q_cols = w_query.shape[1]
    kv_cols = key_projection.shape[1]
    q_heads = q_cols // head_dim
    kv_heads = kv_cols // head_dim
    queries_per_group = q_heads // kv_heads
    ctx_count = lax.axis_size("ctx")
    ctx_index = lax.axis_index("ctx")
    first_row = ctx_index * tokens
    grad_scale = float(tokens * ctx_count) ** (-0.5)
    contract_cols = (((1,), (1,)), ((), ()))
    contract_rows = (((0,), (0,)), ((), ()))
    widened = inputs.astype(jnp.float32)
    inv_rms = lax.rsqrt(jnp.mean(widened * widened, axis=1, keepdims=True) + epsilon)
    x_hat = widened * inv_rms
    normed = (x_hat * norm_gain).astype(jnp.bfloat16)
    stacked = jnp.concatenate([w_query, key_projection, value_projection], axis=1)
    projected = jnp.dot(
        normed,
        lax.all_gather(stacked, "ctx", axis=0, tiled=True),
        preferred_element_type=jnp.float32,
    )
    q_raw = projected[:, :q_cols]
    key_unnormed = projected[:, q_cols : q_cols + kv_cols]
    value_rows = projected[:, q_cols + kv_cols :].astype(jnp.bfloat16)
    query_normalized, q_inverse = head_normalize(q_raw, q_heads, head_dim)
    key_normalized, key_inverse_rms = head_normalize(key_unnormed, kv_heads, head_dim)
    query_multiplier = q_gain * query_scale
    query_rows = (
        (query_normalized * (query_multiplier * LOG2E)).astype(jnp.bfloat16).reshape(tokens, q_cols)
    )
    key_rows = (key_normalized * key_norm_gain).astype(jnp.bfloat16)
    packed_kv = jnp.concatenate([key_rows.reshape(tokens, kv_cols), value_rows], axis=1)
    remote = [from_behind(packed_kv, "ctx", offset) for offset in range(REACH, 0, -1)]
    halves = half_lengths.shape[0]
    upto = lax.iota(jnp.int32, halves)[None, :] <= lax.iota(jnp.int32, halves)[:, None]
    segment_ends = jnp.sum(jnp.where(upto, half_lengths[None, :], 0), axis=1)
    positions = first_row + lax.iota(jnp.int32, tokens)
    begun = jnp.max(jnp.where(segment_ends[None, :] <= positions[:, None], segment_ends[None, :], 0), axis=1)
    lowest = jnp.maximum(positions - (WIN - 1), begun) - (first_row - REACH * tokens)
    d_query_sum, kv_grads = attention(
        query_rows, jnp.concatenate(remote + [packed_kv], axis=0), output_cotangent, lowest[:, None]
    )
    kv_grad_total = kv_grads[REACH * tokens :]
    for offset in range(1, REACH + 1):
        part = kv_grads[(REACH - offset) * tokens : (REACH - offset + 1) * tokens]
        kv_grad_total = kv_grad_total + from_behind(
            part.astype(jnp.bfloat16), "ctx", -offset
        ).astype(jnp.float32)
    d_queries = d_query_sum.reshape(tokens, q_heads, head_dim)
    key_grads = kv_grad_total[:, :kv_cols].reshape(tokens, kv_heads, head_dim)
    dq16 = (
        head_normalize_backward(d_queries, query_normalized, q_inverse, query_multiplier)
        .reshape(tokens, q_cols)
        .astype(jnp.bfloat16)
    )
    key_grads_half16 = (
        head_normalize_backward(key_grads, key_normalized, key_inverse_rms, key_norm_gain)
        .reshape(tokens, kv_cols)
        .astype(jnp.bfloat16)
    )
    value_grads_half16 = kv_grad_total[:, kv_cols:].astype(jnp.bfloat16)
    d_stacked = jnp.concatenate([dq16, key_grads_half16, value_grads_half16], axis=1)
    head_part = lax.dot_general(
        d_stacked,
        lax.all_gather(stacked, "ctx", axis=0, tiled=True),
        contract_cols,
        preferred_element_type=jnp.float32,
    )
    fsdp_index = lax.axis_index("fsdp")
    features = model_width // lax.axis_size("fsdp")
    hat_mine = lax.dynamic_slice_in_dim(x_hat, fsdp_index * features, features, 1)
    gain_mine = lax.dynamic_slice_in_dim(norm_gain, fsdp_index * features, features, 0)
    d_mine = lax.psum_scatter(
        head_part.astype(jnp.bfloat16), "fsdp", scatter_dimension=1, tiled=True
    ).astype(jnp.float32)
    upstream = d_mine * gain_mine
    row_dot = lax.psum(
        jnp.sum(d_stacked.astype(jnp.float32) * projected, axis=1, keepdims=True), "fsdp"
    )
    grad_inputs = (inv_rms * (upstream - hat_mine * row_dot / model_width)).astype(jnp.bfloat16)
    norm_row_dots = row_dot[:, 0] * float(model_width) ** (-0.5)
    gain_term = grad_scale * jnp.sum(d_mine * hat_mine, axis=0)
    weight_term = grad_scale * lax.dot_general(
        normed, d_stacked, contract_rows, preferred_element_type=jnp.float32
    )
    weight_sum, gain_sum = (
        lax.psum_scatter(
            weight_term.astype(jnp.bfloat16), "ctx", scatter_dimension=0, tiled=True
        ).astype(jnp.float32),
        lax.psum_scatter(
            gain_term.astype(jnp.bfloat16), "ctx", scatter_dimension=0, tiled=True
        ).astype(jnp.float32),
    )
    weight_sum = weight_sum.astype(jnp.bfloat16)
    q_term = grad_scale * jnp.sum(d_queries * query_normalized * query_scale, axis=(0, 1))
    k_term = grad_scale * jnp.sum(key_grads * key_normalized, axis=(0, 1))
    grad_q_gain, grad_k_gain = lax.psum((q_term, k_term), ("ctx", "fsdp"))
    return (
        grad_inputs,
        weight_sum[:, :q_cols],
        weight_sum[:, q_cols : q_cols + kv_cols],
        weight_sum[:, q_cols + kv_cols :],
        gain_sum,
        grad_q_gain,
        grad_k_gain,
        norm_row_dots,
    )


def solution(mesh):
    placed = (
        P("ctx", None),
        P("ctx", "fsdp"),
        P("ctx", "fsdp"),
        P("ctx", "fsdp"),
        P("ctx", "fsdp"),
        P(),
        P(),
        P(),
        P(),
    )
    return jax.shard_map(
        on_device,
        mesh=mesh,
        in_specs=placed,
        out_specs=(
            P("ctx", "fsdp"),
            P("ctx", "fsdp"),
            P("ctx", "fsdp"),
            P("ctx", "fsdp"),
            P(("fsdp", "ctx")),
            P(),
            P(),
            P("ctx"),
        ),
        check_vma=False,
    )
```

```python
import jax
import jax.numpy as jnp
from jax import lax
from jax.experimental import pallas as pl
from jax.experimental.pallas import tpu as pltpu
from jax.sharding import PartitionSpec as P

WIN = 1024
REACH = 2


epsilon = 1e-06
query_scale = 168.0 ** (-0.5)


F32, BF16 = jnp.float32, jnp.bfloat16
NT = (((1,), (1,)), ((), ()))
TN = (((0,), (0,)), ((), ()))
MESH = pl.DeviceIdType.MESH
LOG2E = 1.4426950408889634


def attention_kernel(q_ref, kv_ref, do_ref, lo_ref, dq_ref, dkv_ref, v_one, e_all, mask, dkey, dval):
    tokens = q_ref.shape[0]
    half = tokens // 2
    span = 5 * half
    head = 128
    kvs = kv_ref.shape[1] // 2
    kv_heads = kvs // head
    group = q_ref.shape[1] // kvs
    ones = jnp.ones((kv_ref.shape[0], head), BF16)
    for g in range(kv_heads):
        v_one[g, :, :head] = kv_ref[:, kvs + g * head : kvs + (g + 1) * head]
        v_one[g, :, head:] = ones
    for t in range(2):
        col = lax.broadcasted_iota(jnp.int32, (half, span), 1) + t * half
        row = lax.broadcasted_iota(jnp.int32, (half, span), 0) + t * half
        low = lo_ref[t * half : (t + 1) * half, :]
        seen = (col >= low) & (col <= row + 2 * tokens)
        mask[t] = jnp.where(seen, 1.0, 0.0).astype(BF16)
    lane = lax.broadcasted_iota(jnp.int32, (half, head), 1)
    for g in range(kv_heads):
        dkey[...] = jnp.zeros_like(dkey)
        dval[...] = jnp.zeros_like(dval)
        for r in range(group):
            h = g * group + r
            hc = slice(h * head, (h + 1) * head)
            for t in range(2):
                qs = slice(t * half, (t + 1) * half)
                ks = slice(t * half, t * half + span)
                q = q_ref[qs, hc]
                keys = kv_ref[ks, g * head : (g + 1) * head]
                s = lax.dot_general(q, keys, NT, preferred_element_type=F32)
                e_all[...] = jnp.exp2(s).astype(BF16) * mask[t]
                out = jnp.dot(e_all[...], v_one[g, ks, :], preferred_element_type=F32)
                inv = 1.0 / out[:, head:]
                scaled = do_ref[qs, hc].astype(F32) * inv
                delta = jnp.sum(scaled * (out[:, :head] * inv), axis=1, keepdims=True)
                d_hi = delta.astype(BF16).astype(F32)
                tail = jnp.where(lane == 0, -d_hi, jnp.where(lane == 1, d_hi - delta, 0.0))
                scaled16 = scaled.astype(BF16)
                both = jnp.concatenate([scaled16, tail.astype(BF16)], axis=1)
                dp = lax.dot_general(both, v_one[g, ks, :], NT, preferred_element_type=F32)
                ds = dp.astype(BF16) * e_all[...]
                dq_ref[qs, hc] = jnp.dot(ds, keys, preferred_element_type=F32)
                dkey[ks, :] += lax.dot_general(ds, q, TN, preferred_element_type=F32)
                dval[ks, :] += lax.dot_general(e_all[...], scaled16, TN, preferred_element_type=F32)
        dkv_ref[:, g * head : (g + 1) * head] = dkey[...] * (1.0 / LOG2E)
        dkv_ref[:, kvs + g * head : kvs + (g + 1) * head] = dval[...]


def attention(q, kv, do, lo):
    tokens = q.shape[0]
    reach = kv.shape[0]
    half = tokens // 2
    vm = pl.BlockSpec(memory_space=pltpu.VMEM)
    return pl.pallas_call(
        attention_kernel,
        out_shape=(
            jax.ShapeDtypeStruct(q.shape, F32),
            jax.ShapeDtypeStruct(kv.shape, F32),
        ),
        in_specs=[vm] * 4,
        out_specs=(vm, vm),
        scratch_shapes=[
            pltpu.VMEM((kv.shape[1] // 256, reach, 256), BF16),
            pltpu.VMEM((half, 5 * half), BF16),
            pltpu.VMEM((2, half, 5 * half), BF16),
            pltpu.VMEM((reach, 128), F32),
            pltpu.VMEM((reach, 128), F32),
        ],
        compiler_params=pltpu.CompilerParams(vmem_limit_bytes=48 << 20),
        name="attention",
    )(q, kv, do, lo)

def both_reductions(w_ref, nt_ref, d_ref, scale):
    blocks, wide, cols = w_ref.shape
    tokens = d_ref.shape[0]
    part = wide // 2
    wing = cols // 2

    def kernel(w, nt, d, dn_out, wg_out, nt_far, d_far, far, near, half_in, near_in, cross, cross_in,
               swap_s, swap_r, half_s, half_r, near_s, near_r, cross_s, cross_r):
        c, f = lax.axis_index("ctx"), lax.axis_index("fsdp")
        z, x, core = c // 4, lax.rem(c // 2, 2), lax.rem(c, 2)
        xh, y = f // 4, lax.rem(f, 4)
        ring = (
            lambda k: (c, xh * 4 + lax.rem(y + k, 4)),
            lambda k: (lax.rem(z + k, 4) * 4 + x * 2 + core, f),
        )
        across = ((c, (1 - xh) * 4 + y), (z * 4 + (1 - x) * 2 + core, f))
        twin = (z * 4 + x * 2 + 1 - core, f)

        barrier = pltpu.get_barrier_semaphore()
        partners = [twin, *across] + [ring[m](k) for m in range(2) for k in (1, 3)]
        for partner in partners:
            pl.semaphore_signal(barrier, inc=1, device_id=partner, device_id_type=MESH)
        pl.semaphore_wait(barrier, len(partners))

        def copy(src, dst, ss, rs, to):
            return pltpu.make_async_remote_copy(
                src_ref=src, dst_ref=dst, send_sem=ss, recv_sem=rs, device_id=to, device_id_type=MESH
            )

        swaps = [
            copy(d, d_far, swap_s.at[0], swap_r.at[0], twin),
            copy(nt.at[:, 1 - core], nt_far, swap_s.at[1], swap_r.at[1], twin),
        ]
        for swap in swaps:
            swap.start()

        def term(m, s, k, h):
            if m == 0:
                block = (xh if s else 1 - xh) * 4 + lax.rem(y + k, 4)
                rows = w[block, h * part : (h + 1) * part, :]
                return lax.dot_general(rows, d[...], NT, preferred_element_type=F32)
            block = lax.rem(z + k, 4) * 2 + (x if s else 1 - x)
            hs = slice(h * wing, (h + 1) * wing)
            total = jnp.dot(nt[block, core], d[:, hs], preferred_element_type=F32)
            total += jnp.dot(nt_far[block], d_far[:, hs], preferred_element_type=F32)
            return total * scale

        sent = []

        def send_far(m, s):
            for h in range(2):
                far[m, s, h] = term(m, s, 2, h).astype(BF16)
                cp = copy(far.at[m, s, h], half_in.at[m, s, h], half_s.at[m, s, h], half_r.at[m, s, h],
                          ring[m](1 if h == 0 else 3))
                cp.start()
                sent.append(cp)
                halves[m, s, h] = cp

        def make_near(m, s):
            for n, k in enumerate((1, 3)):
                for h in range(2):
                    near[m, s, n, h] = term(m, s, k, h).astype(BF16)

        def send_near(m, s):
            for n, k in enumerate((1, 3)):
                halves[m, s, n].wait_recv()
                near[m, s, n, n] = (near[m, s, n, n].astype(F32) + half_in[m, s, n].astype(F32)).astype(BF16)
                cp = copy(near.at[m, s, n], near_in.at[m, s, n], near_s.at[m, s, n], near_r.at[m, s, n], ring[m](k))
                cp.start()
                sent.append(cp)
                nears[m, s, n] = cp

        def arrived(m, s, h):
            return near_in[m, s, 0, h].astype(F32) + near_in[m, s, 1, h].astype(F32)

        halves, nears, crossed = {}, {}, {}
        send_far(0, 0)
        make_near(0, 0)
        for swap in swaps:
            swap.wait_recv()
        send_far(1, 0)
        send_near(0, 0)
        make_near(1, 0)
        send_far(0, 1)
        send_near(1, 0)
        send_far(1, 1)
        make_near(0, 1)
        send_near(0, 1)
        make_near(1, 1)
        send_near(1, 1)
        for m in range(2):
            for h in range(2):
                if h == 0:
                    mine = [term(m, 0, 0, 0), term(m, 0, 0, 1)]
                    for n in range(2):
                        nears[m, 0, n].wait_recv()
                cross[m, h] = (mine[h] + arrived(m, 0, h)).astype(BF16)
            cp = copy(cross.at[m], cross_in.at[m], cross_s.at[m], cross_r.at[m], across[m])
            cp.start()
            sent.append(cp)
            crossed[m] = cp
        for h in range(2):
            dn_out[h] = term(0, 1, 0, h)
        weights = [term(1, 1, 0, h) for h in range(2)]
        for n in range(2):
            nears[0, 1, n].wait_recv()
        crossed[0].wait_recv()
        for h in range(2):
            dn_out[h] = dn_out[h] + arrived(0, 1, h) + cross_in[0, h].astype(F32)
        for n in range(2):
            nears[1, 1, n].wait_recv()
        crossed[1].wait_recv()
        for h in range(2):
            total = weights[h] + arrived(1, 1, h) + cross_in[1, h].astype(F32)
            wg_out[:, h * wing : (h + 1) * wing] = total.astype(BF16)
        for cp in swaps + sent:
            cp.wait_send()

    vm = pl.BlockSpec(memory_space=pltpu.VMEM)
    dma = pltpu.SemaphoreType.DMA
    block = (2, part, tokens)
    return pl.pallas_call(
        kernel,
        out_shape=(
            jax.ShapeDtypeStruct(block, F32),
            jax.ShapeDtypeStruct((part, cols), BF16),
        ),
        in_specs=[vm] * 3,
        out_specs=(vm, vm),
        scratch_shapes=[
            pltpu.VMEM((blocks, part, tokens), BF16),
            pltpu.VMEM((tokens, cols), BF16),
            pltpu.VMEM((2, 2) + block, BF16),
            pltpu.VMEM((2, 2, 2) + block, BF16),
            pltpu.VMEM((2, 2) + block, BF16),
            pltpu.VMEM((2, 2, 2) + block, BF16),
            pltpu.VMEM((2,) + block, BF16),
            pltpu.VMEM((2,) + block, BF16),
            dma((2,)), dma((2,)),
            dma((2, 2, 2)), dma((2, 2, 2)),
            dma((2, 2, 2)), dma((2, 2, 2)),
            dma((2,)), dma((2,)),
        ],
        compiler_params=pltpu.CompilerParams(
            collective_id=1, has_side_effects=True, vmem_limit_bytes=60 << 20
        ),
        name="both_reductions",
    )(w_ref, nt_ref, d_ref)


def from_behind(value, axis, steps):
    count = lax.axis_size(axis)
    initial, last = (max(0, -steps), min(count, count - steps))
    return lax.ppermute(value, axis, [(source, source + steps) for source in range(initial, last)])


def head_normalize(projected, head_count, head_dim):
    shaped = projected.reshape(projected.shape[0], head_count, head_dim)
    inverse = lax.rsqrt(jnp.mean(shaped * shaped, axis=2, keepdims=True) + epsilon)
    return (shaped * inverse, inverse)


def head_normalize_backward(upstream_grad, normal_part, inverse, gain_vector):
    upstream = upstream_grad * gain_vector
    return inverse * (
        upstream - normal_part * jnp.mean(upstream * normal_part, axis=2, keepdims=True)
    )


def on_device(
    inputs,
    output_cotangent,
    w_query,
    key_projection,
    value_projection,
    norm_gain,
    q_gain,
    key_norm_gain,
    half_lengths,
):
    tokens = inputs.shape[0]
    model_width = inputs.shape[1]
    head_dim = q_gain.shape[0]
    q_cols = w_query.shape[1]
    kv_cols = key_projection.shape[1]
    q_heads = q_cols // head_dim
    kv_heads = kv_cols // head_dim
    queries_per_group = q_heads // kv_heads
    ctx_count = lax.axis_size("ctx")
    ctx_index = lax.axis_index("ctx")
    first_row = ctx_index * tokens
    grad_scale = float(tokens * ctx_count) ** (-0.5)
    widened = inputs.astype(jnp.float32)
    inv_rms = lax.rsqrt(jnp.mean(widened * widened, axis=1, keepdims=True) + epsilon)
    x_hat = widened * inv_rms
    normed = (x_hat * norm_gain).astype(jnp.bfloat16)
    stacked = jnp.concatenate([w_query, key_projection, value_projection], axis=1)
    gathered = lax.all_gather(stacked, "ctx", axis=0, tiled=True)
    projected = jnp.dot(
        normed,
        gathered,
        preferred_element_type=jnp.float32,
    )
    q_raw = projected[:, :q_cols]
    key_unnormed = projected[:, q_cols : q_cols + kv_cols]
    value_rows = projected[:, q_cols + kv_cols :].astype(jnp.bfloat16)
    query_normalized, q_inverse = head_normalize(q_raw, q_heads, head_dim)
    key_normalized, key_inverse_rms = head_normalize(key_unnormed, kv_heads, head_dim)
    query_multiplier = q_gain * query_scale
    query_rows = (
        (query_normalized * (query_multiplier * LOG2E)).astype(jnp.bfloat16).reshape(tokens, q_cols)
    )
    key_rows = (key_normalized * key_norm_gain).astype(jnp.bfloat16)
    packed_kv = jnp.concatenate([key_rows.reshape(tokens, kv_cols), value_rows], axis=1)
    remote = [from_behind(packed_kv, "ctx", offset) for offset in range(REACH, 0, -1)]
    halves = half_lengths.shape[0]
    upto = lax.iota(jnp.int32, halves)[None, :] <= lax.iota(jnp.int32, halves)[:, None]
    segment_ends = jnp.sum(jnp.where(upto, half_lengths[None, :], 0), axis=1)
    positions = first_row + lax.iota(jnp.int32, tokens)
    begun = jnp.max(jnp.where(segment_ends[None, :] <= positions[:, None], segment_ends[None, :], 0), axis=1)
    lowest = jnp.maximum(positions - (WIN - 1), begun) - (first_row - REACH * tokens)
    d_query_sum, kv_grads = attention(
        query_rows, jnp.concatenate(remote + [packed_kv], axis=0), output_cotangent, lowest[:, None]
    )
    kv_grad_total = kv_grads[REACH * tokens :]
    for offset in range(1, REACH + 1):
        part = kv_grads[(REACH - offset) * tokens : (REACH - offset + 1) * tokens]
        kv_grad_total = kv_grad_total + from_behind(
            part.astype(jnp.bfloat16), "ctx", -offset
        ).astype(jnp.float32)
    d_queries = d_query_sum.reshape(tokens, q_heads, head_dim)
    key_grads = kv_grad_total[:, :kv_cols].reshape(tokens, kv_heads, head_dim)
    dq16 = (
        head_normalize_backward(d_queries, query_normalized, q_inverse, query_multiplier)
        .reshape(tokens, q_cols)
        .astype(jnp.bfloat16)
    )
    key_grads_half16 = (
        head_normalize_backward(key_grads, key_normalized, key_inverse_rms, key_norm_gain)
        .reshape(tokens, kv_cols)
        .astype(jnp.bfloat16)
    )
    value_grads_half16 = kv_grad_total[:, kv_cols:].astype(jnp.bfloat16)
    d_stacked = jnp.concatenate([dq16, key_grads_half16, value_grads_half16], axis=1)
    fsdp_index = lax.axis_index("fsdp")
    fsdp_count = lax.axis_size("fsdp")
    features = model_width // fsdp_count
    inputs_t = inputs.T
    inv_row = inv_rms.reshape(1, tokens)
    normed_t = (inputs_t.astype(jnp.float32) * inv_row * norm_gain[:, None]).astype(jnp.bfloat16)
    hat_mine = (
        lax.dynamic_slice_in_dim(inputs_t, fsdp_index * features, features, 0).astype(jnp.float32) * inv_row
    )
    gain_mine = lax.dynamic_slice_in_dim(norm_gain, fsdp_index * features, features, 0)
    d_mine, weight_sum = both_reductions(
        gathered.reshape(fsdp_count, features, -1),
        normed_t.reshape(ctx_count // 2, 2, model_width // ctx_count, tokens),
        d_stacked,
        grad_scale,
    )
    d_mine = d_mine.reshape(features, tokens)
    row_dot = lax.psum(jnp.sum(d_stacked.astype(jnp.float32) * projected, axis=1), "fsdp")
    upstream = d_mine * gain_mine[:, None]
    grad_inputs = (inv_row * (upstream - hat_mine * (row_dot[None, :] / model_width))).astype(jnp.bfloat16).T
    norm_row_dots = row_dot * float(model_width) ** (-0.5)
    gain_term = grad_scale * jnp.sum(d_mine * hat_mine, axis=1)
    gain_sum = lax.psum_scatter(
        gain_term.astype(jnp.bfloat16), "ctx", scatter_dimension=0, tiled=True
    ).astype(jnp.float32)
    q_term = grad_scale * jnp.sum(d_queries * query_normalized * query_scale, axis=(0, 1))
    k_term = grad_scale * jnp.sum(key_grads * key_normalized, axis=(0, 1))
    grad_q_gain, grad_k_gain = lax.psum((q_term, k_term), ("ctx", "fsdp"))
    return (
        grad_inputs,
        weight_sum[:, :q_cols],
        weight_sum[:, q_cols : q_cols + kv_cols],
        weight_sum[:, q_cols + kv_cols :],
        gain_sum,
        grad_q_gain,
        grad_k_gain,
        norm_row_dots,
    )


def solution(mesh):
    placed = (
        P("ctx", None),
        P("ctx", "fsdp"),
        P("ctx", "fsdp"),
        P("ctx", "fsdp"),
        P("ctx", "fsdp"),
        P(),
        P(),
        P(),
        P(),
    )
    return jax.shard_map(
        on_device,
        mesh=mesh,
        in_specs=placed,
        out_specs=(
            P("ctx", "fsdp"),
            P("ctx", "fsdp"),
            P("ctx", "fsdp"),
            P("ctx", "fsdp"),
            P(("fsdp", "ctx")),
            P(),
            P(),
            P("ctx"),
        ),
        check_vma=False,
    )
```

```python
import jax
import jax.numpy as jnp
from jax import lax
from jax.experimental import pallas as pl
from jax.experimental.pallas import tpu as pltpu
from jax.sharding import PartitionSpec as P

WIN = 1024
REACH = 2


epsilon = 1e-06
query_scale = 168.0 ** (-0.5)


F32, BF16 = jnp.float32, jnp.bfloat16
NT = (((1,), (1,)), ((), ()))
TN = (((0,), (0,)), ((), ()))
MESH = pl.DeviceIdType.MESH
LOG2E = 1.4426950408889634


def attention_kernel(q_ref, kv_ref, do_ref, lo_ref, dq_ref, dkv_ref, v_one, e_all, mask, dkey, dval):
    tokens = q_ref.shape[0]
    half = tokens // 2
    span = 5 * half
    head = 128
    kvs = kv_ref.shape[1] // 2
    kv_heads = kvs // head
    group = q_ref.shape[1] // kvs
    ones = jnp.ones((kv_ref.shape[0], head), BF16)
    for g in range(kv_heads):
        v_one[g, :, :head] = kv_ref[:, kvs + g * head : kvs + (g + 1) * head]
        v_one[g, :, head:] = ones
    for t in range(2):
        col = lax.broadcasted_iota(jnp.int32, (half, span), 1) + t * half
        row = lax.broadcasted_iota(jnp.int32, (half, span), 0) + t * half
        low = lo_ref[t * half : (t + 1) * half, :]
        seen = (col >= low) & (col <= row + 2 * tokens)
        mask[t] = jnp.where(seen, 1.0, 0.0).astype(BF16)
    lane = lax.broadcasted_iota(jnp.int32, (half, head), 1)
    for g in range(kv_heads):
        dkey[...] = jnp.zeros_like(dkey)
        dval[...] = jnp.zeros_like(dval)
        for r in range(group):
            h = g * group + r
            hc = slice(h * head, (h + 1) * head)
            for t in range(2):
                qs = slice(t * half, (t + 1) * half)
                ks = slice(t * half, t * half + span)
                q = q_ref[qs, hc]
                keys = kv_ref[ks, g * head : (g + 1) * head]
                s = lax.dot_general(q, keys, NT, preferred_element_type=F32)
                e_all[...] = jnp.exp2(s).astype(BF16) * mask[t]
                out = jnp.dot(e_all[...], v_one[g, ks, :], preferred_element_type=F32)
                inv = 1.0 / out[:, head:]
                scaled = do_ref[qs, hc].astype(F32) * inv
                delta = jnp.sum(scaled * (out[:, :head] * inv), axis=1, keepdims=True)
                d_hi = delta.astype(BF16).astype(F32)
                tail = jnp.where(lane == 0, -d_hi, jnp.where(lane == 1, d_hi - delta, 0.0))
                scaled16 = scaled.astype(BF16)
                both = jnp.concatenate([scaled16, tail.astype(BF16)], axis=1)
                dp = lax.dot_general(both, v_one[g, ks, :], NT, preferred_element_type=F32)
                ds = dp.astype(BF16) * e_all[...]
                dq_ref[qs, hc] = jnp.dot(ds, keys, preferred_element_type=F32)
                dkey[ks, :] += lax.dot_general(ds, q, TN, preferred_element_type=F32)
                dval[ks, :] += lax.dot_general(e_all[...], scaled16, TN, preferred_element_type=F32)
        dkv_ref[:, g * head : (g + 1) * head] = dkey[...] * (1.0 / LOG2E)
        dkv_ref[:, kvs + g * head : kvs + (g + 1) * head] = dval[...]


def attention(q, kv, do, lo):
    tokens = q.shape[0]
    reach = kv.shape[0]
    half = tokens // 2
    vm = pl.BlockSpec(memory_space=pltpu.VMEM)
    return pl.pallas_call(
        attention_kernel,
        out_shape=(
            jax.ShapeDtypeStruct(q.shape, F32),
            jax.ShapeDtypeStruct(kv.shape, F32),
        ),
        in_specs=[vm] * 4,
        out_specs=(vm, vm),
        scratch_shapes=[
            pltpu.VMEM((kv.shape[1] // 256, reach, 256), BF16),
            pltpu.VMEM((half, 5 * half), BF16),
            pltpu.VMEM((2, half, 5 * half), BF16),
            pltpu.VMEM((reach, 128), F32),
            pltpu.VMEM((reach, 128), F32),
        ],
        compiler_params=pltpu.CompilerParams(vmem_limit_bytes=48 << 20),
        name="attention",
    )(q, kv, do, lo)

def both_reductions(w_ref, nt_ref, nt_far_ref, d_ref, hat_ref, small_ref, scale):
    blocks, wide, cols = w_ref.shape
    tokens = d_ref.shape[0]
    part = wide // 2
    wing = cols // 2

    def kernel(w, nt, nt_far, d, hat, small, dn_out, wg_out, sum_f, sum_c, d_far, slots_f, slots_c, mine_c, far, near, half_in, near_in, cross, cross_in,
               swap_s, swap_r, few_s, few_r, half_s, half_r, near_s, near_r, cross_s, cross_r):
        c, f = lax.axis_index("ctx"), lax.axis_index("fsdp")
        z, x, core = c // 4, lax.rem(c // 2, 2), lax.rem(c, 2)
        xh, y = f // 4, lax.rem(f, 4)
        ring = (
            lambda k: (c, xh * 4 + lax.rem(y + k, 4)),
            lambda k: (lax.rem(z + k, 4) * 4 + x * 2 + core, f),
        )
        across = ((c, (1 - xh) * 4 + y), (z * 4 + (1 - x) * 2 + core, f))
        twin = (z * 4 + x * 2 + 1 - core, f)

        barrier = pltpu.get_barrier_semaphore()
        peers_f = [(c, lax.rem(f + k, 8)) for k in range(1, 8)]
        peers_c = [(lax.rem(c + k, 16), f) for k in range(1, 16)]
        partners = peers_f + peers_c
        for partner in partners:
            pl.semaphore_signal(barrier, inc=1, device_id=partner, device_id_type=MESH)
        pl.semaphore_wait(barrier, len(partners))

        def copy(src, dst, ss, rs, to):
            return pltpu.make_async_remote_copy(
                src_ref=src, dst_ref=dst, send_sem=ss, recv_sem=rs, device_id=to, device_id_type=MESH
            )

        swap = copy(d, d_far, swap_s, swap_r, twin)
        swap.start()
        slots_f[f] = small[...]
        few = [
            copy(small, slots_f.at[f], few_s.at[k], few_r.at[k], to) for k, to in enumerate(peers_f)
        ]
        for cp in few:
            cp.start()

        def term(m, s, k, h):
            if m == 0:
                block = (xh if s else 1 - xh) * 4 + lax.rem(y + k, 4)
                rows = w[block, h * part : (h + 1) * part, :]
                return lax.dot_general(rows, d[...], NT, preferred_element_type=F32)
            block = lax.rem(z + k, 4) * 2 + (x if s else 1 - x)
            hs = slice(h * wing, (h + 1) * wing)
            total = jnp.dot(nt[block], d[:, hs], preferred_element_type=F32)
            total += jnp.dot(nt_far[block], d_far[:, hs], preferred_element_type=F32)
            return total * scale

        sent = []

        def send_far(m, s):
            for h in range(2):
                far[m, s, h] = term(m, s, 2, h).astype(BF16)
                cp = copy(far.at[m, s, h], half_in.at[m, s, h], half_s.at[m, s, h], half_r.at[m, s, h],
                          ring[m](1 if h == 0 else 3))
                cp.start()
                sent.append(cp)
                halves[m, s, h] = cp

        def make_near(m, s):
            for n, k in enumerate((1, 3)):
                for h in range(2):
                    near[m, s, n, h] = term(m, s, k, h).astype(BF16)

        def send_near(m, s):
            for n, k in enumerate((1, 3)):
                halves[m, s, n].wait_recv()
                near[m, s, n, n] = (near[m, s, n, n].astype(F32) + half_in[m, s, n].astype(F32)).astype(BF16)
                cp = copy(near.at[m, s, n], near_in.at[m, s, n], near_s.at[m, s, n], near_r.at[m, s, n], ring[m](k))
                cp.start()
                sent.append(cp)
                nears[m, s, n] = cp

        def arrived(m, s, h):
            return near_in[m, s, 0, h].astype(F32) + near_in[m, s, 1, h].astype(F32)

        halves, nears, crossed = {}, {}, {}
        send_far(0, 0)
        send_far(0, 1)
        swap.wait_recv()
        send_far(1, 0)
        send_far(1, 1)
        make_near(0, 0)
        send_near(0, 0)
        make_near(1, 0)
        send_near(1, 0)
        make_near(0, 1)
        send_near(0, 1)
        make_near(1, 1)
        send_near(1, 1)
        for cp in few:
            cp.wait_recv()
        total_f = slots_f[0]
        for k in range(1, 8):
            total_f = total_f + slots_f[k]
        sum_f[...] = total_f
        for m in range(2):
            for h in range(2):
                if h == 0:
                    mine = [term(m, 0, 0, 0), term(m, 0, 0, 1)]
                    for n in range(2):
                        nears[m, 0, n].wait_recv()
                cross[m, h] = (mine[h] + arrived(m, 0, h)).astype(BF16)
            cp = copy(cross.at[m], cross_in.at[m], cross_s.at[m], cross_r.at[m], across[m])
            cp.start()
            sent.append(cp)
            crossed[m] = cp
        for h in range(2):
            dn_out[h] = term(0, 1, 0, h)
        weights = [term(1, 1, 0, h) for h in range(2)]
        for n in range(2):
            nears[0, 1, n].wait_recv()
        crossed[0].wait_recv()
        spread = jnp.zeros((8, 128), F32)
        for h in range(2):
            total = dn_out[h] + arrived(0, 1, h) + cross_in[0, h].astype(F32)
            dn_out[h] = total
            sums = scale * jnp.sum(total * hat[h], axis=1, keepdims=True)
            at = lax.broadcasted_iota(jnp.int32, (part, 128), 0) + h * part
            lane = lax.broadcasted_iota(jnp.int32, (part, 128), 1)
            to_row = jnp.where(at // 128 == lane, sums, 0.0)
            to_lane = jnp.where(lax.rem(at, 128) == lane, 1.0, 0.0)
            spread += lax.dot_general(
                to_row.astype(BF16), to_lane.astype(BF16), TN, preferred_element_type=F32
            )[:8]
        mine_c[...] = spread
        mine_c[6:8, :] = total_f[4:6, :]
        slots_c[c] = mine_c[...]
        few_c = [
            copy(mine_c, slots_c.at[c], few_s.at[7 + k], few_r.at[7 + k], to) for k, to in enumerate(peers_c)
        ]
        for cp in few_c:
            cp.start()
        for n in range(2):
            nears[1, 1, n].wait_recv()
        crossed[1].wait_recv()
        for h in range(2):
            total = weights[h] + arrived(1, 1, h) + cross_in[1, h].astype(F32)
            wg_out[:, h * wing : (h + 1) * wing] = total.astype(BF16)
        for cp in few_c:
            cp.wait_recv()
        total_c = slots_c[0]
        for k in range(1, 16):
            total_c = total_c + slots_c[k]
        sum_c[...] = total_c
        for cp in [swap] + few + few_c + sent:
            cp.wait_send()

    vm = pl.BlockSpec(memory_space=pltpu.VMEM)
    dma = pltpu.SemaphoreType.DMA
    block = (2, part, tokens)
    return pl.pallas_call(
        kernel,
        out_shape=(
            jax.ShapeDtypeStruct(block, F32),
            jax.ShapeDtypeStruct((part, cols), BF16),
            jax.ShapeDtypeStruct((8, 128), F32),
            jax.ShapeDtypeStruct((8, 128), F32),
        ),
        in_specs=[vm] * 6,
        out_specs=(vm,) * 4,
        scratch_shapes=[
            pltpu.VMEM((tokens, cols), BF16),
            pltpu.VMEM((8, 8, 128), F32),
            pltpu.VMEM((16, 8, 128), F32),
            pltpu.VMEM((8, 128), F32),
            pltpu.VMEM((2, 2) + block, BF16),
            pltpu.VMEM((2, 2, 2) + block, BF16),
            pltpu.VMEM((2, 2) + block, BF16),
            pltpu.VMEM((2, 2, 2) + block, BF16),
            pltpu.VMEM((2,) + block, BF16),
            pltpu.VMEM((2,) + block, BF16),
            dma, dma,
            dma((22,)), dma((22,)),
            dma((2, 2, 2)), dma((2, 2, 2)),
            dma((2, 2, 2)), dma((2, 2, 2)),
            dma((2,)), dma((2,)),
        ],
        compiler_params=pltpu.CompilerParams(
            collective_id=1, has_side_effects=True, vmem_limit_bytes=60 << 20
        ),
        name="both_reductions",
    )(w_ref, nt_ref, nt_far_ref, d_ref, hat_ref, small_ref)


def from_behind(value, axis, steps):
    count = lax.axis_size(axis)
    initial, last = (max(0, -steps), min(count, count - steps))
    return lax.ppermute(value, axis, [(source, source + steps) for source in range(initial, last)])


def head_normalize(projected, head_count, head_dim):
    shaped = projected.reshape(projected.shape[0], head_count, head_dim)
    inverse = lax.rsqrt(jnp.mean(shaped * shaped, axis=2, keepdims=True) + epsilon)
    return (shaped * inverse, inverse)


def head_normalize_backward(upstream_grad, normal_part, inverse, gain_vector):
    upstream = upstream_grad * gain_vector
    return inverse * (
        upstream - normal_part * jnp.mean(upstream * normal_part, axis=2, keepdims=True)
    )


def on_device(
    inputs,
    output_cotangent,
    w_query,
    key_projection,
    value_projection,
    norm_gain,
    q_gain,
    key_norm_gain,
    half_lengths,
):
    tokens = inputs.shape[0]
    model_width = inputs.shape[1]
    head_dim = q_gain.shape[0]
    q_cols = w_query.shape[1]
    kv_cols = key_projection.shape[1]
    q_heads = q_cols // head_dim
    kv_heads = kv_cols // head_dim
    queries_per_group = q_heads // kv_heads
    ctx_count = lax.axis_size("ctx")
    ctx_index = lax.axis_index("ctx")
    first_row = ctx_index * tokens
    grad_scale = float(tokens * ctx_count) ** (-0.5)
    widened = inputs.astype(jnp.float32)
    inv_rms = lax.rsqrt(jnp.mean(widened * widened, axis=1, keepdims=True) + epsilon)
    x_hat = widened * inv_rms
    normed = (x_hat * norm_gain).astype(jnp.bfloat16)
    fsdp_index = lax.axis_index("fsdp")
    fsdp_count = lax.axis_size("fsdp")
    features = model_width // fsdp_count
    inputs_t = inputs.T
    inv_row = inv_rms.reshape(1, tokens)
    normed_t = (inputs_t.astype(jnp.float32) * inv_row * norm_gain[:, None]).astype(jnp.bfloat16)
    hat_mine = (
        lax.dynamic_slice_in_dim(inputs_t, fsdp_index * features, features, 0).astype(jnp.float32) * inv_row
    )
    gain_mine = lax.dynamic_slice_in_dim(norm_gain, fsdp_index * features, features, 0)
    blocked = normed_t.reshape(ctx_count // 2, 2, model_width // ctx_count, tokens)
    core = lax.rem(ctx_index, 2)
    normed_kept = lax.dynamic_index_in_dim(blocked, core, 1, keepdims=False)
    normed_far = lax.ppermute(
        lax.dynamic_index_in_dim(blocked, 1 - core, 1, keepdims=False),
        "ctx",
        [(source, source ^ 1) for source in range(ctx_count)],
    )
    stacked = jnp.concatenate([w_query, key_projection, value_projection], axis=1)
    gathered = lax.all_gather(stacked, "ctx", axis=0, tiled=True)
    projected = jnp.dot(
        normed,
        gathered,
        preferred_element_type=jnp.float32,
    )
    q_raw = projected[:, :q_cols]
    key_unnormed = projected[:, q_cols : q_cols + kv_cols]
    value_rows = projected[:, q_cols + kv_cols :].astype(jnp.bfloat16)
    query_normalized, q_inverse = head_normalize(q_raw, q_heads, head_dim)
    key_normalized, key_inverse_rms = head_normalize(key_unnormed, kv_heads, head_dim)
    query_multiplier = q_gain * query_scale
    query_rows = (
        (query_normalized * (query_multiplier * LOG2E)).astype(jnp.bfloat16).reshape(tokens, q_cols)
    )
    key_rows = (key_normalized * key_norm_gain).astype(jnp.bfloat16)
    packed_kv = jnp.concatenate([key_rows.reshape(tokens, kv_cols), value_rows], axis=1)
    remote = [from_behind(packed_kv, "ctx", offset) for offset in range(REACH, 0, -1)]
    halves = half_lengths.shape[0]
    upto = lax.iota(jnp.int32, halves)[None, :] <= lax.iota(jnp.int32, halves)[:, None]
    segment_ends = jnp.sum(jnp.where(upto, half_lengths[None, :], 0), axis=1)
    positions = first_row + lax.iota(jnp.int32, tokens)
    begun = jnp.max(jnp.where(segment_ends[None, :] <= positions[:, None], segment_ends[None, :], 0), axis=1)
    lowest = jnp.maximum(positions - (WIN - 1), begun) - (first_row - REACH * tokens)
    d_query_sum, kv_grads = attention(
        query_rows, jnp.concatenate(remote + [packed_kv], axis=0), output_cotangent, lowest[:, None]
    )
    kv_grad_total = kv_grads[REACH * tokens :]
    for offset in range(1, REACH + 1):
        part = kv_grads[(REACH - offset) * tokens : (REACH - offset + 1) * tokens]
        kv_grad_total = kv_grad_total + from_behind(
            part.astype(jnp.bfloat16), "ctx", -offset
        ).astype(jnp.float32)
    d_queries = d_query_sum.reshape(tokens, q_heads, head_dim)
    key_grads = kv_grad_total[:, :kv_cols].reshape(tokens, kv_heads, head_dim)
    dq16 = (
        head_normalize_backward(d_queries, query_normalized, q_inverse, query_multiplier)
        .reshape(tokens, q_cols)
        .astype(jnp.bfloat16)
    )
    key_grads_half16 = (
        head_normalize_backward(key_grads, key_normalized, key_inverse_rms, key_norm_gain)
        .reshape(tokens, kv_cols)
        .astype(jnp.bfloat16)
    )
    value_grads_half16 = kv_grad_total[:, kv_cols:].astype(jnp.bfloat16)
    d_stacked = jnp.concatenate([dq16, key_grads_half16, value_grads_half16], axis=1)
    q_term = grad_scale * jnp.sum(d_queries * query_normalized * query_scale, axis=(0, 1))
    k_term = grad_scale * jnp.sum(key_grads * key_normalized, axis=(0, 1))
    dots = jnp.sum(d_stacked.astype(jnp.float32) * projected, axis=1)
    small = jnp.concatenate(
        [dots.reshape(4, 128), q_term[None], k_term[None], jnp.zeros((2, 128), jnp.float32)], axis=0
    )
    d_mine, weight_sum, sum_f, sum_c = both_reductions(
        gathered.reshape(fsdp_count, features, -1),
        normed_kept,
        normed_far,
        d_stacked,
        hat_mine.reshape(2, features // 2, tokens),
        small,
        grad_scale,
    )
    d_mine = d_mine.reshape(features, tokens)
    row_dot = sum_f[:4].reshape(tokens)
    upstream = d_mine * gain_mine[:, None]
    grad_inputs = (inv_row * (upstream - hat_mine * (row_dot[None, :] / model_width))).astype(jnp.bfloat16).T
    norm_row_dots = row_dot * float(model_width) ** (-0.5)
    own_features = model_width // (fsdp_count * ctx_count)
    gain_sum = lax.dynamic_slice_in_dim(
        sum_c[:6].reshape(6 * 128), ctx_index * own_features, own_features, 0
    )
    grad_q_gain, grad_k_gain = sum_c[6], sum_c[7]
    return (
        grad_inputs,
        weight_sum[:, :q_cols],
        weight_sum[:, q_cols : q_cols + kv_cols],
        weight_sum[:, q_cols + kv_cols :],
        gain_sum,
        grad_q_gain,
        grad_k_gain,
        norm_row_dots,
    )


def solution(mesh):
    placed = (
        P("ctx", None),
        P("ctx", "fsdp"),
        P("ctx", "fsdp"),
        P("ctx", "fsdp"),
        P("ctx", "fsdp"),
        P(),
        P(),
        P(),
        P(),
    )
    return jax.shard_map(
        on_device,
        mesh=mesh,
        in_specs=placed,
        out_specs=(
            P("ctx", "fsdp"),
            P("ctx", "fsdp"),
            P("ctx", "fsdp"),
            P("ctx", "fsdp"),
            P(("fsdp", "ctx")),
            P(),
            P(),
            P("ctx"),
        ),
        check_vma=False,
    )
```

```python
import jax
import jax.numpy as jnp
from jax import lax
from jax.experimental import pallas as pl
from jax.experimental.pallas import tpu as pltpu
from jax.sharding import PartitionSpec as P

WIN = 1024
REACH = 2


epsilon = 1e-06
query_scale = 168.0 ** (-0.5)


F32, BF16 = jnp.float32, jnp.bfloat16
NT = (((1,), (1,)), ((), ()))
TN = (((0,), (0,)), ((), ()))
MESH = pl.DeviceIdType.MESH
LOG2E = 1.4426950408889634


def attention_kernel(q_ref, kv_ref, do_ref, lo_ref, dq_ref, dkv_ref, v_one, e_all, mask, dkey, dval):
    tokens = q_ref.shape[0]
    half = tokens // 2
    span = 5 * half
    head = 128
    kvs = kv_ref.shape[1] // 2
    kv_heads = kvs // head
    group = q_ref.shape[1] // kvs
    ones = jnp.ones((kv_ref.shape[0], head), BF16)
    for g in range(kv_heads):
        v_one[g, :, :head] = kv_ref[:, kvs + g * head : kvs + (g + 1) * head]
        v_one[g, :, head:] = ones
    for t in range(2):
        col = lax.broadcasted_iota(jnp.int32, (half, span), 1) + t * half
        row = lax.broadcasted_iota(jnp.int32, (half, span), 0) + t * half
        low = lo_ref[t * half : (t + 1) * half, :]
        seen = (col >= low) & (col <= row + 2 * tokens)
        mask[t] = jnp.where(seen, 1.0, 0.0).astype(BF16)
    lane = lax.broadcasted_iota(jnp.int32, (half, head), 1)
    for g in range(kv_heads):
        dkey[...] = jnp.zeros_like(dkey)
        dval[...] = jnp.zeros_like(dval)
        for r in range(group):
            h = g * group + r
            hc = slice(h * head, (h + 1) * head)
            for t in range(2):
                qs = slice(t * half, (t + 1) * half)
                ks = slice(t * half, t * half + span)
                q = q_ref[qs, hc]
                keys = kv_ref[ks, g * head : (g + 1) * head]
                s = lax.dot_general(q, keys, NT, preferred_element_type=F32)
                e_all[...] = jnp.exp2(s).astype(BF16) * mask[t]
                out = jnp.dot(e_all[...], v_one[g, ks, :], preferred_element_type=F32)
                inv = 1.0 / out[:, head:]
                scaled = do_ref[qs, hc].astype(F32) * inv
                delta = jnp.sum(scaled * (out[:, :head] * inv), axis=1, keepdims=True)
                d_hi = delta.astype(BF16).astype(F32)
                tail = jnp.where(lane == 0, -d_hi, jnp.where(lane == 1, d_hi - delta, 0.0))
                scaled16 = scaled.astype(BF16)
                both = jnp.concatenate([scaled16, tail.astype(BF16)], axis=1)
                dp = lax.dot_general(both, v_one[g, ks, :], NT, preferred_element_type=F32)
                ds = dp.astype(BF16) * e_all[...]
                dq_ref[qs, hc] = jnp.dot(ds, keys, preferred_element_type=F32)
                dkey[ks, :] += lax.dot_general(ds, q, TN, preferred_element_type=F32)
                dval[ks, :] += lax.dot_general(e_all[...], scaled16, TN, preferred_element_type=F32)
        dkv_ref[:, g * head : (g + 1) * head] = dkey[...] * (1.0 / LOG2E)
        dkv_ref[:, kvs + g * head : kvs + (g + 1) * head] = dval[...]


def attention(q, kv, do, lo):
    tokens = q.shape[0]
    reach = kv.shape[0]
    half = tokens // 2
    vm = pl.BlockSpec(memory_space=pltpu.VMEM)
    return pl.pallas_call(
        attention_kernel,
        out_shape=(
            jax.ShapeDtypeStruct(q.shape, F32),
            jax.ShapeDtypeStruct(kv.shape, F32),
        ),
        in_specs=[vm] * 4,
        out_specs=(vm, vm),
        scratch_shapes=[
            pltpu.VMEM((kv.shape[1] // 256, reach, 256), BF16),
            pltpu.VMEM((half, 5 * half), BF16),
            pltpu.VMEM((2, half, 5 * half), BF16),
            pltpu.VMEM((reach, 128), F32),
            pltpu.VMEM((reach, 128), F32),
        ],
        compiler_params=pltpu.CompilerParams(vmem_limit_bytes=48 << 20),
        name="attention",
    )(q, kv, do, lo)

def both_reductions(w_ref, nt_ref, nt_far_ref, d_ref, hat_ref, small_ref, scale):
    tokens, cols = d_ref.shape
    part = w_ref.shape[1] // 16
    wing = cols // 2

    def kernel(w, nt, nt_far, d, hat, small, dn_out, wg_out, sum_f, sum_c, d_far, slots_f, slots_c, mine_c, far, near, half_in, near_in, cross, cross_in,
               swap_s, swap_r, few_s, few_r, half_s, half_r, near_s, near_r, cross_s, cross_r):
        c, f = lax.axis_index("ctx"), lax.axis_index("fsdp")
        z, x, core = c // 4, lax.rem(c // 2, 2), lax.rem(c, 2)
        xh, y = f // 4, lax.rem(f, 4)
        ring = (
            lambda k: (c, xh * 4 + lax.rem(y + k, 4)),
            lambda k: (lax.rem(z + k, 4) * 4 + x * 2 + core, f),
        )
        across = ((c, (1 - xh) * 4 + y), (z * 4 + (1 - x) * 2 + core, f))
        twin = (z * 4 + x * 2 + 1 - core, f)

        barrier = pltpu.get_barrier_semaphore()
        peers_f = [(c, lax.rem(f + k, 8)) for k in range(1, 8)]
        peers_c = [(lax.rem(c + k, 16), f) for k in range(1, 16)]
        partners = peers_f + peers_c
        for partner in partners:
            pl.semaphore_signal(barrier, inc=1, device_id=partner, device_id_type=MESH)
        pl.semaphore_wait(barrier, len(partners))

        def copy(src, dst, ss, rs, to):
            return pltpu.make_async_remote_copy(
                src_ref=src, dst_ref=dst, send_sem=ss, recv_sem=rs, device_id=to, device_id_type=MESH
            )

        swap = copy(d, d_far, swap_s, swap_r, twin)
        swap.start()
        slots_f[f] = small[...]
        few = [
            copy(small, slots_f.at[f], few_s.at[k], few_r.at[k], to) for k, to in enumerate(peers_f)
        ]
        for cp in few:
            cp.start()

        def term(m, s, k, h):
            if m == 0:
                block = (xh if s else 1 - xh) * 4 + lax.rem(y + k, 4)
                rows = pl.ds(pl.multiple_of((block * 2 + h) * part, 16), part)
                total = lax.dot_general(w[0, rows, :], d[:, :wing], NT, preferred_element_type=F32)
                total += lax.dot_general(w[1, rows, :], d[:, wing:], NT, preferred_element_type=F32)
                return total
            block = lax.rem(z + k, 4) * 2 + (x if s else 1 - x)
            hs = slice(h * wing, (h + 1) * wing)
            rows = pl.ds(pl.multiple_of((block * 2 + core) * part, 16), part)
            total = jnp.dot(nt[rows, :], d[:, hs], preferred_element_type=F32)
            total += jnp.dot(nt_far[block], d_far[:, hs], preferred_element_type=F32)
            return total * scale

        sent = []

        def send_far(m, s):
            for h in range(2):
                far[m, s, h] = term(m, s, 2, h).astype(BF16)
                cp = copy(far.at[m, s, h], half_in.at[m, s, h], half_s.at[m, s, h], half_r.at[m, s, h],
                          ring[m](1 if h == 0 else 3))
                cp.start()
                sent.append(cp)
                halves[m, s, h] = cp

        def make_near(m, s):
            for n, k in enumerate((1, 3)):
                for h in range(2):
                    near[m, s, n, h] = term(m, s, k, h).astype(BF16)

        def send_near(m, s):
            for n, k in enumerate((1, 3)):
                halves[m, s, n].wait_recv()
                near[m, s, n, n] = (near[m, s, n, n].astype(F32) + half_in[m, s, n].astype(F32)).astype(BF16)
                cp = copy(near.at[m, s, n], near_in.at[m, s, n], near_s.at[m, s, n], near_r.at[m, s, n], ring[m](k))
                cp.start()
                sent.append(cp)
                nears[m, s, n] = cp

        def arrived(m, s, h):
            return near_in[m, s, 0, h].astype(F32) + near_in[m, s, 1, h].astype(F32)

        halves, nears, crossed = {}, {}, {}
        send_far(0, 0)
        send_far(0, 1)
        swap.wait_recv()
        send_far(1, 0)
        send_far(1, 1)
        make_near(0, 0)
        send_near(0, 0)
        make_near(1, 0)
        send_near(1, 0)
        make_near(0, 1)
        send_near(0, 1)
        make_near(1, 1)
        send_near(1, 1)
        for cp in few:
            cp.wait_recv()
        total_f = slots_f[0]
        for k in range(1, 8):
            total_f = total_f + slots_f[k]
        sum_f[...] = total_f
        for m in range(2):
            for h in range(2):
                if h == 0:
                    mine = [term(m, 0, 0, 0), term(m, 0, 0, 1)]
                    for n in range(2):
                        nears[m, 0, n].wait_recv()
                cross[m, h] = (mine[h] + arrived(m, 0, h)).astype(BF16)
            cp = copy(cross.at[m], cross_in.at[m], cross_s.at[m], cross_r.at[m], across[m])
            cp.start()
            sent.append(cp)
            crossed[m] = cp
        for h in range(2):
            dn_out[h] = term(0, 1, 0, h)
        weights = [term(1, 1, 0, h) for h in range(2)]
        for n in range(2):
            nears[0, 1, n].wait_recv()
        crossed[0].wait_recv()
        spread = jnp.zeros((8, 128), F32)
        for h in range(2):
            total = dn_out[h] + arrived(0, 1, h) + cross_in[0, h].astype(F32)
            dn_out[h] = total
            sums = scale * jnp.sum(total * hat[h], axis=1, keepdims=True)
            at = lax.broadcasted_iota(jnp.int32, (part, 128), 0) + h * part
            lane = lax.broadcasted_iota(jnp.int32, (part, 128), 1)
            to_row = jnp.where(at // 128 == lane, sums, 0.0)
            to_lane = jnp.where(lax.rem(at, 128) == lane, 1.0, 0.0)
            spread += lax.dot_general(
                to_row.astype(BF16), to_lane.astype(BF16), TN, preferred_element_type=F32
            )[:8]
        mine_c[...] = spread
        mine_c[6:8, :] = total_f[4:6, :]
        slots_c[c] = mine_c[...]
        few_c = [
            copy(mine_c, slots_c.at[c], few_s.at[7 + k], few_r.at[7 + k], to) for k, to in enumerate(peers_c)
        ]
        for cp in few_c:
            cp.start()
        for n in range(2):
            nears[1, 1, n].wait_recv()
        crossed[1].wait_recv()
        for h in range(2):
            total = weights[h] + arrived(1, 1, h) + cross_in[1, h].astype(F32)
            wg_out[:, h * wing : (h + 1) * wing] = total.astype(BF16)
        for cp in few_c:
            cp.wait_recv()
        total_c = slots_c[0]
        for k in range(1, 16):
            total_c = total_c + slots_c[k]
        sum_c[...] = total_c
        for cp in [swap] + few + few_c + sent:
            cp.wait_send()

    vm = pl.BlockSpec(memory_space=pltpu.VMEM)
    dma = pltpu.SemaphoreType.DMA
    block = (2, part, tokens)
    return pl.pallas_call(
        kernel,
        out_shape=(
            jax.ShapeDtypeStruct(block, F32),
            jax.ShapeDtypeStruct((part, cols), BF16),
            jax.ShapeDtypeStruct((8, 128), F32),
            jax.ShapeDtypeStruct((8, 128), F32),
        ),
        in_specs=[vm] * 6,
        out_specs=(vm,) * 4,
        scratch_shapes=[
            pltpu.VMEM((tokens, cols), BF16),
            pltpu.VMEM((8, 8, 128), F32),
            pltpu.VMEM((16, 8, 128), F32),
            pltpu.VMEM((8, 128), F32),
            pltpu.VMEM((2, 2) + block, BF16),
            pltpu.VMEM((2, 2, 2) + block, BF16),
            pltpu.VMEM((2, 2) + block, BF16),
            pltpu.VMEM((2, 2, 2) + block, BF16),
            pltpu.VMEM((2,) + block, BF16),
            pltpu.VMEM((2,) + block, BF16),
            dma, dma,
            dma((22,)), dma((22,)),
            dma((2, 2, 2)), dma((2, 2, 2)),
            dma((2, 2, 2)), dma((2, 2, 2)),
            dma((2,)), dma((2,)),
        ],
        compiler_params=pltpu.CompilerParams(
            collective_id=1, has_side_effects=True, vmem_limit_bytes=60 << 20
        ),
        name="both_reductions",
    )(w_ref, nt_ref, nt_far_ref, d_ref, hat_ref, small_ref)


def gather_and_project(x_ref, wq_ref, wk_ref, wv_ref, gain_ref, q_mul_ref, k_mul_ref):
    tokens, width = x_ref.shape
    deep, q_cols = wq_ref.shape
    kv_cols = wk_ref.shape[1]
    head = q_mul_ref.shape[1]
    wing = q_cols // 2

    def kernel(x, wq, wk, wv, gain, q_mul, k_mul, w_all, nt, nt_far, proj, q16, kv, inv, normed,
               x_s, x_r, near_s, near_r, far_s, far_r, twin_s, twin_r, swap_s, swap_r, kv_s, kv_r):
        c, f = lax.axis_index("ctx"), lax.axis_index("fsdp")
        z, xl, core = c // 4, lax.rem(c // 2, 2), lax.rem(c, 2)
        twin = (z * 4 + xl * 2 + 1 - core, f)
        mate = (z * 4 + (1 - xl) * 2 + core, f)
        along = lambda k: (lax.rem(z + k, 4) * 4 + xl * 2 + core, f)
        later = [(lax.rem(c + k, 16), f) for k in (1, 2)]
        earlier = [(lax.rem(c + 16 - k, 16), f) for k in (1, 2)]

        barrier = pltpu.get_barrier_semaphore()
        for to in [twin, mate, along(1), along(3)] + later + earlier:
            pl.semaphore_signal(barrier, inc=1, device_id=to, device_id_type=MESH)
        pl.semaphore_wait(barrier, 8)

        def rows(k, xx, who=None):
            place = lax.rem(z + k, 4) * 4 + (1 - xl if xx else xl) * 2 + (core if who is None else who)
            return pl.ds(pl.multiple_of(place * deep, 16), deep)

        def copy(src, dst, ss, rs, to):
            return pltpu.make_async_remote_copy(
                src_ref=src, dst_ref=dst, send_sem=ss, recv_sem=rs, device_id=to, device_id_type=MESH
            )

        started = []

        def go(ref, ss, rs, to):
            cp = copy(ref, ref, ss, rs, to)
            cp.start()
            started.append(cp)

        def wait_for(ref, ss, rs):
            copy(ref, ref, ss, rs, twin).wait_recv()

        def to_twin(s, k, xx):
            go(w_all.at[s, rows(k, xx)], twin_s.at[s, xx, k], twin_r.at[s, xx, k], twin)

        def to_near(s, xx):
            for n, k in enumerate((1, 3)):
                go(w_all.at[s, rows(0, xx)], near_s.at[s, xx, n], near_r.at[s, xx, n], along(k))

        def near_and_forward(s, xx):
            for n, k in enumerate((3, 1)):
                wait_for(w_all.at[s, rows(k, xx)], near_s.at[s, xx, n], near_r.at[s, xx, n])
                go(w_all.at[s, rows(k, xx), pl.ds(n * wing, wing)], far_s.at[s, xx, n], far_r.at[s, xx, n],
                   along(1 if n == 0 else 3))
                to_twin(s, k, xx)

        def far(s, xx):
            for n in range(2):
                wait_for(w_all.at[s, rows(2, xx), pl.ds(n * wing, wing)], far_s.at[s, xx, n], far_r.at[s, xx, n])
            to_twin(s, 2, xx)

        def to_mate(s):
            go(w_all.at[s, rows(0, 0)], x_s.at[s], x_r.at[s], mate)

        def from_mate(s):
            wait_for(w_all.at[s, rows(0, 1)], x_s.at[s], x_r.at[s])

        def all_from_twin(s, ks):
            for xx in range(2):
                for k in ks:
                    wait_for(w_all.at[s, rows(k, xx, 1 - core)], twin_s.at[s, xx, k], twin_r.at[s, xx, k])

        w_all[1, rows(0, 0), :kv_cols] = wk[...]
        w_all[1, rows(0, 0), kv_cols:] = wv[...]
        to_mate(1)
        to_near(1, 0)
        w_all[0, rows(0, 0), :] = wq[...]
        to_twin(1, 0, 0)

        tile = 32

        def norm_tile(i, carry):
            at = pl.ds(pl.multiple_of(i * tile, tile), tile)
            wide = x[at, :].astype(F32)
            one = lax.rsqrt(jnp.sum(wide * wide, axis=1, keepdims=True) * (1.0 / width) + epsilon)
            inv[at, :] = one
            normed[at, :] = (wide * one * gain[...]).astype(BF16)
            return carry

        lax.fori_loop(0, tokens // tile, norm_tile, 0)
        from_mate(1)
        to_near(1, 1)
        to_mate(0)
        to_twin(1, 0, 1)

        strip = 256

        def turn(i, carry):
            at = pl.ds(pl.multiple_of(i * strip, strip), strip)
            nt[at, :] = normed[:, at].T
            return carry

        near_and_forward(1, 0)
        to_near(0, 0)
        to_twin(0, 0, 0)
        lax.fori_loop(0, width // strip, turn, 0)
        near_and_forward(1, 1)
        from_mate(0)
        to_near(0, 1)
        to_twin(0, 0, 1)
        swaps = []
        for j in range(8):
            src = pl.ds(pl.multiple_of((j * 2 + 1 - core) * deep, 16), deep)
            cp = copy(nt.at[src], nt_far.at[j], swap_s.at[j], swap_r.at[j], twin)
            cp.start()
            swaps.append(cp)
        far(1, 0)
        far(1, 1)
        all_from_twin(1, range(4))
        proj[:, q_cols:] = jnp.dot(normed[...], w_all[1], preferred_element_type=F32)

        def head_norm(raw, mul):
            one = lax.rsqrt(jnp.mean(raw * raw, axis=1, keepdims=True) + epsilon)
            return (raw * one * mul).astype(BF16)

        last = pl.ds(2 * tokens, tokens)
        for g in range(kv_cols // head):
            at = slice(q_cols + g * head, q_cols + (g + 1) * head)
            kv[last, g * head : (g + 1) * head] = head_norm(proj[:, at], k_mul[...])
        kv[last, kv_cols:] = proj[:, q_cols + kv_cols :].astype(BF16)
        passed = []
        for n in range(2):
            cp = copy(kv.at[last], kv.at[pl.ds((1 - n) * tokens, tokens)], kv_s.at[n], kv_r.at[n], later[n])
            cp.start()
            passed.append(cp)
        near_and_forward(0, 0)
        near_and_forward(0, 1)
        all_from_twin(0, (0, 1, 3))
        span = width // 2
        pair = z // 2
        near_half = pl.ds(pl.multiple_of(pair * span, 128), span)
        proj[:, :q_cols] = jnp.dot(normed[:, near_half], w_all[0, near_half, :], preferred_element_type=F32)
        far(0, 0)
        far(0, 1)
        all_from_twin(0, (2,))
        far_half = pl.ds(pl.multiple_of((1 - pair) * span, 128), span)
        proj[:, :q_cols] += jnp.dot(normed[:, far_half], w_all[0, far_half, :], preferred_element_type=F32)
        for h in range(q_cols // head):
            at = slice(h * head, (h + 1) * head)
            q16[:, at] = head_norm(proj[:, at], q_mul[...])
        for cp in passed + swaps:
            cp.wait_recv()
        for cp in passed + swaps + started:
            cp.wait_send()

    vm = pl.BlockSpec(memory_space=pltpu.VMEM)
    dma = pltpu.SemaphoreType.DMA
    return pl.pallas_call(
        kernel,
        out_shape=(
            jax.ShapeDtypeStruct((2, width, q_cols), BF16),
            jax.ShapeDtypeStruct((width, tokens), BF16),
            jax.ShapeDtypeStruct((8, deep, tokens), BF16),
            jax.ShapeDtypeStruct((tokens, 2 * q_cols), F32),
            jax.ShapeDtypeStruct((tokens, q_cols), BF16),
            jax.ShapeDtypeStruct((3 * tokens, 2 * kv_cols), BF16),
            jax.ShapeDtypeStruct((tokens, 1), F32),
        ),
        in_specs=[vm] * 7,
        out_specs=(vm,) * 7,
        scratch_shapes=[
            pltpu.VMEM((tokens, width), BF16),
            dma((2,)), dma((2,)),
            dma((2, 2, 2)), dma((2, 2, 2)),
            dma((2, 2, 2)), dma((2, 2, 2)),
            dma((2, 2, 4)), dma((2, 2, 4)),
            dma((8,)), dma((8,)),
            dma((2,)), dma((2,)),
        ],
        compiler_params=pltpu.CompilerParams(
            collective_id=2, has_side_effects=True, vmem_limit_bytes=60 << 20
        ),
        name="gather_and_project",
    )(x_ref, wq_ref, wk_ref, wv_ref, gain_ref, q_mul_ref, k_mul_ref)


def from_behind(value, axis, steps):
    count = lax.axis_size(axis)
    initial, last = (max(0, -steps), min(count, count - steps))
    return lax.ppermute(value, axis, [(source, source + steps) for source in range(initial, last)])


def head_normalize(projected, head_count, head_dim):
    shaped = projected.reshape(projected.shape[0], head_count, head_dim)
    inverse = lax.rsqrt(jnp.mean(shaped * shaped, axis=2, keepdims=True) + epsilon)
    return (shaped * inverse, inverse)


def head_normalize_backward(upstream_grad, normal_part, inverse, gain_vector):
    upstream = upstream_grad * gain_vector
    return inverse * (
        upstream - normal_part * jnp.mean(upstream * normal_part, axis=2, keepdims=True)
    )


def on_device(
    inputs,
    output_cotangent,
    w_query,
    key_projection,
    value_projection,
    norm_gain,
    q_gain,
    key_norm_gain,
    half_lengths,
):
    tokens = inputs.shape[0]
    model_width = inputs.shape[1]
    head_dim = q_gain.shape[0]
    q_cols = w_query.shape[1]
    kv_cols = key_projection.shape[1]
    q_heads = q_cols // head_dim
    kv_heads = kv_cols // head_dim
    ctx_count = lax.axis_size("ctx")
    ctx_index = lax.axis_index("ctx")
    first_row = ctx_index * tokens
    grad_scale = float(tokens * ctx_count) ** (-0.5)
    query_multiplier = q_gain * query_scale
    gathered, normed_t, normed_far, projected, query_rows, kv_span, inv_rms = gather_and_project(
        inputs, w_query, key_projection, value_projection, norm_gain[None],
        (query_multiplier * LOG2E)[None], key_norm_gain[None],
    )
    inv_row = inv_rms.reshape(1, tokens)
    fsdp_index = lax.axis_index("fsdp")
    fsdp_count = lax.axis_size("fsdp")
    features = model_width // fsdp_count
    hat_mine = (
        lax.dynamic_slice_in_dim(inputs, fsdp_index * features, features, 1).T.astype(jnp.float32) * inv_row
    )
    gain_mine = lax.dynamic_slice_in_dim(norm_gain, fsdp_index * features, features, 0)
    q_raw = projected[:, :q_cols]
    key_unnormed = projected[:, q_cols : q_cols + kv_cols]
    query_normalized, q_inverse = head_normalize(q_raw, q_heads, head_dim)
    key_normalized, key_inverse_rms = head_normalize(key_unnormed, kv_heads, head_dim)
    halves = half_lengths.shape[0]
    upto = lax.iota(jnp.int32, halves)[None, :] <= lax.iota(jnp.int32, halves)[:, None]
    segment_ends = jnp.sum(jnp.where(upto, half_lengths[None, :], 0), axis=1)
    positions = first_row + lax.iota(jnp.int32, tokens)
    begun = jnp.max(jnp.where(segment_ends[None, :] <= positions[:, None], segment_ends[None, :], 0), axis=1)
    lowest = jnp.maximum(positions - (WIN - 1), begun) - (first_row - REACH * tokens)
    d_query_sum, kv_grads = attention(
        query_rows, kv_span, output_cotangent, lowest[:, None]
    )
    kv_grad_total = kv_grads[REACH * tokens :]
    for offset in range(1, REACH + 1):
        part = kv_grads[(REACH - offset) * tokens : (REACH - offset + 1) * tokens]
        kv_grad_total = kv_grad_total + from_behind(
            part.astype(jnp.bfloat16), "ctx", -offset
        ).astype(jnp.float32)
    d_queries = d_query_sum.reshape(tokens, q_heads, head_dim)
    key_grads = kv_grad_total[:, :kv_cols].reshape(tokens, kv_heads, head_dim)
    dq16 = (
        head_normalize_backward(d_queries, query_normalized, q_inverse, query_multiplier)
        .reshape(tokens, q_cols)
        .astype(jnp.bfloat16)
    )
    key_grads_half16 = (
        head_normalize_backward(key_grads, key_normalized, key_inverse_rms, key_norm_gain)
        .reshape(tokens, kv_cols)
        .astype(jnp.bfloat16)
    )
    value_grads_half16 = kv_grad_total[:, kv_cols:].astype(jnp.bfloat16)
    d_stacked = jnp.concatenate([dq16, key_grads_half16, value_grads_half16], axis=1)
    q_term = grad_scale * jnp.sum(d_queries * query_normalized * query_scale, axis=(0, 1))
    k_term = grad_scale * jnp.sum(key_grads * key_normalized, axis=(0, 1))
    dots = jnp.sum(d_stacked.astype(jnp.float32) * projected, axis=1)
    small = jnp.concatenate(
        [dots.reshape(4, 128), q_term[None], k_term[None], jnp.zeros((2, 128), jnp.float32)], axis=0
    )
    d_mine, weight_sum, sum_f, sum_c = both_reductions(
        gathered,
        normed_t,
        normed_far,
        d_stacked,
        hat_mine.reshape(2, features // 2, tokens),
        small,
        grad_scale,
    )
    d_mine = d_mine.reshape(features, tokens)
    row_dot = sum_f[:4].reshape(tokens)
    upstream = d_mine * gain_mine[:, None]
    grad_inputs = (inv_row * (upstream - hat_mine * (row_dot[None, :] / model_width))).astype(jnp.bfloat16).T
    norm_row_dots = row_dot * float(model_width) ** (-0.5)
    own_features = model_width // (fsdp_count * ctx_count)
    gain_sum = lax.dynamic_slice_in_dim(
        sum_c[:6].reshape(6 * 128), ctx_index * own_features, own_features, 0
    )
    grad_q_gain, grad_k_gain = sum_c[6], sum_c[7]
    return (
        grad_inputs,
        weight_sum[:, :q_cols],
        weight_sum[:, q_cols : q_cols + kv_cols],
        weight_sum[:, q_cols + kv_cols :],
        gain_sum,
        grad_q_gain,
        grad_k_gain,
        norm_row_dots,
    )


def solution(mesh):
    placed = (
        P("ctx", None),
        P("ctx", "fsdp"),
        P("ctx", "fsdp"),
        P("ctx", "fsdp"),
        P("ctx", "fsdp"),
        P(),
        P(),
        P(),
        P(),
    )
    return jax.shard_map(
        on_device,
        mesh=mesh,
        in_specs=placed,
        out_specs=(
            P("ctx", "fsdp"),
            P("ctx", "fsdp"),
            P("ctx", "fsdp"),
            P("ctx", "fsdp"),
            P(("fsdp", "ctx")),
            P(),
            P(),
            P("ctx"),
        ),
        check_vma=False,
    )
```

```python
import jax
import jax.numpy as jnp
from jax import lax
from jax.experimental import pallas as pl
from jax.experimental.pallas import tpu as pltpu
from jax.sharding import PartitionSpec as P

WIN = 1024
REACH = 2


epsilon = 1e-06
query_scale = 168.0 ** (-0.5)


F32, BF16 = jnp.float32, jnp.bfloat16
NT = (((1,), (1,)), ((), ()))
TN = (((0,), (0,)), ((), ()))
MESH = pl.DeviceIdType.MESH
LOG2E = 1.4426950408889634


def attention_and_reductions(w_ref, nt_ref, nt_far_ref, q_ref, kv_ref, do_ref, lo_ref, proj_ref, q_mul_ref, k_mul_ref,
                             x_mine_ref, inv_ref, scale, q_scale):
    tokens, q_cols = q_ref.shape
    cols = proj_ref.shape[1]
    part = w_ref.shape[1] // 16
    wing = cols // 2
    kvs = kv_ref.shape[1] // 2
    head = q_mul_ref.shape[1]
    kv_heads = kvs // head
    group = q_cols // kvs
    half = tokens // 2
    span = 5 * half
    reach = kv_ref.shape[0]
    quarter = tokens // 2

    def kernel(w_hbm, nt_hbm, nt_far_hbm, q, kv, do, lo, proj, q_mul, k_mul, x_mine, inv,
               dn_out, wg_out, sum_f, sum_c,
               w, nt, nt_far, v_one, e_all, mask, dkey, dval, kvg, kvg_in, own_kv, d, d_far, small,
               slots_f, slots_c, mine_c, far, near, far_in, near_in, cross, cross_in,
               fetch_sem, kvg_s, kvg_r, swap_s, swap_r, few_s, few_r, far_s, far_r, near_s, near_r, cross_s, cross_r):
        c, f = lax.axis_index("ctx"), lax.axis_index("fsdp")
        z, x, core = c // 4, lax.rem(c // 2, 2), lax.rem(c, 2)
        xh, y = f // 4, lax.rem(f, 4)
        ring = (
            lambda k: (c, xh * 4 + lax.rem(y + k, 4)),
            lambda k: (lax.rem(z + k, 4) * 4 + x * 2 + core, f),
        )
        across = ((c, (1 - xh) * 4 + y), (z * 4 + (1 - x) * 2 + core, f))
        twin = (z * 4 + x * 2 + 1 - core, f)
        peers_f = [(c, lax.rem(f + k, 8)) for k in range(1, 8)]
        peers_c = [(lax.rem(c + k, 16), f) for k in range(1, 16)]

        def rows_of(block):
            return pl.ds(pl.multiple_of(block * part, 16), part)

        barrier = pltpu.get_barrier_semaphore()
        partners = peers_f + peers_c
        for partner in partners:
            pl.semaphore_signal(barrier, inc=1, device_id=partner, device_id_type=MESH)
        fetches = [pltpu.make_async_copy(nt_hbm.at[rows_of(j * 2 + core)], nt.at[j], fetch_sem.at[j]) for j in range(8)]
        fetches.append(pltpu.make_async_copy(nt_far_hbm, nt_far, fetch_sem.at[8]))
        fetches.append(pltpu.make_async_copy(w_hbm, w, fetch_sem.at[9]))
        for cp in fetches:
            cp.start()

        def copy(src, dst, ss, rs, to):
            return pltpu.make_async_remote_copy(
                src_ref=src, dst_ref=dst, send_sem=ss, recv_sem=rs, device_id=to, device_id_type=MESH
            )

        sent = []

        def go(*what):
            cp = copy(*what)
            cp.start()
            sent.append(cp)
            return cp

        ones = jnp.ones((reach, head), BF16)
        for g in range(kv_heads):
            v_one[g, :, :head] = kv[:, kvs + g * head : kvs + (g + 1) * head]
            v_one[g, :, head:] = ones
        for t in range(2):
            col = lax.broadcasted_iota(jnp.int32, (half, span), 1) + t * half
            row = lax.broadcasted_iota(jnp.int32, (half, span), 0) + t * half
            seen = (col >= lo[t * half : (t + 1) * half, :]) & (col <= row + 2 * tokens)
            mask[t] = jnp.where(seen, 1.0, 0.0).astype(BF16)
        lane = lax.broadcasted_iota(jnp.int32, (half, head), 1)

        def norm_back(grad, raw, mul):
            one = lax.rsqrt(jnp.mean(raw * raw, axis=1, keepdims=True) + epsilon)
            hat = raw * one
            up = grad * mul
            back = one * (up - hat * jnp.mean(up * hat, axis=1, keepdims=True))
            return back.astype(BF16), jnp.sum(grad * hat, axis=0, keepdims=True)

        q_term = jnp.zeros((1, head), F32)
        kv_copies = []
        for g in range(kv_heads):
            dkey[...] = jnp.zeros_like(dkey)
            dval[...] = jnp.zeros_like(dval)
            for r in range(group):
                h = g * group + r
                hc = slice(h * head, (h + 1) * head)
                for t in range(2):
                    qs = slice(t * half, (t + 1) * half)
                    ks = slice(t * half, t * half + span)
                    qt = q[qs, hc]
                    keys = kv[ks, g * head : (g + 1) * head]
                    s = lax.dot_general(qt, keys, NT, preferred_element_type=F32)
                    e_all[...] = jnp.exp2(s).astype(BF16) * mask[t]
                    out = jnp.dot(e_all[...], v_one[g, ks, :], preferred_element_type=F32)
                    inv_l = 1.0 / out[:, head:]
                    scaled = do[qs, hc].astype(F32) * inv_l
                    delta = jnp.sum(scaled * (out[:, :head] * inv_l), axis=1, keepdims=True)
                    d_hi = delta.astype(BF16).astype(F32)
                    tail = jnp.where(lane == 0, -d_hi, jnp.where(lane == 1, d_hi - delta, 0.0))
                    scaled16 = scaled.astype(BF16)
                    both = jnp.concatenate([scaled16, tail.astype(BF16)], axis=1)
                    dp = lax.dot_general(both, v_one[g, ks, :], NT, preferred_element_type=F32)
                    ds = dp.astype(BF16) * e_all[...]
                    dq = jnp.dot(ds, keys, preferred_element_type=F32)
                    dkey[ks, :] += lax.dot_general(ds, qt, TN, preferred_element_type=F32)
                    dval[ks, :] += lax.dot_general(e_all[...], scaled16, TN, preferred_element_type=F32)
                    d[qs, hc], term_q = norm_back(dq, proj[qs, hc], q_mul[...])
                    q_term += term_q
            if g == 0:
                pl.semaphore_wait(barrier, len(partners))
            for n in range(2):
                away = slice((1 - n) * tokens, (2 - n) * tokens)
                kvg[g, n, :, :head] = (dkey[away, :] * (1.0 / LOG2E)).astype(BF16)
                kvg[g, n, :, head:] = dval[away, :].astype(BF16)
                kv_copies.append(
                    go(kvg.at[g, n], kvg_in.at[g, n], kvg_s.at[g, n], kvg_r.at[g, n], (lax.rem(c + 15 - n, 16), f))
                )
            own_kv[:, g * head : (g + 1) * head] = dkey[2 * tokens :, :] * (1.0 / LOG2E)
            own_kv[:, kvs + g * head : kvs + (g + 1) * head] = dval[2 * tokens :, :]
        swap_q = go(d.at[:, pl.ds(0, wing)], d_far.at[:, pl.ds(0, wing)], swap_s.at[0], swap_r.at[0], twin)

        def term(m, s, k, h):
            if m == 0:
                block = (xh if s else 1 - xh) * 4 + lax.rem(y + k, 4)
                rows = rows_of(block * 2 + h)
                total = lax.dot_general(w[0, rows, :], d[:, :wing], NT, preferred_element_type=F32)
                total += lax.dot_general(w[1, rows, :], d[:, wing:], NT, preferred_element_type=F32)
                return total
            block = lax.rem(z + k, 4) * 2 + (x if s else 1 - x)
            hs = slice(h * wing, (h + 1) * wing)
            total = jnp.dot(nt[block], d[:, hs], preferred_element_type=F32)
            total += jnp.dot(nt_far[block], d_far[:, hs], preferred_element_type=F32)
            return total * scale

        fars, nears, crossed = {}, {}, {}

        def send_far(m, s, h):
            far[m, s, h] = term(m, s, 2, h).astype(BF16)
            for n, k in enumerate((1, 3)):
                fars[m, s, h, n] = go(
                    far.at[m, s, h, :, pl.ds(n * quarter, quarter)], far_in.at[m, s, h, n],
                    far_s.at[m, s, h, n], far_r.at[m, s, h, n], ring[m](k),
                )

        def make_near(m, s, h):
            for n, k in enumerate((1, 3)):
                near[m, s, n, h] = term(m, s, k, h).astype(BF16)

        def send_near(m, s, h):
            for n, k in enumerate((1, 3)):
                fars[m, s, h, n].wait_recv()
                at = slice(n * quarter, (n + 1) * quarter)
                near[m, s, n, h, :, at] = (
                    near[m, s, n, h, :, at].astype(F32) + far_in[m, s, h, n].astype(F32)
                ).astype(BF16)
                nears[m, s, n, h] = go(
                    near.at[m, s, n, h], near_in.at[m, s, n, h], near_s.at[m, s, n, h], near_r.at[m, s, n, h], ring[m](k)
                )

        def arrived(m, s, h):
            for n in range(2):
                nears[m, s, n, h].wait_recv()
            return near_in[m, s, 0, h].astype(F32) + near_in[m, s, 1, h].astype(F32)

        def send_cross(m, h):
            mine = term(m, 0, 0, h)
            cross[m, h] = (mine + arrived(m, 0, h)).astype(BF16)
            crossed[m, h] = go(cross.at[m, h], cross_in.at[m, h], cross_s.at[m, h], cross_r.at[m, h], across[m])

        for cp in fetches[:9]:
            cp.wait()
        swap_q.wait_recv()
        send_far(1, 0, 0)
        make_near(1, 0, 0)
        send_near(1, 0, 0)

        k_term = jnp.zeros((1, head), F32)
        for cp in kv_copies:
            cp.wait_recv()
        for g in range(kv_heads):
            at = slice(g * head, (g + 1) * head)
            there = slice(wing + g * head, wing + (g + 1) * head)
            grad = own_kv[:, at] + (kvg_in[g, 0, :, :head].astype(F32) + kvg_in[g, 1, :, :head].astype(F32))
            d[:, there], term_k = norm_back(grad, proj[:, there], k_mul[...])
            k_term += term_k
            at = slice(kvs + g * head, kvs + (g + 1) * head)
            grad = own_kv[:, at] + (kvg_in[g, 0, :, head:].astype(F32) + kvg_in[g, 1, :, head:].astype(F32))
            d[:, wing + kvs + g * head : wing + kvs + (g + 1) * head] = grad.astype(BF16)
        swap_kv = go(d.at[:, pl.ds(wing, wing)], d_far.at[:, pl.ds(wing, wing)], swap_s.at[1], swap_r.at[1], twin)
        fetches[9].wait()
        send_far(0, 0, 0)
        make_near(0, 0, 0)
        send_far(0, 0, 1)
        send_near(0, 0, 0)
        swap_kv.wait_recv()
        send_far(1, 0, 1)
        make_near(0, 0, 1)
        send_far(0, 1, 0)
        send_near(0, 0, 1)
        make_near(1, 0, 1)
        send_far(1, 1, 0)
        send_near(1, 0, 1)

        product = d[...].astype(F32) * proj[...]
        upper = product.astype(BF16)
        lower = (product - upper.astype(F32)).astype(BF16)
        ones_row = jnp.ones((8, cols), BF16)
        dots = lax.dot_general(ones_row, upper, NT, preferred_element_type=F32)
        dots += lax.dot_general(ones_row, lower, NT, preferred_element_type=F32)
        small[...] = dots
        small[1:2, :head] = q_term * (scale * q_scale)
        small[1:2, head : 2 * head] = k_term * scale
        slots_f[f] = small[...]
        few = [go(small, slots_f.at[f], few_s.at[k], few_r.at[k], to) for k, to in enumerate(peers_f)]

        send_cross(0, 0)
        make_near(0, 1, 0)
        send_far(0, 1, 1)
        send_near(0, 1, 0)
        send_cross(1, 0)
        send_cross(0, 1)
        make_near(1, 1, 0)
        send_far(1, 1, 1)
        send_near(1, 1, 0)
        send_cross(1, 1)
        make_near(0, 1, 1)
        send_near(0, 1, 1)
        make_near(1, 1, 1)
        send_near(1, 1, 1)
        for cp in few:
            cp.wait_recv()
        total_f = slots_f[0]
        for k in range(1, 8):
            total_f = total_f + slots_f[k]
        sum_f[...] = total_f
        for h in range(2):
            dn_out[h] = term(0, 1, 0, h)
        for h in range(2):
            own_kv[:part, :] = term(1, 1, 0, h)
            crossed[1, h].wait_recv()
            total = own_kv[:part, :] + cross_in[1, h].astype(F32) + arrived(1, 1, h)
            wg_out[:, h * wing : (h + 1) * wing] = total.astype(BF16)
        spread = jnp.zeros((128, 128), F32)
        for h in range(2):
            crossed[0, h].wait_recv()
            total = dn_out[h] + cross_in[0, h].astype(F32) + arrived(0, 1, h)
            dn_out[h] = total
            hat = x_mine[h * part : (h + 1) * part, :].astype(F32) * inv[...]
            sums = scale * jnp.sum(total * hat, axis=1, keepdims=True)
            at = lax.broadcasted_iota(jnp.int32, (part, 128), 0) + h * part
            lanes = lax.broadcasted_iota(jnp.int32, (part, 128), 1)
            to_row = jnp.where(at // 128 == lanes, sums, 0.0)
            to_lane = jnp.where(lax.rem(at, 128) == lanes, 1.0, 0.0)
            spread += lax.dot_general(to_row.astype(BF16), to_lane.astype(BF16), TN, preferred_element_type=F32)
        mine_c[...] = spread[:8]
        mine_c[6:7, :] = total_f[1:2, :head]
        mine_c[7:8, :] = total_f[1:2, head : 2 * head]
        slots_c[c] = mine_c[...]
        few_c = [go(mine_c, slots_c.at[c], few_s.at[7 + k], few_r.at[7 + k], to) for k, to in enumerate(peers_c)]
        for cp in few_c:
            cp.wait_recv()
        total_c = slots_c[0]
        for k in range(1, 16):
            total_c = total_c + slots_c[k]
        sum_c[...] = total_c
        for cp in sent:
            cp.wait_send()

    vm = pl.BlockSpec(memory_space=pltpu.VMEM)
    anywhere = pl.BlockSpec(memory_space=pl.ANY)
    dma = pltpu.SemaphoreType.DMA
    block = (2, part, tokens)
    return pl.pallas_call(
        kernel,
        out_shape=(
            jax.ShapeDtypeStruct(block, F32),
            jax.ShapeDtypeStruct((part, cols), BF16),
            jax.ShapeDtypeStruct((8, tokens), F32),
            jax.ShapeDtypeStruct((8, 128), F32),
        ),
        in_specs=[anywhere] * 3 + [vm] * 9,
        out_specs=(vm,) * 4,
        scratch_shapes=[
            pltpu.VMEM(w_ref.shape, BF16),
            pltpu.VMEM((8, part, tokens), BF16),
            pltpu.VMEM((8, part, tokens), BF16),
            pltpu.VMEM((kv_heads, reach, 2 * head), BF16),
            pltpu.VMEM((half, span), BF16),
            pltpu.VMEM((2, half, span), BF16),
            pltpu.VMEM((reach, head), F32),
            pltpu.VMEM((reach, head), F32),
            pltpu.VMEM((2, 2, tokens, 2 * head), BF16),
            pltpu.VMEM((2, 2, tokens, 2 * head), BF16),
            pltpu.VMEM((tokens, 2 * kvs), F32),
            pltpu.VMEM((tokens, cols), BF16),
            pltpu.VMEM((tokens, cols), BF16),
            pltpu.VMEM((8, tokens), F32),
            pltpu.VMEM((8, 8, tokens), F32),
            pltpu.VMEM((16, 8, 128), F32),
            pltpu.VMEM((8, 128), F32),
            pltpu.VMEM((2, 2) + block, BF16),
            pltpu.VMEM((2, 2, 2) + block, BF16),
            pltpu.VMEM((2, 2, 2, 2, part, quarter), BF16),
            pltpu.VMEM((2, 2, 2) + block, BF16),
            pltpu.VMEM((2,) + block, BF16),
            pltpu.VMEM((2,) + block, BF16),
            dma((10,)),
            dma((2, 2)), dma((2, 2)),
            dma((2,)), dma((2,)),
            dma((22,)), dma((22,)),
            dma((2, 2, 2, 2)), dma((2, 2, 2, 2)),
            dma((2, 2, 2, 2)), dma((2, 2, 2, 2)),
            dma((2, 2)), dma((2, 2)),
        ],
        compiler_params=pltpu.CompilerParams(
            collective_id=1, has_side_effects=True, vmem_limit_bytes=60 << 20
        ),
        name="attention_and_reductions",
    )(w_ref, nt_ref, nt_far_ref, q_ref, kv_ref, do_ref, lo_ref, proj_ref, q_mul_ref, k_mul_ref, x_mine_ref, inv_ref)


def gather_and_project(x_ref, wq_ref, wk_ref, wv_ref, gain_ref, q_mul_ref, k_mul_ref):
    tokens, width = x_ref.shape
    deep, q_cols = wq_ref.shape
    kv_cols = wk_ref.shape[1]
    head = q_mul_ref.shape[1]
    wing = q_cols // 2

    def kernel(x, wq, wk, wv, gain, q_mul, k_mul, w_all, nt, nt_far, proj, q16, kv, inv, x_mine, normed, one_of, xt,
               x_s, x_r, near_s, near_r, far_s, far_r, twin_s, twin_r, swap_s, swap_r, kv_s, kv_r):
        c, f = lax.axis_index("ctx"), lax.axis_index("fsdp")
        z, xl, core = c // 4, lax.rem(c // 2, 2), lax.rem(c, 2)
        twin = (z * 4 + xl * 2 + 1 - core, f)
        mate = (z * 4 + (1 - xl) * 2 + core, f)
        along = lambda k: (lax.rem(z + k, 4) * 4 + xl * 2 + core, f)
        later = [(lax.rem(c + k, 16), f) for k in (1, 2)]
        earlier = [(lax.rem(c + 16 - k, 16), f) for k in (1, 2)]

        barrier = pltpu.get_barrier_semaphore()
        for to in [twin, mate, along(1), along(3)] + later + earlier:
            pl.semaphore_signal(barrier, inc=1, device_id=to, device_id_type=MESH)
        pl.semaphore_wait(barrier, 8)

        def rows(k, xx, who=None):
            place = lax.rem(z + k, 4) * 4 + (1 - xl if xx else xl) * 2 + (core if who is None else who)
            return pl.ds(pl.multiple_of(place * deep, 16), deep)

        def copy(src, dst, ss, rs, to):
            return pltpu.make_async_remote_copy(
                src_ref=src, dst_ref=dst, send_sem=ss, recv_sem=rs, device_id=to, device_id_type=MESH
            )

        started = []

        def go(ref, ss, rs, to):
            cp = copy(ref, ref, ss, rs, to)
            cp.start()
            started.append(cp)

        def wait_for(ref, ss, rs):
            copy(ref, ref, ss, rs, twin).wait_recv()

        def to_twin(s, k, xx):
            go(w_all.at[s, rows(k, xx)], twin_s.at[s, xx, k], twin_r.at[s, xx, k], twin)

        def to_near(s, xx):
            for n, k in enumerate((1, 3)):
                go(w_all.at[s, rows(0, xx)], near_s.at[s, xx, n], near_r.at[s, xx, n], along(k))

        def near_and_forward(s, xx):
            for n, k in enumerate((3, 1)):
                wait_for(w_all.at[s, rows(k, xx)], near_s.at[s, xx, n], near_r.at[s, xx, n])
                go(w_all.at[s, rows(k, xx), pl.ds(n * wing, wing)], far_s.at[s, xx, n], far_r.at[s, xx, n],
                   along(1 if n == 0 else 3))
                to_twin(s, k, xx)

        def far(s, xx):
            for n in range(2):
                wait_for(w_all.at[s, rows(2, xx), pl.ds(n * wing, wing)], far_s.at[s, xx, n], far_r.at[s, xx, n])
            to_twin(s, 2, xx)

        def to_mate(s):
            go(w_all.at[s, rows(0, 0)], x_s.at[s], x_r.at[s], mate)

        def from_mate(s):
            wait_for(w_all.at[s, rows(0, 1)], x_s.at[s], x_r.at[s])

        def all_from_twin(s, ks):
            for xx in range(2):
                for k in ks:
                    wait_for(w_all.at[s, rows(k, xx, 1 - core)], twin_s.at[s, xx, k], twin_r.at[s, xx, k])

        w_all[1, rows(0, 0), :kv_cols] = wk[...]
        w_all[1, rows(0, 0), kv_cols:] = wv[...]
        to_mate(1)
        to_near(1, 0)
        w_all[0, rows(0, 0), :] = wq[...]
        to_twin(1, 0, 0)

        tile = 32

        def norm_tile(i, carry):
            at = pl.ds(pl.multiple_of(i * tile, tile), tile)
            wide = x[at, :].astype(F32)
            one = lax.rsqrt(jnp.sum(wide * wide, axis=1, keepdims=True) * (1.0 / width) + epsilon)
            one_of[at, :] = jnp.broadcast_to(one, (tile, 128))
            normed[at, :] = (wide * one * gain[...]).astype(BF16)
            return carry

        lax.fori_loop(0, tokens // tile, norm_tile, 0)
        from_mate(1)
        to_near(1, 1)
        to_mate(0)
        to_twin(1, 0, 1)

        strip = 256

        def turn(i, carry):
            at = pl.ds(pl.multiple_of(i * strip, strip), strip)
            nt[at, :] = normed[:, at].T
            xt[at, :] = x[:, at].T
            return carry

        near_and_forward(1, 0)
        to_near(0, 0)
        to_twin(0, 0, 0)
        lax.fori_loop(0, width // strip, turn, 0)
        inv[...] = one_of[...].T[:1]
        x_mine[...] = xt[pl.ds(pl.multiple_of(f * (2 * deep), 16), 2 * deep), :]
        near_and_forward(1, 1)
        from_mate(0)
        to_near(0, 1)
        to_twin(0, 0, 1)
        swaps = []
        for j in range(8):
            src = pl.ds(pl.multiple_of((j * 2 + 1 - core) * deep, 16), deep)
            cp = copy(nt.at[src], nt_far.at[j], swap_s.at[j], swap_r.at[j], twin)
            cp.start()
            swaps.append(cp)
        far(1, 0)
        far(1, 1)
        all_from_twin(1, range(4))
        proj[:, q_cols:] = jnp.dot(normed[...], w_all[1], preferred_element_type=F32)

        def head_norm(raw, mul):
            one = lax.rsqrt(jnp.mean(raw * raw, axis=1, keepdims=True) + epsilon)
            return (raw * one * mul).astype(BF16)

        last = pl.ds(2 * tokens, tokens)
        for g in range(kv_cols // head):
            at = slice(q_cols + g * head, q_cols + (g + 1) * head)
            kv[last, g * head : (g + 1) * head] = head_norm(proj[:, at], k_mul[...])
        kv[last, kv_cols:] = proj[:, q_cols + kv_cols :].astype(BF16)
        passed = []
        for n in range(2):
            cp = copy(kv.at[last], kv.at[pl.ds((1 - n) * tokens, tokens)], kv_s.at[n], kv_r.at[n], later[n])
            cp.start()
            passed.append(cp)
        near_and_forward(0, 0)
        near_and_forward(0, 1)
        all_from_twin(0, (0, 1, 3))
        span = width // 2
        pair = z // 2
        near_half = pl.ds(pl.multiple_of(pair * span, 128), span)
        proj[:, :q_cols] = jnp.dot(normed[:, near_half], w_all[0, near_half, :], preferred_element_type=F32)
        far(0, 0)
        far(0, 1)
        all_from_twin(0, (2,))
        far_half = pl.ds(pl.multiple_of((1 - pair) * span, 128), span)
        proj[:, :q_cols] += jnp.dot(normed[:, far_half], w_all[0, far_half, :], preferred_element_type=F32)
        for h in range(q_cols // head):
            at = slice(h * head, (h + 1) * head)
            q16[:, at] = head_norm(proj[:, at], q_mul[...])
        for cp in passed + swaps:
            cp.wait_recv()
        for cp in passed + swaps + started:
            cp.wait_send()

    vm = pl.BlockSpec(memory_space=pltpu.VMEM)
    dma = pltpu.SemaphoreType.DMA
    return pl.pallas_call(
        kernel,
        out_shape=(
            jax.ShapeDtypeStruct((2, width, q_cols), BF16),
            jax.ShapeDtypeStruct((width, tokens), BF16),
            jax.ShapeDtypeStruct((8, deep, tokens), BF16),
            jax.ShapeDtypeStruct((tokens, 2 * q_cols), F32),
            jax.ShapeDtypeStruct((tokens, q_cols), BF16),
            jax.ShapeDtypeStruct((3 * tokens, 2 * kv_cols), BF16),
            jax.ShapeDtypeStruct((1, tokens), F32),
            jax.ShapeDtypeStruct((2 * deep, tokens), BF16),
        ),
        in_specs=[vm] * 7,
        out_specs=(vm,) * 8,
        scratch_shapes=[
            pltpu.VMEM((tokens, width), BF16),
            pltpu.VMEM((tokens, 128), F32),
            pltpu.VMEM((width, tokens), BF16),
            dma((2,)), dma((2,)),
            dma((2, 2, 2)), dma((2, 2, 2)),
            dma((2, 2, 2)), dma((2, 2, 2)),
            dma((2, 2, 4)), dma((2, 2, 4)),
            dma((8,)), dma((8,)),
            dma((2,)), dma((2,)),
        ],
        compiler_params=pltpu.CompilerParams(
            collective_id=2, has_side_effects=True, vmem_limit_bytes=60 << 20
        ),
        name="gather_and_project",
    )(x_ref, wq_ref, wk_ref, wv_ref, gain_ref, q_mul_ref, k_mul_ref)


def on_device(
    inputs,
    output_cotangent,
    w_query,
    key_projection,
    value_projection,
    norm_gain,
    q_gain,
    key_norm_gain,
    half_lengths,
):
    tokens = inputs.shape[0]
    model_width = inputs.shape[1]
    head_dim = q_gain.shape[0]
    q_cols = w_query.shape[1]
    kv_cols = key_projection.shape[1]
    ctx_count = lax.axis_size("ctx")
    ctx_index = lax.axis_index("ctx")
    first_row = ctx_index * tokens
    grad_scale = float(tokens * ctx_count) ** (-0.5)
    query_multiplier = q_gain * query_scale
    gathered, normed_t, normed_far, projected, query_rows, kv_span, inv_row, inputs_mine = gather_and_project(
        inputs, w_query, key_projection, value_projection, norm_gain[None],
        (query_multiplier * LOG2E)[None], key_norm_gain[None],
    )
    fsdp_index = lax.axis_index("fsdp")
    fsdp_count = lax.axis_size("fsdp")
    features = model_width // fsdp_count
    hat_mine = inputs_mine.astype(jnp.float32) * inv_row
    gain_mine = lax.dynamic_slice_in_dim(norm_gain, fsdp_index * features, features, 0)
    halves = half_lengths.shape[0]
    upto = lax.iota(jnp.int32, halves)[None, :] <= lax.iota(jnp.int32, halves)[:, None]
    segment_ends = jnp.sum(jnp.where(upto, half_lengths[None, :], 0), axis=1)
    positions = first_row + lax.iota(jnp.int32, tokens)
    begun = jnp.max(jnp.where(segment_ends[None, :] <= positions[:, None], segment_ends[None, :], 0), axis=1)
    lowest = jnp.maximum(positions - (WIN - 1), begun) - (first_row - REACH * tokens)
    d_mine, weight_sum, sum_f, sum_c = attention_and_reductions(
        gathered, normed_t, normed_far, query_rows, kv_span, output_cotangent, lowest[:, None], projected,
        query_multiplier[None], key_norm_gain[None], inputs_mine, inv_row, grad_scale, query_scale,
    )
    d_mine = d_mine.reshape(features, tokens)
    row_dot = sum_f[0]
    upstream = d_mine * gain_mine[:, None]
    grad_inputs = (inv_row * (upstream - hat_mine * (row_dot[None, :] / model_width))).astype(jnp.bfloat16).T
    norm_row_dots = row_dot * float(model_width) ** (-0.5)
    own_features = model_width // (fsdp_count * ctx_count)
    gain_sum = lax.dynamic_slice_in_dim(
        sum_c[:6].reshape(6 * 128), ctx_index * own_features, own_features, 0
    )
    grad_q_gain, grad_k_gain = sum_c[6], sum_c[7]
    return (
        grad_inputs,
        weight_sum[:, :q_cols],
        weight_sum[:, q_cols : q_cols + kv_cols],
        weight_sum[:, q_cols + kv_cols :],
        gain_sum,
        grad_q_gain,
        grad_k_gain,
        norm_row_dots,
    )


def solution(mesh):
    placed = (
        P("ctx", None),
        P("ctx", "fsdp"),
        P("ctx", "fsdp"),
        P("ctx", "fsdp"),
        P("ctx", "fsdp"),
        P(),
        P(),
        P(),
        P(),
    )
    return jax.shard_map(
        on_device,
        mesh=mesh,
        in_specs=placed,
        out_specs=(
            P("ctx", "fsdp"),
            P("ctx", "fsdp"),
            P("ctx", "fsdp"),
            P("ctx", "fsdp"),
            P(("fsdp", "ctx")),
            P(),
            P(),
            P("ctx"),
        ),
        check_vma=False,
    )
```

```python
import jax
import jax.numpy as jnp
from jax import lax
from jax.experimental import pallas as pl
from jax.experimental.pallas import tpu as pltpu
from jax.sharding import PartitionSpec as P

WIN = 1024
REACH = 2


epsilon = 1e-06
query_scale = 168.0 ** (-0.5)


F32, BF16 = jnp.float32, jnp.bfloat16
NT = (((1,), (1,)), ((), ()))
TN = (((0,), (0,)), ((), ()))
MESH = pl.DeviceIdType.MESH
LOG2E = 1.4426950408889634


def attention_and_reductions(w_ref, nt_ref, nt_far_ref, q_ref, kv_ref, do_ref, lengths_ref, proj_ref, q_gain_ref, k_mul_ref,
                             x_mine_ref, inv_ref, scale, q_scale):
    tokens, q_cols = q_ref.shape
    cols = proj_ref.shape[1]
    part = w_ref.shape[1] // 16
    wing = cols // 2
    kvs = kv_ref.shape[1] // 2
    head = q_gain_ref.shape[1]
    kv_heads = kvs // head
    segs = lengths_ref.shape[0]
    group = q_cols // kvs
    half = tokens // 2
    span = 5 * half
    reach = kv_ref.shape[0]
    quarter = tokens // 2

    def kernel(w_hbm, nt_hbm, nt_far_hbm, q, kv, do, lengths, proj, q_gain, k_mul, x_mine, inv,
               dn_out, wg_out, sum_f, sum_c,
               w, nt, nt_far, v_one, e_all, mask, dkey, dval, kvg, kvg_in, own_kv, d, d_far, small,
               slots_f, slots_c, mine_c, far, near, far_in, near_in, cross, cross_in,
               fetch_sem, kvg_s, kvg_r, swap_s, swap_r, few_s, few_r, far_s, far_r, near_s, near_r, cross_s, cross_r):
        c, f = lax.axis_index("ctx"), lax.axis_index("fsdp")
        z, x, core = c // 4, lax.rem(c // 2, 2), lax.rem(c, 2)
        xh, y = f // 4, lax.rem(f, 4)
        ring = (
            lambda k: (c, xh * 4 + lax.rem(y + k, 4)),
            lambda k: (lax.rem(z + k, 4) * 4 + x * 2 + core, f),
        )
        across = ((c, (1 - xh) * 4 + y), (z * 4 + (1 - x) * 2 + core, f))
        twin = (z * 4 + x * 2 + 1 - core, f)
        peers_f = [(c, lax.rem(f + k, 8)) for k in range(1, 8)]
        peers_c = [(lax.rem(c + k, 16), f) for k in range(1, 16)]

        def rows_of(block):
            return pl.ds(pl.multiple_of(block * part, 16), part)

        barrier = pltpu.get_barrier_semaphore()
        partners = peers_f + peers_c
        for partner in partners:
            pl.semaphore_signal(barrier, inc=1, device_id=partner, device_id_type=MESH)
        fetches = [pltpu.make_async_copy(nt_hbm.at[rows_of(j * 2 + core)], nt.at[j], fetch_sem.at[j]) for j in range(8)]
        fetches.append(pltpu.make_async_copy(nt_far_hbm, nt_far, fetch_sem.at[8]))
        fetches.append(pltpu.make_async_copy(w_hbm, w, fetch_sem.at[9]))
        for cp in fetches:
            cp.start()

        def copy(src, dst, ss, rs, to):
            return pltpu.make_async_remote_copy(
                src_ref=src, dst_ref=dst, send_sem=ss, recv_sem=rs, device_id=to, device_id_type=MESH
            )

        sent = []

        def go(*what):
            cp = copy(*what)
            cp.start()
            sent.append(cp)
            return cp

        ones = jnp.ones((reach, head), BF16)
        for g in range(kv_heads):
            v_one[g, :, :head] = kv[:, kvs + g * head : kvs + (g + 1) * head]
            v_one[g, :, head:] = ones
        q_mul = q_gain[...] * q_scale
        first_row = c * tokens
        ends = [lengths[0]]
        for n in range(1, segs):
            ends.append(ends[-1] + lengths[n])
        for t in range(2):
            at = lax.broadcasted_iota(jnp.int32, (half, 1), 0) + (first_row + t * half)
            begun = jnp.zeros((half, 1), jnp.int32)
            for end in ends:
                begun = jnp.where(at >= end, end, begun)
            low = jnp.maximum(at - (WIN - 1), begun) - (first_row - REACH * tokens)
            col = lax.broadcasted_iota(jnp.int32, (half, span), 1) + t * half
            row = lax.broadcasted_iota(jnp.int32, (half, span), 0) + t * half
            seen = (col >= low) & (col <= row + 2 * tokens)
            mask[t] = jnp.where(seen, 1.0, 0.0).astype(BF16)
        lane = lax.broadcasted_iota(jnp.int32, (half, head), 1)

        def norm_back(grad, raw, mul):
            one = lax.rsqrt(jnp.mean(raw * raw, axis=1, keepdims=True) + epsilon)
            hat = raw * one
            up = grad * mul
            back = one * (up - hat * jnp.mean(up * hat, axis=1, keepdims=True))
            return back.astype(BF16), jnp.sum(grad * hat, axis=0, keepdims=True)

        q_term = jnp.zeros((1, head), F32)
        kv_copies = []
        for g in range(kv_heads):
            dkey[...] = jnp.zeros_like(dkey)
            dval[...] = jnp.zeros_like(dval)
            for r in range(group):
                h = g * group + r
                hc = slice(h * head, (h + 1) * head)
                for t in range(2):
                    qs = slice(t * half, (t + 1) * half)
                    ks = slice(t * half, t * half + span)
                    qt = q[qs, hc]
                    keys = kv[ks, g * head : (g + 1) * head]
                    s = lax.dot_general(qt, keys, NT, preferred_element_type=F32)
                    e_all[...] = jnp.exp2(s).astype(BF16) * mask[t]
                    out = jnp.dot(e_all[...], v_one[g, ks, :], preferred_element_type=F32)
                    inv_l = 1.0 / out[:, head:]
                    scaled = do[qs, hc].astype(F32) * inv_l
                    delta = jnp.sum(scaled * (out[:, :head] * inv_l), axis=1, keepdims=True)
                    d_hi = delta.astype(BF16).astype(F32)
                    tail = jnp.where(lane == 0, -d_hi, jnp.where(lane == 1, d_hi - delta, 0.0))
                    scaled16 = scaled.astype(BF16)
                    both = jnp.concatenate([scaled16, tail.astype(BF16)], axis=1)
                    dp = lax.dot_general(both, v_one[g, ks, :], NT, preferred_element_type=F32)
                    ds = dp.astype(BF16) * e_all[...]
                    dq = jnp.dot(ds, keys, preferred_element_type=F32)
                    dkey[ks, :] += lax.dot_general(ds, qt, TN, preferred_element_type=F32)
                    dval[ks, :] += lax.dot_general(e_all[...], scaled16, TN, preferred_element_type=F32)
                    d[qs, hc], term_q = norm_back(dq, proj[qs, hc], q_mul)
                    q_term += term_q
            if g == 0:
                pl.semaphore_wait(barrier, len(partners))
            for n in range(2):
                away = slice((1 - n) * tokens, (2 - n) * tokens)
                kvg[g, n, :, :head] = (dkey[away, :] * (1.0 / LOG2E)).astype(BF16)
                kvg[g, n, :, head:] = dval[away, :].astype(BF16)
                kv_copies.append(
                    go(kvg.at[g, n], kvg_in.at[g, n], kvg_s.at[g, n], kvg_r.at[g, n], (lax.rem(c + 15 - n, 16), f))
                )
            own_kv[:, g * head : (g + 1) * head] = dkey[2 * tokens :, :] * (1.0 / LOG2E)
            own_kv[:, kvs + g * head : kvs + (g + 1) * head] = dval[2 * tokens :, :]
        swap_q = go(d.at[:, pl.ds(0, wing)], d_far.at[:, pl.ds(0, wing)], swap_s.at[0], swap_r.at[0], twin)

        def term(m, s, k, h):
            if m == 0:
                block = (xh if s else 1 - xh) * 4 + lax.rem(y + k, 4)
                rows = rows_of(block * 2 + h)
                total = lax.dot_general(w[0, rows, :], d[:, :wing], NT, preferred_element_type=F32)
                total += lax.dot_general(w[1, rows, :], d[:, wing:], NT, preferred_element_type=F32)
                return total
            block = lax.rem(z + k, 4) * 2 + (x if s else 1 - x)
            hs = slice(h * wing, (h + 1) * wing)
            total = jnp.dot(nt[block], d[:, hs], preferred_element_type=F32)
            total += jnp.dot(nt_far[block], d_far[:, hs], preferred_element_type=F32)
            return total * scale

        fars, nears, crossed = {}, {}, {}

        def send_far(m, s, h):
            far[m, s, h] = term(m, s, 2, h).astype(BF16)
            for n, k in enumerate((1, 3)):
                fars[m, s, h, n] = go(
                    far.at[m, s, h, :, pl.ds(n * quarter, quarter)], far_in.at[m, s, h, n],
                    far_s.at[m, s, h, n], far_r.at[m, s, h, n], ring[m](k),
                )

        def make_near(m, s, h):
            for n, k in enumerate((1, 3)):
                near[m, s, n, h] = term(m, s, k, h).astype(BF16)

        def send_near(m, s, h):
            for n, k in enumerate((1, 3)):
                fars[m, s, h, n].wait_recv()
                at = slice(n * quarter, (n + 1) * quarter)
                near[m, s, n, h, :, at] = (
                    near[m, s, n, h, :, at].astype(F32) + far_in[m, s, h, n].astype(F32)
                ).astype(BF16)
                nears[m, s, n, h] = go(
                    near.at[m, s, n, h], near_in.at[m, s, n, h], near_s.at[m, s, n, h], near_r.at[m, s, n, h], ring[m](k)
                )

        def arrived(m, s, h):
            for n in range(2):
                nears[m, s, n, h].wait_recv()
            return near_in[m, s, 0, h].astype(F32) + near_in[m, s, 1, h].astype(F32)

        def send_cross(m, h):
            mine = term(m, 0, 0, h)
            cross[m, h] = (mine + arrived(m, 0, h)).astype(BF16)
            crossed[m, h] = go(cross.at[m, h], cross_in.at[m, h], cross_s.at[m, h], cross_r.at[m, h], across[m])

        for cp in fetches[:9]:
            cp.wait()
        swap_q.wait_recv()
        send_far(1, 0, 0)
        make_near(1, 0, 0)
        send_far(1, 1, 0)
        make_near(1, 1, 0)
        send_near(1, 0, 0)

        k_term = jnp.zeros((1, head), F32)
        for cp in kv_copies:
            cp.wait_recv()
        for g in range(kv_heads):
            at = slice(g * head, (g + 1) * head)
            there = slice(wing + g * head, wing + (g + 1) * head)
            grad = own_kv[:, at] + (kvg_in[g, 0, :, :head].astype(F32) + kvg_in[g, 1, :, :head].astype(F32))
            d[:, there], term_k = norm_back(grad, proj[:, there], k_mul[...])
            k_term += term_k
            at = slice(kvs + g * head, kvs + (g + 1) * head)
            grad = own_kv[:, at] + (kvg_in[g, 0, :, head:].astype(F32) + kvg_in[g, 1, :, head:].astype(F32))
            d[:, wing + kvs + g * head : wing + kvs + (g + 1) * head] = grad.astype(BF16)
        swap_kv = go(d.at[:, pl.ds(wing, wing)], d_far.at[:, pl.ds(wing, wing)], swap_s.at[1], swap_r.at[1], twin)
        fetches[9].wait()
        send_far(0, 0, 0)
        make_near(0, 0, 0)
        send_far(0, 0, 1)
        send_near(1, 1, 0)
        send_near(0, 0, 0)
        make_near(0, 0, 1)
        send_far(0, 1, 0)
        swap_kv.wait_recv()
        send_far(1, 0, 1)
        make_near(1, 0, 1)
        send_near(0, 0, 1)
        send_far(1, 1, 1)
        make_near(1, 1, 1)
        make_near(0, 1, 0)
        send_near(1, 0, 1)
        send_cross(1, 0)

        product = d[...].astype(F32) * proj[...]
        upper = product.astype(BF16)
        lower = (product - upper.astype(F32)).astype(BF16)
        ones_row = jnp.ones((8, cols), BF16)
        dots = lax.dot_general(ones_row, upper, NT, preferred_element_type=F32)
        dots += lax.dot_general(ones_row, lower, NT, preferred_element_type=F32)
        small[...] = dots
        small[1:2, :head] = q_term * (scale * q_scale)
        small[1:2, head : 2 * head] = k_term * scale
        slots_f[f] = small[...]
        few = [go(small, slots_f.at[f], few_s.at[k], few_r.at[k], to) for k, to in enumerate(peers_f)]

        send_far(0, 1, 1)
        make_near(0, 1, 1)
        send_near(0, 1, 0)
        send_cross(0, 0)
        send_near(1, 1, 1)
        send_cross(0, 1)
        send_cross(1, 1)
        send_near(0, 1, 1)
        for cp in few:
            cp.wait_recv()
        total_f = slots_f[0]
        for k in range(1, 8):
            total_f = total_f + slots_f[k]
        sum_f[...] = total_f
        for h in range(2):
            dn_out[h] = term(0, 1, 0, h)
        for h in range(2):
            own_kv[:part, :] = term(1, 1, 0, h)
            crossed[1, h].wait_recv()
            total = own_kv[:part, :] + cross_in[1, h].astype(F32) + arrived(1, 1, h)
            wg_out[:, h * wing : (h + 1) * wing] = total.astype(BF16)
        spread = jnp.zeros((128, 128), F32)
        for h in range(2):
            crossed[0, h].wait_recv()
            total = dn_out[h] + cross_in[0, h].astype(F32) + arrived(0, 1, h)
            dn_out[h] = total
            hat = x_mine[h * part : (h + 1) * part, :].astype(F32) * inv[...]
            sums = scale * jnp.sum(total * hat, axis=1, keepdims=True)
            at = lax.broadcasted_iota(jnp.int32, (part, 128), 0) + h * part
            lanes = lax.broadcasted_iota(jnp.int32, (part, 128), 1)
            to_row = jnp.where(at // 128 == lanes, sums, 0.0)
            to_lane = jnp.where(lax.rem(at, 128) == lanes, 1.0, 0.0)
            spread += lax.dot_general(to_row.astype(BF16), to_lane.astype(BF16), TN, preferred_element_type=F32)
        mine_c[...] = spread[:8]
        mine_c[6:7, :] = total_f[1:2, :head]
        mine_c[7:8, :] = total_f[1:2, head : 2 * head]
        slots_c[c] = mine_c[...]
        few_c = [go(mine_c, slots_c.at[c], few_s.at[7 + k], few_r.at[7 + k], to) for k, to in enumerate(peers_c)]
        for cp in few_c:
            cp.wait_recv()
        total_c = slots_c[0]
        for k in range(1, 16):
            total_c = total_c + slots_c[k]
        sum_c[...] = total_c
        for cp in sent:
            cp.wait_send()

    vm = pl.BlockSpec(memory_space=pltpu.VMEM)
    anywhere = pl.BlockSpec(memory_space=pl.ANY)
    dma = pltpu.SemaphoreType.DMA
    block = (2, part, tokens)
    return pl.pallas_call(
        kernel,
        out_shape=(
            jax.ShapeDtypeStruct(block, F32),
            jax.ShapeDtypeStruct((part, cols), BF16),
            jax.ShapeDtypeStruct((8, tokens), F32),
            jax.ShapeDtypeStruct((8, 128), F32),
        ),
        in_specs=[anywhere] * 3 + [vm] * 3 + [pl.BlockSpec(memory_space=pltpu.SMEM)] + [vm] * 5,
        out_specs=(vm,) * 4,
        scratch_shapes=[
            pltpu.VMEM(w_ref.shape, BF16),
            pltpu.VMEM((8, part, tokens), BF16),
            pltpu.VMEM((8, part, tokens), BF16),
            pltpu.VMEM((kv_heads, reach, 2 * head), BF16),
            pltpu.VMEM((half, span), BF16),
            pltpu.VMEM((2, half, span), BF16),
            pltpu.VMEM((reach, head), F32),
            pltpu.VMEM((reach, head), F32),
            pltpu.VMEM((2, 2, tokens, 2 * head), BF16),
            pltpu.VMEM((2, 2, tokens, 2 * head), BF16),
            pltpu.VMEM((tokens, 2 * kvs), F32),
            pltpu.VMEM((tokens, cols), BF16),
            pltpu.VMEM((tokens, cols), BF16),
            pltpu.VMEM((8, tokens), F32),
            pltpu.VMEM((8, 8, tokens), F32),
            pltpu.VMEM((16, 8, 128), F32),
            pltpu.VMEM((8, 128), F32),
            pltpu.VMEM((2, 2) + block, BF16),
            pltpu.VMEM((2, 2, 2) + block, BF16),
            pltpu.VMEM((2, 2, 2, 2, part, quarter), BF16),
            pltpu.VMEM((2, 2, 2) + block, BF16),
            pltpu.VMEM((2,) + block, BF16),
            pltpu.VMEM((2,) + block, BF16),
            dma((10,)),
            dma((2, 2)), dma((2, 2)),
            dma((2,)), dma((2,)),
            dma((22,)), dma((22,)),
            dma((2, 2, 2, 2)), dma((2, 2, 2, 2)),
            dma((2, 2, 2, 2)), dma((2, 2, 2, 2)),
            dma((2, 2)), dma((2, 2)),
        ],
        compiler_params=pltpu.CompilerParams(
            collective_id=1, has_side_effects=True, vmem_limit_bytes=60 << 20
        ),
        name="attention_and_reductions",
    )(w_ref, nt_ref, nt_far_ref, q_ref, kv_ref, do_ref, lengths_ref, proj_ref, q_gain_ref, k_mul_ref, x_mine_ref, inv_ref)


def gather_and_project(x_ref, wq_ref, wk_ref, wv_ref, gain_ref, q_gain_ref, k_mul_ref, q_scale):
    tokens, width = x_ref.shape
    deep, q_cols = wq_ref.shape
    kv_cols = wk_ref.shape[1]
    head = q_gain_ref.shape[1]
    wing = q_cols // 2

    def kernel(x_hbm, wq, wk, wv, gain, q_gain, k_mul, w_out, nt_out, nt_far, proj, q16, kv, inv, x_mine,
               x, w_all, nt, normed, one_of, xt, own_s,
               x_s, x_r, near_s, near_r, far_s, far_r, twin_s, twin_r, swap_s, swap_r, kv_s, kv_r):
        c, f = lax.axis_index("ctx"), lax.axis_index("fsdp")
        z, xl, core = c // 4, lax.rem(c // 2, 2), lax.rem(c, 2)
        twin = (z * 4 + xl * 2 + 1 - core, f)
        mate = (z * 4 + (1 - xl) * 2 + core, f)
        along = lambda k: (lax.rem(z + k, 4) * 4 + xl * 2 + core, f)
        later = [(lax.rem(c + k, 16), f) for k in (1, 2)]
        earlier = [(lax.rem(c + 16 - k, 16), f) for k in (1, 2)]

        x_copy = pltpu.make_async_copy(x_hbm, x, own_s.at[0])
        x_copy.start()
        barrier = pltpu.get_barrier_semaphore()
        for to in [twin, mate, along(1), along(3)] + later + earlier:
            pl.semaphore_signal(barrier, inc=1, device_id=to, device_id_type=MESH)
        pl.semaphore_wait(barrier, 8)

        def rows(k, xx, who=None):
            place = lax.rem(z + k, 4) * 4 + (1 - xl if xx else xl) * 2 + (core if who is None else who)
            return pl.ds(pl.multiple_of(place * deep, 16), deep)

        def copy(src, dst, ss, rs, to):
            return pltpu.make_async_remote_copy(
                src_ref=src, dst_ref=dst, send_sem=ss, recv_sem=rs, device_id=to, device_id_type=MESH
            )

        started = []

        def go(ref, ss, rs, to):
            cp = copy(ref, ref, ss, rs, to)
            cp.start()
            started.append(cp)

        def wait_for(ref, ss, rs):
            copy(ref, ref, ss, rs, twin).wait_recv()

        def to_twin(s, k, xx):
            go(w_all.at[s, rows(k, xx)], twin_s.at[s, xx, k], twin_r.at[s, xx, k], twin)

        def to_near(s, xx):
            for n, k in enumerate((1, 3)):
                go(w_all.at[s, rows(0, xx)], near_s.at[s, xx, n], near_r.at[s, xx, n], along(k))

        def near_and_forward(s, xx):
            for n, k in enumerate((3, 1)):
                wait_for(w_all.at[s, rows(k, xx)], near_s.at[s, xx, n], near_r.at[s, xx, n])
                go(w_all.at[s, rows(k, xx), pl.ds(n * wing, wing)], far_s.at[s, xx, n], far_r.at[s, xx, n],
                   along(1 if n == 0 else 3))
                to_twin(s, k, xx)

        def far(s, xx):
            for n in range(2):
                wait_for(w_all.at[s, rows(2, xx), pl.ds(n * wing, wing)], far_s.at[s, xx, n], far_r.at[s, xx, n])
            to_twin(s, 2, xx)

        def to_mate(s):
            go(w_all.at[s, rows(0, 0)], x_s.at[s], x_r.at[s], mate)

        def from_mate(s):
            wait_for(w_all.at[s, rows(0, 1)], x_s.at[s], x_r.at[s])

        def all_from_twin(s, ks):
            for xx in range(2):
                for k in ks:
                    wait_for(w_all.at[s, rows(k, xx, 1 - core)], twin_s.at[s, xx, k], twin_r.at[s, xx, k])

        w_all[1, rows(0, 0), :kv_cols] = wk[...]
        w_all[1, rows(0, 0), kv_cols:] = wv[...]
        to_mate(1)
        to_near(1, 0)
        w_all[0, rows(0, 0), :] = wq[...]
        to_twin(1, 0, 0)

        tile = 32

        def norm_tile(i, carry):
            at = pl.ds(pl.multiple_of(i * tile, tile), tile)
            wide = x[at, :].astype(F32)
            one = lax.rsqrt(jnp.sum(wide * wide, axis=1, keepdims=True) * (1.0 / width) + epsilon)
            one_of[at, :] = jnp.broadcast_to(one, (tile, 128))
            hat = wide * one
            for j in range(width // 128):
                strip_j = slice(j * 128, (j + 1) * 128)
                normed[at, strip_j] = (hat[:, strip_j] * gain[j : j + 1, :]).astype(BF16)
            return carry

        x_copy.wait()
        lax.fori_loop(0, tokens // tile, norm_tile, 0)
        from_mate(1)
        to_near(1, 1)
        to_mate(0)
        to_twin(1, 0, 1)

        strip = 256

        def turn(i, carry):
            at = pl.ds(pl.multiple_of(i * strip, strip), strip)
            nt[at, :] = normed[:, at].T
            xt[at, :] = x[:, at].T
            return carry

        near_and_forward(1, 0)
        to_near(0, 0)
        to_twin(0, 0, 0)
        lax.fori_loop(0, width // strip, turn, 0)
        outward = [pltpu.make_async_copy(nt, nt_out, own_s.at[1])]
        outward[0].start()
        inv[...] = one_of[...].T[:1]
        x_mine[...] = xt[pl.ds(pl.multiple_of(f * (2 * deep), 16), 2 * deep), :]
        near_and_forward(1, 1)
        from_mate(0)
        to_near(0, 1)
        to_twin(0, 0, 1)
        swaps = []
        for j in range(8):
            src = pl.ds(pl.multiple_of((j * 2 + 1 - core) * deep, 16), deep)
            cp = copy(nt.at[src], nt_far.at[j], swap_s.at[j], swap_r.at[j], twin)
            cp.start()
            swaps.append(cp)
        far(1, 0)
        far(1, 1)
        all_from_twin(1, range(4))
        def to_hbm(s, at, n):
            cp = pltpu.make_async_copy(w_all.at[s, at], w_out.at[s, at], own_s.at[n])
            cp.start()
            outward.append(cp)

        to_hbm(1, pl.ds(0, width), 2)
        proj[:, q_cols:] = jnp.dot(normed[...], w_all[1], preferred_element_type=F32)

        def head_norm(raw, mul):
            one = lax.rsqrt(jnp.mean(raw * raw, axis=1, keepdims=True) + epsilon)
            return (raw * one * mul).astype(BF16)

        last = pl.ds(2 * tokens, tokens)
        for g in range(kv_cols // head):
            at = slice(q_cols + g * head, q_cols + (g + 1) * head)
            kv[last, g * head : (g + 1) * head] = head_norm(proj[:, at], k_mul[...])
        kv[last, kv_cols:] = proj[:, q_cols + kv_cols :].astype(BF16)
        passed = []
        for n in range(2):
            cp = copy(kv.at[last], kv.at[pl.ds((1 - n) * tokens, tokens)], kv_s.at[n], kv_r.at[n], later[n])
            cp.start()
            passed.append(cp)
        near_and_forward(0, 0)
        near_and_forward(0, 1)
        all_from_twin(0, (0, 1, 3))
        span = width // 2
        pair = z // 2
        near_half = pl.ds(pl.multiple_of(pair * span, 128), span)
        to_hbm(0, near_half, 3)
        proj[:, :q_cols] = jnp.dot(normed[:, near_half], w_all[0, near_half, :], preferred_element_type=F32)
        far(0, 0)
        far(0, 1)
        all_from_twin(0, (2,))
        far_half = pl.ds(pl.multiple_of((1 - pair) * span, 128), span)
        to_hbm(0, far_half, 4)
        proj[:, :q_cols] += jnp.dot(normed[:, far_half], w_all[0, far_half, :], preferred_element_type=F32)
        for h in range(q_cols // head):
            at = slice(h * head, (h + 1) * head)
            q16[:, at] = head_norm(proj[:, at], q_gain[...] * (q_scale * LOG2E))
        for cp in passed + swaps:
            cp.wait_recv()
        for cp in passed + swaps + started:
            cp.wait_send()
        for cp in outward:
            cp.wait()

    vm = pl.BlockSpec(memory_space=pltpu.VMEM)
    anywhere = pl.BlockSpec(memory_space=pl.ANY)
    dma = pltpu.SemaphoreType.DMA
    return pl.pallas_call(
        kernel,
        out_shape=(
            jax.ShapeDtypeStruct((2, width, q_cols), BF16),
            jax.ShapeDtypeStruct((width, tokens), BF16),
            jax.ShapeDtypeStruct((8, deep, tokens), BF16),
            jax.ShapeDtypeStruct((tokens, 2 * q_cols), F32),
            jax.ShapeDtypeStruct((tokens, q_cols), BF16),
            jax.ShapeDtypeStruct((3 * tokens, 2 * kv_cols), BF16),
            jax.ShapeDtypeStruct((1, tokens), F32),
            jax.ShapeDtypeStruct((2 * deep, tokens), BF16),
        ),
        in_specs=[anywhere] + [vm] * 6,
        out_specs=(anywhere,) * 3 + (vm,) * 5,
        scratch_shapes=[
            pltpu.VMEM((tokens, width), BF16),
            pltpu.VMEM((2, width, q_cols), BF16),
            pltpu.VMEM((width, tokens), BF16),
            pltpu.VMEM((tokens, width), BF16),
            pltpu.VMEM((tokens, 128), F32),
            pltpu.VMEM((width, tokens), BF16),
            dma((5,)),
            dma((2,)), dma((2,)),
            dma((2, 2, 2)), dma((2, 2, 2)),
            dma((2, 2, 2)), dma((2, 2, 2)),
            dma((2, 2, 4)), dma((2, 2, 4)),
            dma((8,)), dma((8,)),
            dma((2,)), dma((2,)),
        ],
        compiler_params=pltpu.CompilerParams(
            collective_id=2, has_side_effects=True, vmem_limit_bytes=60 << 20
        ),
        name="gather_and_project",
    )(x_ref, wq_ref, wk_ref, wv_ref, gain_ref, q_gain_ref, k_mul_ref)


def on_device(
    inputs,
    output_cotangent,
    w_query,
    key_projection,
    value_projection,
    norm_gain,
    q_gain,
    key_norm_gain,
    half_lengths,
):
    tokens = inputs.shape[0]
    model_width = inputs.shape[1]
    head_dim = q_gain.shape[0]
    q_cols = w_query.shape[1]
    kv_cols = key_projection.shape[1]
    ctx_count = lax.axis_size("ctx")
    ctx_index = lax.axis_index("ctx")
    grad_scale = float(tokens * ctx_count) ** (-0.5)
    gathered, normed_t, normed_far, projected, query_rows, kv_span, inv_row, inputs_mine = gather_and_project(
        inputs, w_query, key_projection, value_projection, norm_gain.reshape(model_width // 128, 128),
        q_gain[None], key_norm_gain[None], query_scale,
    )
    fsdp_index = lax.axis_index("fsdp")
    fsdp_count = lax.axis_size("fsdp")
    features = model_width // fsdp_count
    hat_mine = inputs_mine.astype(jnp.float32) * inv_row
    gain_mine = lax.dynamic_slice_in_dim(norm_gain, fsdp_index * features, features, 0)
    d_mine, weight_sum, sum_f, sum_c = attention_and_reductions(
        gathered, normed_t, normed_far, query_rows, kv_span, output_cotangent, half_lengths, projected,
        q_gain[None], key_norm_gain[None], inputs_mine, inv_row, grad_scale, query_scale,
    )
    d_mine = d_mine.reshape(features, tokens)
    row_dot = sum_f[0]
    upstream = d_mine * gain_mine[:, None]
    grad_inputs = (inv_row * (upstream - hat_mine * (row_dot[None, :] / model_width))).astype(jnp.bfloat16).T
    norm_row_dots = row_dot * float(model_width) ** (-0.5)
    own_features = model_width // (fsdp_count * ctx_count)
    gain_sum = lax.dynamic_slice_in_dim(
        sum_c[:6].reshape(6 * 128), ctx_index * own_features, own_features, 0
    )
    grad_q_gain, grad_k_gain = sum_c[6], sum_c[7]
    return (
        grad_inputs,
        weight_sum[:, :q_cols],
        weight_sum[:, q_cols : q_cols + kv_cols],
        weight_sum[:, q_cols + kv_cols :],
        gain_sum,
        grad_q_gain,
        grad_k_gain,
        norm_row_dots,
    )


def solution(mesh):
    placed = (
        P("ctx", None),
        P("ctx", "fsdp"),
        P("ctx", "fsdp"),
        P("ctx", "fsdp"),
        P("ctx", "fsdp"),
        P(),
        P(),
        P(),
        P(),
    )
    return jax.shard_map(
        on_device,
        mesh=mesh,
        in_specs=placed,
        out_specs=(
            P("ctx", "fsdp"),
            P("ctx", "fsdp"),
            P("ctx", "fsdp"),
            P("ctx", "fsdp"),
            P(("fsdp", "ctx")),
            P(),
            P(),
            P("ctx"),
        ),
        check_vma=False,
    )
```

```python
import jax
import jax.numpy as jnp
from jax import lax
from jax.experimental import pallas as pl
from jax.experimental.pallas import tpu as pltpu
from jax.sharding import PartitionSpec as P

WIN = 1024
REACH = 2


epsilon = 1e-06
query_scale = 168.0 ** (-0.5)


F32, BF16 = jnp.float32, jnp.bfloat16
NT = (((1,), (1,)), ((), ()))
TN = (((0,), (0,)), ((), ()))
MESH = pl.DeviceIdType.MESH
LOG2E = 1.4426950408889634


def attention_and_reductions(w_ref, nt_ref, nt_far_ref, q_ref, kv_ref, do_ref, lengths_ref, proj_ref, q_gain_ref, k_mul_ref,
                             x_mine_ref, inv_ref, scale, q_scale):
    tokens, q_cols = q_ref.shape
    cols = proj_ref.shape[1]
    part = w_ref.shape[1] // 16
    wing = cols // 2
    kvs = kv_ref.shape[1] // 2
    head = q_gain_ref.shape[1]
    kv_heads = kvs // head
    segs = lengths_ref.shape[0]
    group = q_cols // kvs
    half = tokens // 2
    span = 5 * half
    reach = kv_ref.shape[0]
    quarter = tokens // 2

    def kernel(w_hbm, nt_hbm, nt_far_hbm, q, kv, do, lengths, proj, q_gain, k_mul, x_mine, inv,
               dn_out, wg_out, sum_f, sum_c,
               w, nt, nt_far, v_one, e_all, mask, dkey, dval, kvg, kvg_in, own_kv, d, d_far, small,
               slots_f, slots_c, mine_c, far, near, far_in, near_in, cross, cross_in,
               fetch_sem, kvg_s, kvg_r, swap_s, swap_r, few_s, few_r, far_s, far_r, near_s, near_r, cross_s, cross_r):
        c, f = lax.axis_index("ctx"), lax.axis_index("fsdp")
        z, x, core = c // 4, lax.rem(c // 2, 2), lax.rem(c, 2)
        xh, y = f // 4, lax.rem(f, 4)
        ring = (
            lambda k: (c, xh * 4 + lax.rem(y + k, 4)),
            lambda k: (lax.rem(z + k, 4) * 4 + x * 2 + core, f),
        )
        across = ((c, (1 - xh) * 4 + y), (z * 4 + (1 - x) * 2 + core, f))
        twin = (z * 4 + x * 2 + 1 - core, f)
        peers_f = [(c, lax.rem(f + k, 8)) for k in range(1, 8)]
        peers_c = [(lax.rem(c + k, 16), f) for k in range(1, 16)]

        def rows_of(block):
            return pl.ds(pl.multiple_of(block * part, 16), part)

        barrier = pltpu.get_barrier_semaphore()
        partners = peers_f + peers_c
        for partner in partners:
            pl.semaphore_signal(barrier, inc=1, device_id=partner, device_id_type=MESH)
        fetches = [pltpu.make_async_copy(nt_hbm.at[rows_of(j * 2 + core)], nt.at[j], fetch_sem.at[j]) for j in range(8)]
        fetches.append(pltpu.make_async_copy(nt_far_hbm, nt_far, fetch_sem.at[8]))
        fetches.append(pltpu.make_async_copy(w_hbm, w, fetch_sem.at[9]))
        for cp in fetches:
            cp.start()

        def copy(src, dst, ss, rs, to):
            return pltpu.make_async_remote_copy(
                src_ref=src, dst_ref=dst, send_sem=ss, recv_sem=rs, device_id=to, device_id_type=MESH
            )

        sent = []

        def go(*what):
            cp = copy(*what)
            cp.start()
            sent.append(cp)
            return cp

        ones = jnp.ones((reach, head), BF16)
        for g in range(kv_heads):
            v_one[g, :, :head] = kv[:, kvs + g * head : kvs + (g + 1) * head]
            v_one[g, :, head:] = ones
        q_mul = q_gain[...] * q_scale
        first_row = c * tokens
        ends = [lengths[0]]
        for n in range(1, segs):
            ends.append(ends[-1] + lengths[n])
        for t in range(2):
            at = lax.broadcasted_iota(jnp.int32, (half, 1), 0) + (first_row + t * half)
            begun = jnp.zeros((half, 1), jnp.int32)
            for end in ends:
                begun = jnp.where(at >= end, end, begun)
            low = jnp.maximum(at - (WIN - 1), begun) - (first_row - REACH * tokens)
            col = lax.broadcasted_iota(jnp.int32, (half, span), 1) + t * half
            row = lax.broadcasted_iota(jnp.int32, (half, span), 0) + t * half
            seen = (col >= low) & (col <= row + 2 * tokens)
            mask[t] = jnp.where(seen, 1.0, 0.0).astype(BF16)
        lane = lax.broadcasted_iota(jnp.int32, (half, head), 1)

        def norm_back(grad, raw, mul):
            one = lax.rsqrt(jnp.mean(raw * raw, axis=1, keepdims=True) + epsilon)
            hat = raw * one
            up = grad * mul
            back = one * (up - hat * jnp.mean(up * hat, axis=1, keepdims=True))
            return back.astype(BF16), jnp.sum(grad * hat, axis=0, keepdims=True)

        q_term = jnp.zeros((1, head), F32)
        kv_copies = []
        for g in range(kv_heads):
            dkey[...] = jnp.zeros_like(dkey)
            dval[...] = jnp.zeros_like(dval)
            for r in range(group):
                h = g * group + r
                hc = slice(h * head, (h + 1) * head)
                for t in range(2):
                    qs = slice(t * half, (t + 1) * half)
                    ks = slice(t * half, t * half + span)
                    qt = q[qs, hc]
                    keys = kv[ks, g * head : (g + 1) * head]
                    s = lax.dot_general(qt, keys, NT, preferred_element_type=F32)
                    e_all[...] = jnp.exp2(s).astype(BF16) * mask[t]
                    out = jnp.dot(e_all[...], v_one[g, ks, :], preferred_element_type=F32)
                    inv_l = 1.0 / out[:, head:]
                    scaled = do[qs, hc].astype(F32) * inv_l
                    delta = jnp.sum(scaled * (out[:, :head] * inv_l), axis=1, keepdims=True)
                    d_hi = delta.astype(BF16).astype(F32)
                    tail = jnp.where(lane == 0, -d_hi, jnp.where(lane == 1, d_hi - delta, 0.0))
                    scaled16 = scaled.astype(BF16)
                    both = jnp.concatenate([scaled16, tail.astype(BF16)], axis=1)
                    dp = lax.dot_general(both, v_one[g, ks, :], NT, preferred_element_type=F32)
                    ds = dp.astype(BF16) * e_all[...]
                    dq = jnp.dot(ds, keys, preferred_element_type=F32)
                    dkey[ks, :] += lax.dot_general(ds, qt, TN, preferred_element_type=F32)
                    dval[ks, :] += lax.dot_general(e_all[...], scaled16, TN, preferred_element_type=F32)
                    d[qs, hc], term_q = norm_back(dq, proj[qs, hc], q_mul)
                    q_term += term_q
            if g == 0:
                pl.semaphore_wait(barrier, len(partners))
            for n in range(2):
                away = slice((1 - n) * tokens, (2 - n) * tokens)
                kvg[g, n, :, :head] = (dkey[away, :] * (1.0 / LOG2E)).astype(BF16)
                kvg[g, n, :, head:] = dval[away, :].astype(BF16)
                kv_copies.append(
                    go(kvg.at[g, n], kvg_in.at[g, n], kvg_s.at[g, n], kvg_r.at[g, n], (lax.rem(c + 15 - n, 16), f))
                )
            own_kv[:, g * head : (g + 1) * head] = dkey[2 * tokens :, :] * (1.0 / LOG2E)
            own_kv[:, kvs + g * head : kvs + (g + 1) * head] = dval[2 * tokens :, :]
        swap_q = go(d.at[:, pl.ds(0, wing)], d_far.at[:, pl.ds(0, wing)], swap_s.at[0], swap_r.at[0], twin)

        def term(m, s, k, h):
            if m == 0:
                block = (xh if s else 1 - xh) * 4 + lax.rem(y + k, 4)
                rows = rows_of(block * 2 + h)
                total = lax.dot_general(w[0, rows, :], d[:, :wing], NT, preferred_element_type=F32)
                total += lax.dot_general(w[1, rows, :], d[:, wing:], NT, preferred_element_type=F32)
                return total
            block = lax.rem(z + k, 4) * 2 + (x if s else 1 - x)
            hs = slice(h * wing, (h + 1) * wing)
            total = jnp.dot(nt[block], d[:, hs], preferred_element_type=F32)
            total += jnp.dot(nt_far[block], d_far[:, hs], preferred_element_type=F32)
            return total * scale

        fars, nears, crossed = {}, {}, {}

        def send_far(m, s, h):
            far[m, s, h] = term(m, s, 2, h).astype(BF16)
            for n, k in enumerate((1, 3)):
                fars[m, s, h, n] = go(
                    far.at[m, s, h, :, pl.ds(n * quarter, quarter)], far_in.at[m, s, h, n],
                    far_s.at[m, s, h, n], far_r.at[m, s, h, n], ring[m](k),
                )

        def make_near(m, s, h):
            for n, k in enumerate((1, 3)):
                near[m, s, n, h] = term(m, s, k, h).astype(BF16)

        def send_near(m, s, h):
            for n, k in enumerate((1, 3)):
                fars[m, s, h, n].wait_recv()
                at = slice(n * quarter, (n + 1) * quarter)
                near[m, s, n, h, :, at] = (
                    near[m, s, n, h, :, at].astype(F32) + far_in[m, s, h, n].astype(F32)
                ).astype(BF16)
                nears[m, s, n, h] = go(
                    near.at[m, s, n, h], near_in.at[m, s, n, h], near_s.at[m, s, n, h], near_r.at[m, s, n, h], ring[m](k)
                )

        def arrived(m, s, h):
            for n in range(2):
                nears[m, s, n, h].wait_recv()
            return near_in[m, s, 0, h].astype(F32) + near_in[m, s, 1, h].astype(F32)

        def send_cross(m, h):
            mine = term(m, 0, 0, h)
            cross[m, h] = (mine + arrived(m, 0, h)).astype(BF16)
            crossed[m, h] = go(cross.at[m, h], cross_in.at[m, h], cross_s.at[m, h], cross_r.at[m, h], across[m])

        for cp in fetches[:9]:
            cp.wait()
        swap_q.wait_recv()
        send_far(1, 0, 0)
        make_near(1, 0, 0)
        send_far(1, 1, 0)
        send_near(1, 0, 0)
        make_near(1, 1, 0)

        k_term = jnp.zeros((1, head), F32)
        for cp in kv_copies:
            cp.wait_recv()
        for g in range(kv_heads):
            at = slice(g * head, (g + 1) * head)
            there = slice(wing + g * head, wing + (g + 1) * head)
            grad = own_kv[:, at] + (kvg_in[g, 0, :, :head].astype(F32) + kvg_in[g, 1, :, :head].astype(F32))
            d[:, there], term_k = norm_back(grad, proj[:, there], k_mul[...])
            k_term += term_k
            at = slice(kvs + g * head, kvs + (g + 1) * head)
            grad = own_kv[:, at] + (kvg_in[g, 0, :, head:].astype(F32) + kvg_in[g, 1, :, head:].astype(F32))
            d[:, wing + kvs + g * head : wing + kvs + (g + 1) * head] = grad.astype(BF16)
        swap_kv = go(d.at[:, pl.ds(wing, wing)], d_far.at[:, pl.ds(wing, wing)], swap_s.at[1], swap_r.at[1], twin)
        fetches[9].wait()
        send_far(0, 0, 0)
        make_near(0, 0, 0)
        send_far(0, 0, 1)
        swap_kv.wait_recv()
        send_far(1, 0, 1)
        send_near(0, 0, 0)
        make_near(1, 0, 1)
        make_near(0, 0, 1)
        send_cross(1, 0)
        send_far(0, 1, 0)
        send_near(0, 0, 1)
        send_near(1, 0, 1)
        send_near(1, 1, 0)
        send_far(1, 1, 1)
        make_near(0, 1, 0)

        product = d[...].astype(F32) * proj[...]
        upper = product.astype(BF16)
        lower = (product - upper.astype(F32)).astype(BF16)
        ones_row = jnp.ones((8, cols), BF16)
        dots = lax.dot_general(ones_row, upper, NT, preferred_element_type=F32)
        dots += lax.dot_general(ones_row, lower, NT, preferred_element_type=F32)
        small[...] = dots
        small[1:2, :head] = q_term * (scale * q_scale)
        small[1:2, head : 2 * head] = k_term * scale
        slots_f[f] = small[...]
        few = [go(small, slots_f.at[f], few_s.at[k], few_r.at[k], to) for k, to in enumerate(peers_f)]

        send_cross(0, 0)
        send_far(0, 1, 1)
        send_near(0, 1, 0)
        make_near(1, 1, 1)
        send_cross(1, 1)
        make_near(0, 1, 1)
        send_near(1, 1, 1)
        send_cross(0, 1)
        send_near(0, 1, 1)
        for cp in few:
            cp.wait_recv()
        total_f = slots_f[0]
        for k in range(1, 8):
            total_f = total_f + slots_f[k]
        sum_f[...] = total_f
        for h in range(2):
            dn_out[h] = term(0, 1, 0, h)
        spread = jnp.zeros((128, 128), F32)

        def finish_weights(h):
            own_kv[:part, :] = term(1, 1, 0, h)
            crossed[1, h].wait_recv()
            total = own_kv[:part, :] + cross_in[1, h].astype(F32) + arrived(1, 1, h)
            wg_out[:, h * wing : (h + 1) * wing] = total.astype(BF16)

        finish_weights(0)
        for h in range(2):
            crossed[0, h].wait_recv()
            total = dn_out[h] + cross_in[0, h].astype(F32) + arrived(0, 1, h)
            dn_out[h] = total
            hat = x_mine[h * part : (h + 1) * part, :].astype(F32) * inv[...]
            sums = scale * jnp.sum(total * hat, axis=1, keepdims=True)
            at = lax.broadcasted_iota(jnp.int32, (part, 128), 0) + h * part
            lanes = lax.broadcasted_iota(jnp.int32, (part, 128), 1)
            to_row = jnp.where(at // 128 == lanes, sums, 0.0)
            to_lane = jnp.where(lax.rem(at, 128) == lanes, 1.0, 0.0)
            spread += lax.dot_general(to_row.astype(BF16), to_lane.astype(BF16), TN, preferred_element_type=F32)
        mine_c[...] = spread[:8]
        mine_c[6:7, :] = total_f[1:2, :head]
        mine_c[7:8, :] = total_f[1:2, head : 2 * head]
        slots_c[c] = mine_c[...]
        few_c = [go(mine_c, slots_c.at[c], few_s.at[7 + k], few_r.at[7 + k], to) for k, to in enumerate(peers_c)]
        finish_weights(1)
        for cp in few_c:
            cp.wait_recv()
        total_c = slots_c[0]
        for k in range(1, 16):
            total_c = total_c + slots_c[k]
        sum_c[...] = total_c
        for cp in sent:
            cp.wait_send()

    vm = pl.BlockSpec(memory_space=pltpu.VMEM)
    anywhere = pl.BlockSpec(memory_space=pl.ANY)
    dma = pltpu.SemaphoreType.DMA
    block = (2, part, tokens)
    return pl.pallas_call(
        kernel,
        out_shape=(
            jax.ShapeDtypeStruct(block, F32),
            jax.ShapeDtypeStruct((part, cols), BF16),
            jax.ShapeDtypeStruct((8, tokens), F32),
            jax.ShapeDtypeStruct((8, 128), F32),
        ),
        in_specs=[anywhere] * 3 + [vm] * 3 + [pl.BlockSpec(memory_space=pltpu.SMEM)] + [vm] * 5,
        out_specs=(vm,) * 4,
        scratch_shapes=[
            pltpu.VMEM(w_ref.shape, BF16),
            pltpu.VMEM((8, part, tokens), BF16),
            pltpu.VMEM((8, part, tokens), BF16),
            pltpu.VMEM((kv_heads, reach, 2 * head), BF16),
            pltpu.VMEM((half, span), BF16),
            pltpu.VMEM((2, half, span), BF16),
            pltpu.VMEM((reach, head), F32),
            pltpu.VMEM((reach, head), F32),
            pltpu.VMEM((2, 2, tokens, 2 * head), BF16),
            pltpu.VMEM((2, 2, tokens, 2 * head), BF16),
            pltpu.VMEM((tokens, 2 * kvs), F32),
            pltpu.VMEM((tokens, cols), BF16),
            pltpu.VMEM((tokens, cols), BF16),
            pltpu.VMEM((8, tokens), F32),
            pltpu.VMEM((8, 8, tokens), F32),
            pltpu.VMEM((16, 8, 128), F32),
            pltpu.VMEM((8, 128), F32),
            pltpu.VMEM((2, 2) + block, BF16),
            pltpu.VMEM((2, 2, 2) + block, BF16),
            pltpu.VMEM((2, 2, 2, 2, part, quarter), BF16),
            pltpu.VMEM((2, 2, 2) + block, BF16),
            pltpu.VMEM((2,) + block, BF16),
            pltpu.VMEM((2,) + block, BF16),
            dma((10,)),
            dma((2, 2)), dma((2, 2)),
            dma((2,)), dma((2,)),
            dma((22,)), dma((22,)),
            dma((2, 2, 2, 2)), dma((2, 2, 2, 2)),
            dma((2, 2, 2, 2)), dma((2, 2, 2, 2)),
            dma((2, 2)), dma((2, 2)),
        ],
        compiler_params=pltpu.CompilerParams(
            collective_id=1, has_side_effects=True, vmem_limit_bytes=60 << 20
        ),
        name="attention_and_reductions",
    )(w_ref, nt_ref, nt_far_ref, q_ref, kv_ref, do_ref, lengths_ref, proj_ref, q_gain_ref, k_mul_ref, x_mine_ref, inv_ref)


def gather_and_project(x_ref, wq_ref, wk_ref, wv_ref, gain_ref, q_gain_ref, k_mul_ref, q_scale):
    tokens, width = x_ref.shape
    deep, q_cols = wq_ref.shape
    kv_cols = wk_ref.shape[1]
    head = q_gain_ref.shape[1]
    wing = q_cols // 2

    def kernel(x_hbm, wq, wk, wv, gain, q_gain, k_mul, w_out, nt_out, nt_far, proj, q16, kv, inv, x_mine,
               x, w_all, nt, normed, one_of, xt, own_s,
               x_s, x_r, near_s, near_r, far_s, far_r, twin_s, twin_r, swap_s, swap_r, kv_s, kv_r):
        c, f = lax.axis_index("ctx"), lax.axis_index("fsdp")
        z, xl, core = c // 4, lax.rem(c // 2, 2), lax.rem(c, 2)
        twin = (z * 4 + xl * 2 + 1 - core, f)
        mate = (z * 4 + (1 - xl) * 2 + core, f)
        along = lambda k: (lax.rem(z + k, 4) * 4 + xl * 2 + core, f)
        later = [(lax.rem(c + k, 16), f) for k in (1, 2)]
        earlier = [(lax.rem(c + 16 - k, 16), f) for k in (1, 2)]

        x_copy = pltpu.make_async_copy(x_hbm, x, own_s.at[0])
        x_copy.start()
        barrier = pltpu.get_barrier_semaphore()
        for to in [twin, mate, along(1), along(3)] + later + earlier:
            pl.semaphore_signal(barrier, inc=1, device_id=to, device_id_type=MESH)
        pl.semaphore_wait(barrier, 8)

        def rows(k, xx, who=None):
            place = lax.rem(z + k, 4) * 4 + (1 - xl if xx else xl) * 2 + (core if who is None else who)
            return pl.ds(pl.multiple_of(place * deep, 16), deep)

        def copy(src, dst, ss, rs, to):
            return pltpu.make_async_remote_copy(
                src_ref=src, dst_ref=dst, send_sem=ss, recv_sem=rs, device_id=to, device_id_type=MESH
            )

        started = []

        def go(ref, ss, rs, to):
            cp = copy(ref, ref, ss, rs, to)
            cp.start()
            started.append(cp)

        def wait_for(ref, ss, rs):
            copy(ref, ref, ss, rs, twin).wait_recv()

        def to_twin(s, k, xx):
            go(w_all.at[s, rows(k, xx)], twin_s.at[s, xx, k], twin_r.at[s, xx, k], twin)

        def to_near(s, xx):
            for n, k in enumerate((1, 3)):
                go(w_all.at[s, rows(0, xx)], near_s.at[s, xx, n], near_r.at[s, xx, n], along(k))

        def near_and_forward(s, xx):
            for n, k in enumerate((3, 1)):
                wait_for(w_all.at[s, rows(k, xx)], near_s.at[s, xx, n], near_r.at[s, xx, n])
                go(w_all.at[s, rows(k, xx), pl.ds(n * wing, wing)], far_s.at[s, xx, n], far_r.at[s, xx, n],
                   along(1 if n == 0 else 3))
                to_twin(s, k, xx)

        def far(s, xx):
            for n in range(2):
                wait_for(w_all.at[s, rows(2, xx), pl.ds(n * wing, wing)], far_s.at[s, xx, n], far_r.at[s, xx, n])
            to_twin(s, 2, xx)

        def to_mate(s):
            go(w_all.at[s, rows(0, 0)], x_s.at[s], x_r.at[s], mate)

        def from_mate(s):
            wait_for(w_all.at[s, rows(0, 1)], x_s.at[s], x_r.at[s])

        def all_from_twin(s, ks):
            for xx in range(2):
                for k in ks:
                    wait_for(w_all.at[s, rows(k, xx, 1 - core)], twin_s.at[s, xx, k], twin_r.at[s, xx, k])

        w_all[1, rows(0, 0), :kv_cols] = wk[...]
        w_all[1, rows(0, 0), kv_cols:] = wv[...]
        to_mate(1)
        to_near(1, 0)
        w_all[0, rows(0, 0), :] = wq[...]
        to_twin(1, 0, 0)

        tile = 32

        def norm_tile(i, carry):
            at = pl.ds(pl.multiple_of(i * tile, tile), tile)
            wide = x[at, :].astype(F32)
            one = lax.rsqrt(jnp.sum(wide * wide, axis=1, keepdims=True) * (1.0 / width) + epsilon)
            one_of[at, :] = jnp.broadcast_to(one, (tile, 128))
            hat = wide * one
            for j in range(width // 128):
                strip_j = slice(j * 128, (j + 1) * 128)
                normed[at, strip_j] = (hat[:, strip_j] * gain[j : j + 1, :]).astype(BF16)
            return carry

        x_copy.wait()
        lax.fori_loop(0, tokens // tile, norm_tile, 0)
        from_mate(1)
        to_near(1, 1)
        to_mate(0)
        to_twin(1, 0, 1)

        strip = 256

        def turn(i, carry):
            at = pl.ds(pl.multiple_of(i * strip, strip), strip)
            nt[at, :] = normed[:, at].T
            xt[at, :] = x[:, at].T
            return carry

        near_and_forward(1, 0)
        to_near(0, 0)
        to_twin(0, 0, 0)
        lax.fori_loop(0, width // strip, turn, 0)
        outward = [pltpu.make_async_copy(nt, nt_out, own_s.at[1])]
        outward[0].start()
        inv[...] = one_of[...].T[:1]
        x_mine[...] = xt[pl.ds(pl.multiple_of(f * (2 * deep), 16), 2 * deep), :]
        near_and_forward(1, 1)
        from_mate(0)
        to_near(0, 1)
        to_twin(0, 0, 1)
        swaps = []
        for j in range(8):
            src = pl.ds(pl.multiple_of((j * 2 + 1 - core) * deep, 16), deep)
            cp = copy(nt.at[src], nt_far.at[j], swap_s.at[j], swap_r.at[j], twin)
            cp.start()
            swaps.append(cp)
        far(1, 0)
        far(1, 1)
        all_from_twin(1, range(4))
        def to_hbm(s, at, n):
            cp = pltpu.make_async_copy(w_all.at[s, at], w_out.at[s, at], own_s.at[n])
            cp.start()
            outward.append(cp)

        to_hbm(1, pl.ds(0, width), 2)
        proj[:, q_cols:] = jnp.dot(normed[...], w_all[1], preferred_element_type=F32)

        def head_norm(raw, mul):
            one = lax.rsqrt(jnp.mean(raw * raw, axis=1, keepdims=True) + epsilon)
            return (raw * one * mul).astype(BF16)

        last = pl.ds(2 * tokens, tokens)
        for g in range(kv_cols // head):
            at = slice(q_cols + g * head, q_cols + (g + 1) * head)
            kv[last, g * head : (g + 1) * head] = head_norm(proj[:, at], k_mul[...])
        kv[last, kv_cols:] = proj[:, q_cols + kv_cols :].astype(BF16)
        passed = []
        for n in range(2):
            cp = copy(kv.at[last], kv.at[pl.ds((1 - n) * tokens, tokens)], kv_s.at[n], kv_r.at[n], later[n])
            cp.start()
            passed.append(cp)
        near_and_forward(0, 0)
        near_and_forward(0, 1)
        all_from_twin(0, (0, 1, 3))
        span = width // 2
        pair = z // 2
        near_half = pl.ds(pl.multiple_of(pair * span, 128), span)
        to_hbm(0, near_half, 3)
        proj[:, :q_cols] = jnp.dot(normed[:, near_half], w_all[0, near_half, :], preferred_element_type=F32)
        far(0, 0)
        far(0, 1)
        all_from_twin(0, (2,))
        far_half = pl.ds(pl.multiple_of((1 - pair) * span, 128), span)
        to_hbm(0, far_half, 4)
        proj[:, :q_cols] += jnp.dot(normed[:, far_half], w_all[0, far_half, :], preferred_element_type=F32)
        for h in range(q_cols // head):
            at = slice(h * head, (h + 1) * head)
            q16[:, at] = head_norm(proj[:, at], q_gain[...] * (q_scale * LOG2E))
        for cp in passed + swaps:
            cp.wait_recv()
        for cp in passed + swaps + started:
            cp.wait_send()
        for cp in outward:
            cp.wait()

    vm = pl.BlockSpec(memory_space=pltpu.VMEM)
    anywhere = pl.BlockSpec(memory_space=pl.ANY)
    dma = pltpu.SemaphoreType.DMA
    return pl.pallas_call(
        kernel,
        out_shape=(
            jax.ShapeDtypeStruct((2, width, q_cols), BF16),
            jax.ShapeDtypeStruct((width, tokens), BF16),
            jax.ShapeDtypeStruct((8, deep, tokens), BF16),
            jax.ShapeDtypeStruct((tokens, 2 * q_cols), F32),
            jax.ShapeDtypeStruct((tokens, q_cols), BF16),
            jax.ShapeDtypeStruct((3 * tokens, 2 * kv_cols), BF16),
            jax.ShapeDtypeStruct((1, tokens), F32),
            jax.ShapeDtypeStruct((2 * deep, tokens), BF16),
        ),
        in_specs=[anywhere] + [vm] * 6,
        out_specs=(anywhere,) * 3 + (vm,) * 5,
        scratch_shapes=[
            pltpu.VMEM((tokens, width), BF16),
            pltpu.VMEM((2, width, q_cols), BF16),
            pltpu.VMEM((width, tokens), BF16),
            pltpu.VMEM((tokens, width), BF16),
            pltpu.VMEM((tokens, 128), F32),
            pltpu.VMEM((width, tokens), BF16),
            dma((5,)),
            dma((2,)), dma((2,)),
            dma((2, 2, 2)), dma((2, 2, 2)),
            dma((2, 2, 2)), dma((2, 2, 2)),
            dma((2, 2, 4)), dma((2, 2, 4)),
            dma((8,)), dma((8,)),
            dma((2,)), dma((2,)),
        ],
        compiler_params=pltpu.CompilerParams(
            collective_id=2, has_side_effects=True, vmem_limit_bytes=60 << 20
        ),
        name="gather_and_project",
    )(x_ref, wq_ref, wk_ref, wv_ref, gain_ref, q_gain_ref, k_mul_ref)


def on_device(
    inputs,
    output_cotangent,
    w_query,
    key_projection,
    value_projection,
    norm_gain,
    q_gain,
    key_norm_gain,
    half_lengths,
):
    tokens = inputs.shape[0]
    model_width = inputs.shape[1]
    head_dim = q_gain.shape[0]
    q_cols = w_query.shape[1]
    kv_cols = key_projection.shape[1]
    ctx_count = lax.axis_size("ctx")
    ctx_index = lax.axis_index("ctx")
    grad_scale = float(tokens * ctx_count) ** (-0.5)
    gathered, normed_t, normed_far, projected, query_rows, kv_span, inv_row, inputs_mine = gather_and_project(
        inputs, w_query, key_projection, value_projection, norm_gain.reshape(model_width // 128, 128),
        q_gain[None], key_norm_gain[None], query_scale,
    )
    fsdp_index = lax.axis_index("fsdp")
    fsdp_count = lax.axis_size("fsdp")
    features = model_width // fsdp_count
    hat_mine = inputs_mine.astype(jnp.float32) * inv_row
    gain_mine = lax.dynamic_slice_in_dim(norm_gain, fsdp_index * features, features, 0)
    d_mine, weight_sum, sum_f, sum_c = attention_and_reductions(
        gathered, normed_t, normed_far, query_rows, kv_span, output_cotangent, half_lengths, projected,
        q_gain[None], key_norm_gain[None], inputs_mine, inv_row, grad_scale, query_scale,
    )
    d_mine = d_mine.reshape(features, tokens)
    row_dot = sum_f[0]
    upstream = d_mine * gain_mine[:, None]
    grad_inputs = (inv_row * (upstream - hat_mine * (row_dot[None, :] / model_width))).astype(jnp.bfloat16).T
    norm_row_dots = row_dot * float(model_width) ** (-0.5)
    own_features = model_width // (fsdp_count * ctx_count)
    gain_sum = lax.dynamic_slice_in_dim(
        sum_c[:6].reshape(6 * 128), ctx_index * own_features, own_features, 0
    )
    grad_q_gain, grad_k_gain = sum_c[6], sum_c[7]
    return (
        grad_inputs,
        weight_sum[:, :q_cols],
        weight_sum[:, q_cols : q_cols + kv_cols],
        weight_sum[:, q_cols + kv_cols :],
        gain_sum,
        grad_q_gain,
        grad_k_gain,
        norm_row_dots,
    )


def solution(mesh):
    placed = (
        P("ctx", None),
        P("ctx", "fsdp"),
        P("ctx", "fsdp"),
        P("ctx", "fsdp"),
        P("ctx", "fsdp"),
        P(),
        P(),
        P(),
        P(),
    )
    return jax.shard_map(
        on_device,
        mesh=mesh,
        in_specs=placed,
        out_specs=(
            P("ctx", "fsdp"),
            P("ctx", "fsdp"),
            P("ctx", "fsdp"),
            P("ctx", "fsdp"),
            P(("fsdp", "ctx")),
            P(),
            P(),
            P("ctx"),
        ),
        check_vma=False,
    )
```

```python
import jax
import jax.numpy as jnp
from jax import lax
from jax.experimental import pallas as pl
from jax.experimental.pallas import tpu as pltpu
from jax.sharding import PartitionSpec as P

WIN = 1024
REACH = 2


epsilon = 1e-06
query_scale = 168.0 ** (-0.5)


F32, BF16 = jnp.float32, jnp.bfloat16
NT = (((1,), (1,)), ((), ()))
TN = (((0,), (0,)), ((), ()))
MESH = pl.DeviceIdType.MESH
LOG2E = 1.4426950408889634


def attention_and_reductions(w_ref, nt_ref, nt_far_ref, q_ref, kv_ref, do_ref, lengths_ref, proj_ref, q_gain_ref, k_mul_ref,
                             x_mine_ref, inv_ref, scale, q_scale):
    tokens, q_cols = q_ref.shape
    cols = proj_ref.shape[1]
    part = w_ref.shape[1] // 16
    wing = cols // 2
    kvs = kv_ref.shape[1] // 2
    head = q_gain_ref.shape[1]
    kv_heads = kvs // head
    segs = lengths_ref.shape[0]
    group = q_cols // kvs
    half = tokens // 2
    span = 5 * half
    reach = kv_ref.shape[0]
    quarter = tokens // 2

    def kernel(w_hbm, nt_hbm, nt_far_hbm, q, kv, do, lengths, proj_hbm, q_gain, k_mul, x_mine_hbm, inv,
               dn_out, wg_out, sum_f, sum_c,
               w, nt, nt_far, proj, x_mine, v_one, e_all, mask, dkey, dval, kvg, kvg_in, own_kv, d, d_far, small,
               slots_f, slots_c, mine_c, far, near, far_in, near_in, cross, cross_in,
               fetch_sem, kvg_s, kvg_r, swap_s, swap_r, few_s, few_r, far_s, far_r, near_s, near_r, cross_s, cross_r):
        c, f = lax.axis_index("ctx"), lax.axis_index("fsdp")
        z, x, core = c // 4, lax.rem(c // 2, 2), lax.rem(c, 2)
        xh, y = f // 4, lax.rem(f, 4)
        ring = (
            lambda k: (c, xh * 4 + lax.rem(y + k, 4)),
            lambda k: (lax.rem(z + k, 4) * 4 + x * 2 + core, f),
        )
        across = ((c, (1 - xh) * 4 + y), (z * 4 + (1 - x) * 2 + core, f))
        twin = (z * 4 + x * 2 + 1 - core, f)
        peers_f = [(c, lax.rem(f + k, 8)) for k in range(1, 8)]
        peers_c = [(lax.rem(c + k, 16), f) for k in range(1, 16)]

        def rows_of(block):
            return pl.ds(pl.multiple_of(block * part, 16), part)

        barrier = pltpu.get_barrier_semaphore()
        partners = peers_f + peers_c
        for partner in partners:
            pl.semaphore_signal(barrier, inc=1, device_id=partner, device_id_type=MESH)
        fetches = [pltpu.make_async_copy(nt_hbm.at[rows_of(j * 2 + core)], nt.at[j], fetch_sem.at[j]) for j in range(8)]
        fetches.append(pltpu.make_async_copy(nt_far_hbm, nt_far, fetch_sem.at[8]))
        fetches.append(pltpu.make_async_copy(w_hbm, w, fetch_sem.at[9]))
        fetches.append(pltpu.make_async_copy(x_mine_hbm, x_mine, fetch_sem.at[10]))
        proj_copy = pltpu.make_async_copy(proj_hbm, proj, fetch_sem.at[11])
        for cp in [proj_copy, *fetches]:
            cp.start()

        def copy(src, dst, ss, rs, to):
            return pltpu.make_async_remote_copy(
                src_ref=src, dst_ref=dst, send_sem=ss, recv_sem=rs, device_id=to, device_id_type=MESH
            )

        sent = []

        def go(*what):
            cp = copy(*what)
            cp.start()
            sent.append(cp)
            return cp

        ones = jnp.ones((reach, head), BF16)
        for g in range(kv_heads):
            v_one[g, :, :head] = kv[:, kvs + g * head : kvs + (g + 1) * head]
            v_one[g, :, head:] = ones
        q_mul = q_gain[...] * q_scale
        first_row = c * tokens
        ends = [lengths[0]]
        for n in range(1, segs):
            ends.append(ends[-1] + lengths[n])
        for t in range(2):
            at = lax.broadcasted_iota(jnp.int32, (half, 1), 0) + (first_row + t * half)
            begun = jnp.zeros((half, 1), jnp.int32)
            for end in ends:
                begun = jnp.where(at >= end, end, begun)
            low = jnp.maximum(at - (WIN - 1), begun) - (first_row - REACH * tokens)
            col = lax.broadcasted_iota(jnp.int32, (half, span), 1) + t * half
            row = lax.broadcasted_iota(jnp.int32, (half, span), 0) + t * half
            seen = (col >= low) & (col <= row + 2 * tokens)
            mask[t] = jnp.where(seen, 1.0, 0.0).astype(BF16)
        lane = lax.broadcasted_iota(jnp.int32, (half, head), 1)

        def norm_back(grad, raw, mul):
            one = lax.rsqrt(jnp.mean(raw * raw, axis=1, keepdims=True) + epsilon)
            hat = raw * one
            up = grad * mul
            back = one * (up - hat * jnp.mean(up * hat, axis=1, keepdims=True))
            return back.astype(BF16), jnp.sum(grad * hat, axis=0, keepdims=True)

        proj_copy.wait()
        q_term = jnp.zeros((1, head), F32)
        kv_first, kv_second = [], []

        def pass_on(g):
            kv_first[g].wait_recv()
            pre = jnp.where(core == 1, kvg_in[g, 0].astype(F32), 0.0)
            kvg[g, 1] = (kvg[g, 1].astype(F32) + pre).astype(BF16)
            kv_second.append(
                go(kvg.at[g, 1], kvg_in.at[g, 1], kvg_s.at[g, 1], kvg_r.at[g, 1], (lax.rem(c + 14, 16), f))
            )

        for g in range(kv_heads):
            dkey[...] = jnp.zeros_like(dkey)
            dval[...] = jnp.zeros_like(dval)
            for r in range(group):
                if g and r == 1:
                    pass_on(g - 1)
                h = g * group + r
                hc = slice(h * head, (h + 1) * head)
                for t in range(2):
                    qs = slice(t * half, (t + 1) * half)
                    ks = slice(t * half, t * half + span)
                    qt = q[qs, hc]
                    keys = kv[ks, g * head : (g + 1) * head]
                    s = lax.dot_general(qt, keys, NT, preferred_element_type=F32)
                    e_all[...] = jnp.exp2(s).astype(BF16) * mask[t]
                    out = jnp.dot(e_all[...], v_one[g, ks, :], preferred_element_type=F32)
                    inv_l = 1.0 / out[:, head:]
                    scaled = do[qs, hc].astype(F32) * inv_l
                    delta = jnp.sum(scaled * (out[:, :head] * inv_l), axis=1, keepdims=True)
                    d_hi = delta.astype(BF16).astype(F32)
                    tail = jnp.where(lane == 0, -d_hi, jnp.where(lane == 1, d_hi - delta, 0.0))
                    scaled16 = scaled.astype(BF16)
                    both = jnp.concatenate([scaled16, tail.astype(BF16)], axis=1)
                    dp = lax.dot_general(both, v_one[g, ks, :], NT, preferred_element_type=F32)
                    ds = dp.astype(BF16) * e_all[...]
                    dq = jnp.dot(ds, keys, preferred_element_type=F32)
                    dkey[ks, :] += lax.dot_general(ds, qt, TN, preferred_element_type=F32)
                    dval[ks, :] += lax.dot_general(e_all[...], scaled16, TN, preferred_element_type=F32)
                    d[qs, hc], term_q = norm_back(dq, proj[qs, hc], q_mul)
                    q_term += term_q
            if g == 0:
                pl.semaphore_wait(barrier, len(partners))
            for n in range(2):
                away = slice((1 - n) * tokens, (2 - n) * tokens)
                kvg[g, n, :, :head] = (dkey[away, :] * (1.0 / LOG2E)).astype(BF16)
                kvg[g, n, :, head:] = dval[away, :].astype(BF16)
            kv_first.append(go(kvg.at[g, 0], kvg_in.at[g, 0], kvg_s.at[g, 0], kvg_r.at[g, 0], twin))
            own_kv[:, g * head : (g + 1) * head] = dkey[2 * tokens :, :] * (1.0 / LOG2E)
            own_kv[:, kvs + g * head : kvs + (g + 1) * head] = dval[2 * tokens :, :]
        swap_q = go(d.at[:, pl.ds(0, wing)], d_far.at[:, pl.ds(0, wing)], swap_s.at[0], swap_r.at[0], twin)

        pass_on(kv_heads - 1)

        def term(m, s, k, h):
            if m == 0:
                block = (xh if s else 1 - xh) * 4 + lax.rem(y + k, 4)
                rows = rows_of(block * 2 + h)
                total = lax.dot_general(w[0, rows, :], d[:, :wing], NT, preferred_element_type=F32)
                total += lax.dot_general(w[1, rows, :], d[:, wing:], NT, preferred_element_type=F32)
                return total
            block = lax.rem(z + k, 4) * 2 + (x if s else 1 - x)
            hs = slice(h * wing, (h + 1) * wing)
            total = jnp.dot(nt[block], d[:, hs], preferred_element_type=F32)
            total += jnp.dot(nt_far[block], d_far[:, hs], preferred_element_type=F32)
            return total * scale

        fars, nears, crossed = {}, {}, {}

        def send_far(m, s, h):
            far[m, s, h] = term(m, s, 2, h).astype(BF16)
            for n, k in enumerate((1, 3)):
                fars[m, s, h, n] = go(
                    far.at[m, s, h, :, pl.ds(n * quarter, quarter)], far_in.at[m, s, h, n],
                    far_s.at[m, s, h, n], far_r.at[m, s, h, n], ring[m](k),
                )

        def make_near(m, s, h):
            for n, k in enumerate((1, 3)):
                near[m, s, n, h] = term(m, s, k, h).astype(BF16)

        def send_near(m, s, h):
            for n, k in enumerate((1, 3)):
                fars[m, s, h, n].wait_recv()
                at = slice(n * quarter, (n + 1) * quarter)
                near[m, s, n, h, :, at] = (
                    near[m, s, n, h, :, at].astype(F32) + far_in[m, s, h, n].astype(F32)
                ).astype(BF16)
                nears[m, s, n, h] = go(
                    near.at[m, s, n, h], near_in.at[m, s, n, h], near_s.at[m, s, n, h], near_r.at[m, s, n, h], ring[m](k)
                )

        def arrived(m, s, h):
            for n in range(2):
                nears[m, s, n, h].wait_recv()
            return near_in[m, s, 0, h].astype(F32) + near_in[m, s, 1, h].astype(F32)

        def send_cross(m, h):
            mine = term(m, 0, 0, h)
            cross[m, h] = (mine + arrived(m, 0, h)).astype(BF16)
            crossed[m, h] = go(cross.at[m, h], cross_in.at[m, h], cross_s.at[m, h], cross_r.at[m, h], across[m])

        for cp in fetches[:9]:
            cp.wait()
        swap_q.wait_recv()
        send_far(1, 0, 0)
        make_near(1, 0, 0)
        send_far(1, 1, 0)
        send_near(1, 0, 0)
        make_near(1, 1, 0)

        k_term = jnp.zeros((1, head), F32)
        for cp in kv_second:
            cp.wait_recv()
        for g in range(kv_heads):
            at = slice(g * head, (g + 1) * head)
            there = slice(wing + g * head, wing + (g + 1) * head)
            grad = own_kv[:, at] + (jnp.where(core == 0, kvg_in[g, 0, :, :head].astype(F32), 0.0) + kvg_in[g, 1, :, :head].astype(F32))
            d[:, there], term_k = norm_back(grad, proj[:, there], k_mul[...])
            k_term += term_k
            at = slice(kvs + g * head, kvs + (g + 1) * head)
            grad = own_kv[:, at] + (jnp.where(core == 0, kvg_in[g, 0, :, head:].astype(F32), 0.0) + kvg_in[g, 1, :, head:].astype(F32))
            d[:, wing + kvs + g * head : wing + kvs + (g + 1) * head] = grad.astype(BF16)
        swap_kv = go(d.at[:, pl.ds(wing, wing)], d_far.at[:, pl.ds(wing, wing)], swap_s.at[1], swap_r.at[1], twin)
        fetches[9].wait()
        fetches[10].wait()
        send_far(0, 0, 0)
        make_near(0, 0, 0)
        send_far(0, 0, 1)
        swap_kv.wait_recv()
        send_far(1, 0, 1)
        send_near(0, 0, 0)
        make_near(1, 0, 1)
        make_near(0, 0, 1)
        send_cross(1, 0)
        send_far(0, 1, 0)
        send_near(0, 0, 1)
        send_near(1, 0, 1)
        send_near(1, 1, 0)
        send_far(1, 1, 1)
        make_near(0, 1, 0)

        product = d[...].astype(F32) * proj[...]
        upper = product.astype(BF16)
        lower = (product - upper.astype(F32)).astype(BF16)
        ones_row = jnp.ones((8, cols), BF16)
        dots = lax.dot_general(ones_row, upper, NT, preferred_element_type=F32)
        dots += lax.dot_general(ones_row, lower, NT, preferred_element_type=F32)
        small[...] = jnp.zeros_like(small)
        for n in range(tokens // 128):
            small[n : n + 1, :] = dots[:1, n * 128 : (n + 1) * 128]
        small[4:5, :] = q_term * (scale * q_scale)
        small[5:6, :] = k_term * scale
        slots_f[f] = small[...]
        few = [go(small, slots_f.at[f], few_s.at[k], few_r.at[k], to) for k, to in enumerate(peers_f)]

        send_cross(0, 0)
        send_far(0, 1, 1)
        send_near(0, 1, 0)
        make_near(1, 1, 1)
        send_cross(1, 1)
        make_near(0, 1, 1)
        send_near(1, 1, 1)
        send_cross(0, 1)
        send_near(0, 1, 1)
        for cp in few:
            cp.wait_recv()
        total_f = slots_f[0]
        for k in range(1, 8):
            total_f = total_f + slots_f[k]
        sum_f[...] = total_f
        for h in range(2):
            dn_out[h] = term(0, 1, 0, h)
        spread = jnp.zeros((128, 128), F32)

        def finish_weights(h):
            own_kv[:part, :] = term(1, 1, 0, h)
            crossed[1, h].wait_recv()
            total = own_kv[:part, :] + cross_in[1, h].astype(F32) + arrived(1, 1, h)
            wg_out[:, h * wing : (h + 1) * wing] = total.astype(BF16)

        finish_weights(0)
        for h in range(2):
            if h == 1:
                for cp in sent:
                    cp.wait_send()
            crossed[0, h].wait_recv()
            total = dn_out[h] + cross_in[0, h].astype(F32) + arrived(0, 1, h)
            dn_out[h] = total
            hat = x_mine[h * part : (h + 1) * part, :].astype(F32) * inv[...]
            sums = scale * jnp.sum(total * hat, axis=1, keepdims=True)
            at = lax.broadcasted_iota(jnp.int32, (part, 128), 0) + h * part
            lanes = lax.broadcasted_iota(jnp.int32, (part, 128), 1)
            to_row = jnp.where(at // 128 == lanes, sums, 0.0)
            to_lane = jnp.where(lax.rem(at, 128) == lanes, 1.0, 0.0)
            spread += lax.dot_general(to_row.astype(BF16), to_lane.astype(BF16), TN, preferred_element_type=F32)
        mine_c[...] = spread[:8]
        mine_c[6:8, :] = total_f[4:6, :]
        slots_c[c] = mine_c[...]
        few_c = [go(mine_c, slots_c.at[c], few_s.at[7 + k], few_r.at[7 + k], to) for k, to in enumerate(peers_c)]
        finish_weights(1)
        for cp in few_c:
            cp.wait_recv()
        total_c = slots_c[0]
        for k in range(1, 16):
            total_c = total_c + slots_c[k]
        sum_c[...] = total_c
        for cp in few_c:
            cp.wait_send()

    vm = pl.BlockSpec(memory_space=pltpu.VMEM)
    anywhere = pl.BlockSpec(memory_space=pl.ANY)
    dma = pltpu.SemaphoreType.DMA
    block = (2, part, tokens)
    return pl.pallas_call(
        kernel,
        out_shape=(
            jax.ShapeDtypeStruct(block, F32),
            jax.ShapeDtypeStruct((part, cols), BF16),
            jax.ShapeDtypeStruct((8, 128), F32),
            jax.ShapeDtypeStruct((8, 128), F32),
        ),
        in_specs=[anywhere] * 3 + [vm] * 3 + [pl.BlockSpec(memory_space=pltpu.SMEM), anywhere, vm, vm, anywhere, vm],
        out_specs=(vm,) * 4,
        scratch_shapes=[
            pltpu.VMEM(w_ref.shape, BF16),
            pltpu.VMEM((8, part, tokens), BF16),
            pltpu.VMEM((8, part, tokens), BF16),
            pltpu.VMEM(proj_ref.shape, F32),
            pltpu.VMEM(x_mine_ref.shape, BF16),
            pltpu.VMEM((kv_heads, reach, 2 * head), BF16),
            pltpu.VMEM((half, span), BF16),
            pltpu.VMEM((2, half, span), BF16),
            pltpu.VMEM((reach, head), F32),
            pltpu.VMEM((reach, head), F32),
            pltpu.VMEM((2, 2, tokens, 2 * head), BF16),
            pltpu.VMEM((2, 2, tokens, 2 * head), BF16),
            pltpu.VMEM((tokens, 2 * kvs), F32),
            pltpu.VMEM((tokens, cols), BF16),
            pltpu.VMEM((tokens, cols), BF16),
            pltpu.VMEM((8, 128), F32),
            pltpu.VMEM((8, 8, 128), F32),
            pltpu.VMEM((16, 8, 128), F32),
            pltpu.VMEM((8, 128), F32),
            pltpu.VMEM((2, 2) + block, BF16),
            pltpu.VMEM((2, 2, 2) + block, BF16),
            pltpu.VMEM((2, 2, 2, 2, part, quarter), BF16),
            pltpu.VMEM((2, 2, 2) + block, BF16),
            pltpu.VMEM((2,) + block, BF16),
            pltpu.VMEM((2,) + block, BF16),
            dma((12,)),
            dma((2, 2)), dma((2, 2)),
            dma((2,)), dma((2,)),
            dma((22,)), dma((22,)),
            dma((2, 2, 2, 2)), dma((2, 2, 2, 2)),
            dma((2, 2, 2, 2)), dma((2, 2, 2, 2)),
            dma((2, 2)), dma((2, 2)),
        ],
        compiler_params=pltpu.CompilerParams(
            collective_id=1, has_side_effects=True, vmem_limit_bytes=60 << 20
        ),
        name="attention_and_reductions",
    )(w_ref, nt_ref, nt_far_ref, q_ref, kv_ref, do_ref, lengths_ref, proj_ref, q_gain_ref, k_mul_ref, x_mine_ref, inv_ref)


def gather_and_project(x_ref, wq_ref, wk_ref, wv_ref, gain_ref, q_gain_ref, k_mul_ref, q_scale):
    tokens, width = x_ref.shape
    deep, q_cols = wq_ref.shape
    kv_cols = wk_ref.shape[1]
    head = q_gain_ref.shape[1]
    wing = q_cols // 2

    def kernel(x_hbm, wq, wk, wv, gain, q_gain, k_mul, w_out, nt_out, nt_far, proj, q16, kv, inv, x_mine,
               x, w_all, nt, normed, one_of, xt, own_s,
               x_s, x_r, near_s, near_r, far_s, far_r, twin_s, twin_r, swap_s, swap_r, kv_s, kv_r):
        c, f = lax.axis_index("ctx"), lax.axis_index("fsdp")
        z, xl, core = c // 4, lax.rem(c // 2, 2), lax.rem(c, 2)
        twin = (z * 4 + xl * 2 + 1 - core, f)
        mate = (z * 4 + (1 - xl) * 2 + core, f)
        along = lambda k: (lax.rem(z + k, 4) * 4 + xl * 2 + core, f)
        later = [(lax.rem(c + k, 16), f) for k in (1, 2)]
        earlier = [(lax.rem(c + 16 - k, 16), f) for k in (1, 2)]

        x_copy = pltpu.make_async_copy(x_hbm, x, own_s.at[0])
        x_copy.start()
        barrier = pltpu.get_barrier_semaphore()
        for to in [twin, mate, along(1), along(3)] + later + earlier:
            pl.semaphore_signal(barrier, inc=1, device_id=to, device_id_type=MESH)
        pl.semaphore_wait(barrier, 8)

        def rows(k, xx, who=None):
            place = lax.rem(z + k, 4) * 4 + (1 - xl if xx else xl) * 2 + (core if who is None else who)
            return pl.ds(pl.multiple_of(place * deep, 16), deep)

        def copy(src, dst, ss, rs, to):
            return pltpu.make_async_remote_copy(
                src_ref=src, dst_ref=dst, send_sem=ss, recv_sem=rs, device_id=to, device_id_type=MESH
            )

        started = []

        def go(ref, ss, rs, to):
            cp = copy(ref, ref, ss, rs, to)
            cp.start()
            started.append(cp)

        def wait_for(ref, ss, rs):
            copy(ref, ref, ss, rs, twin).wait_recv()

        def to_twin(s, k, xx):
            go(w_all.at[s, rows(k, xx)], twin_s.at[s, xx, k], twin_r.at[s, xx, k], twin)

        def to_near(s, xx):
            for n, k in enumerate((1, 3)):
                go(w_all.at[s, rows(0, xx)], near_s.at[s, xx, n], near_r.at[s, xx, n], along(k))

        def near_and_forward(s, xx):
            for n, k in enumerate((3, 1)):
                wait_for(w_all.at[s, rows(k, xx)], near_s.at[s, xx, n], near_r.at[s, xx, n])
                go(w_all.at[s, rows(k, xx), pl.ds(n * wing, wing)], far_s.at[s, xx, n], far_r.at[s, xx, n],
                   along(1 if n == 0 else 3))
                to_twin(s, k, xx)

        def far(s, xx):
            for n in range(2):
                wait_for(w_all.at[s, rows(2, xx), pl.ds(n * wing, wing)], far_s.at[s, xx, n], far_r.at[s, xx, n])
            to_twin(s, 2, xx)

        def to_mate(s):
            go(w_all.at[s, rows(0, 0)], x_s.at[s], x_r.at[s], mate)

        def from_mate(s):
            wait_for(w_all.at[s, rows(0, 1)], x_s.at[s], x_r.at[s])

        def all_from_twin(s, ks):
            for xx in range(2):
                for k in ks:
                    wait_for(w_all.at[s, rows(k, xx, 1 - core)], twin_s.at[s, xx, k], twin_r.at[s, xx, k])

        w_all[1, rows(0, 0), :kv_cols] = wk[...]
        w_all[1, rows(0, 0), kv_cols:] = wv[...]
        to_mate(1)
        to_near(1, 0)
        w_all[0, rows(0, 0), :] = wq[...]
        to_twin(1, 0, 0)

        tile = 32

        def norm_tile(i, carry):
            at = pl.ds(pl.multiple_of(i * tile, tile), tile)
            wide = x[at, :].astype(F32)
            one = lax.rsqrt(jnp.sum(wide * wide, axis=1, keepdims=True) * (1.0 / width) + epsilon)
            one_of[at, :] = jnp.broadcast_to(one, (tile, 128))
            hat = wide * one
            for j in range(width // 128):
                strip_j = slice(j * 128, (j + 1) * 128)
                normed[at, strip_j] = (hat[:, strip_j] * gain[j : j + 1, :]).astype(BF16)
            return carry

        x_copy.wait()
        lax.fori_loop(0, tokens // tile, norm_tile, 0)
        from_mate(1)
        to_near(1, 1)
        to_mate(0)
        to_twin(1, 0, 1)

        strip = 256

        def turn(i, carry):
            at = pl.ds(pl.multiple_of(i * strip, strip), strip)
            nt[at, :] = normed[:, at].T
            xt[at, :] = x[:, at].T
            return carry

        near_and_forward(1, 0)
        to_near(0, 0)
        to_twin(0, 0, 0)
        lax.fori_loop(0, width // strip, turn, 0)
        outward = [pltpu.make_async_copy(nt, nt_out, own_s.at[1])]
        outward[0].start()
        inv[...] = one_of[...].T[:1]
        x_mine[...] = xt[pl.ds(pl.multiple_of(f * (2 * deep), 16), 2 * deep), :]
        near_and_forward(1, 1)
        from_mate(0)
        to_near(0, 1)
        to_twin(0, 0, 1)
        swaps = []
        for j in range(8):
            src = pl.ds(pl.multiple_of((j * 2 + 1 - core) * deep, 16), deep)
            cp = copy(nt.at[src], nt_far.at[j], swap_s.at[j], swap_r.at[j], twin)
            cp.start()
            swaps.append(cp)
        far(1, 0)
        far(1, 1)
        all_from_twin(1, range(4))
        def to_hbm(s, at, n):
            cp = pltpu.make_async_copy(w_all.at[s, at], w_out.at[s, at], own_s.at[n])
            cp.start()
            outward.append(cp)

        to_hbm(1, pl.ds(0, width), 2)
        proj[:, q_cols:] = jnp.dot(normed[...], w_all[1], preferred_element_type=F32)

        def head_norm(raw, mul):
            one = lax.rsqrt(jnp.mean(raw * raw, axis=1, keepdims=True) + epsilon)
            return (raw * one * mul).astype(BF16)

        last = pl.ds(2 * tokens, tokens)
        for g in range(kv_cols // head):
            at = slice(q_cols + g * head, q_cols + (g + 1) * head)
            kv[last, g * head : (g + 1) * head] = head_norm(proj[:, at], k_mul[...])
        kv[last, kv_cols:] = proj[:, q_cols + kv_cols :].astype(BF16)
        passed = []
        for n in range(2):
            cp = copy(kv.at[last], kv.at[pl.ds((1 - n) * tokens, tokens)], kv_s.at[n], kv_r.at[n], later[n])
            cp.start()
            passed.append(cp)
        near_and_forward(0, 0)
        near_and_forward(0, 1)
        all_from_twin(0, (0, 1, 3))
        span = width // 2
        pair = z // 2
        near_half = pl.ds(pl.multiple_of(pair * span, 128), span)
        to_hbm(0, near_half, 3)
        proj[:, :q_cols] = jnp.dot(normed[:, near_half], w_all[0, near_half, :], preferred_element_type=F32)
        far(0, 0)
        far(0, 1)
        all_from_twin(0, (2,))
        far_half = pl.ds(pl.multiple_of((1 - pair) * span, 128), span)
        to_hbm(0, far_half, 4)
        proj[:, :q_cols] += jnp.dot(normed[:, far_half], w_all[0, far_half, :], preferred_element_type=F32)
        for h in range(q_cols // head):
            at = slice(h * head, (h + 1) * head)
            q16[:, at] = head_norm(proj[:, at], q_gain[...] * (q_scale * LOG2E))
        for cp in passed + swaps:
            cp.wait_recv()
        for cp in passed + swaps + started:
            cp.wait_send()
        for cp in outward:
            cp.wait()

    vm = pl.BlockSpec(memory_space=pltpu.VMEM)
    anywhere = pl.BlockSpec(memory_space=pl.ANY)
    dma = pltpu.SemaphoreType.DMA
    return pl.pallas_call(
        kernel,
        out_shape=(
            jax.ShapeDtypeStruct((2, width, q_cols), BF16),
            jax.ShapeDtypeStruct((width, tokens), BF16),
            jax.ShapeDtypeStruct((8, deep, tokens), BF16),
            jax.ShapeDtypeStruct((tokens, 2 * q_cols), F32),
            jax.ShapeDtypeStruct((tokens, q_cols), BF16),
            jax.ShapeDtypeStruct((3 * tokens, 2 * kv_cols), BF16),
            jax.ShapeDtypeStruct((1, tokens), F32),
            jax.ShapeDtypeStruct((2 * deep, tokens), BF16),
        ),
        in_specs=[anywhere] + [vm] * 6,
        out_specs=(anywhere,) * 3 + (vm,) * 5,
        scratch_shapes=[
            pltpu.VMEM((tokens, width), BF16),
            pltpu.VMEM((2, width, q_cols), BF16),
            pltpu.VMEM((width, tokens), BF16),
            pltpu.VMEM((tokens, width), BF16),
            pltpu.VMEM((tokens, 128), F32),
            pltpu.VMEM((width, tokens), BF16),
            dma((5,)),
            dma((2,)), dma((2,)),
            dma((2, 2, 2)), dma((2, 2, 2)),
            dma((2, 2, 2)), dma((2, 2, 2)),
            dma((2, 2, 4)), dma((2, 2, 4)),
            dma((8,)), dma((8,)),
            dma((2,)), dma((2,)),
        ],
        compiler_params=pltpu.CompilerParams(
            collective_id=2, has_side_effects=True, vmem_limit_bytes=60 << 20
        ),
        name="gather_and_project",
    )(x_ref, wq_ref, wk_ref, wv_ref, gain_ref, q_gain_ref, k_mul_ref)


def on_device(
    inputs,
    output_cotangent,
    w_query,
    key_projection,
    value_projection,
    norm_gain,
    q_gain,
    key_norm_gain,
    half_lengths,
):
    tokens = inputs.shape[0]
    model_width = inputs.shape[1]
    head_dim = q_gain.shape[0]
    q_cols = w_query.shape[1]
    kv_cols = key_projection.shape[1]
    ctx_count = lax.axis_size("ctx")
    ctx_index = lax.axis_index("ctx")
    grad_scale = float(tokens * ctx_count) ** (-0.5)
    gathered, normed_t, normed_far, projected, query_rows, kv_span, inv_row, inputs_mine = gather_and_project(
        inputs, w_query, key_projection, value_projection, norm_gain.reshape(model_width // 128, 128),
        q_gain[None], key_norm_gain[None], query_scale,
    )
    fsdp_index = lax.axis_index("fsdp")
    fsdp_count = lax.axis_size("fsdp")
    features = model_width // fsdp_count
    hat_mine = inputs_mine.astype(jnp.float32) * inv_row
    gain_mine = lax.dynamic_slice_in_dim(norm_gain, fsdp_index * features, features, 0)
    d_mine, weight_sum, sum_f, sum_c = attention_and_reductions(
        gathered, normed_t, normed_far, query_rows, kv_span, output_cotangent, half_lengths, projected,
        q_gain[None], key_norm_gain[None], inputs_mine, inv_row, grad_scale, query_scale,
    )
    d_mine = d_mine.reshape(features, tokens)
    row_dot = sum_f[:4].reshape(tokens)
    upstream = d_mine * gain_mine[:, None]
    grad_inputs = (inv_row * (upstream - hat_mine * (row_dot[None, :] / model_width))).astype(jnp.bfloat16).T
    norm_row_dots = row_dot * float(model_width) ** (-0.5)
    own_features = model_width // (fsdp_count * ctx_count)
    gain_sum = lax.dynamic_slice_in_dim(
        sum_c[:6].reshape(6 * 128), ctx_index * own_features, own_features, 0
    )
    grad_q_gain, grad_k_gain = sum_c[6], sum_c[7]
    return (
        grad_inputs,
        weight_sum[:, :q_cols],
        weight_sum[:, q_cols : q_cols + kv_cols],
        weight_sum[:, q_cols + kv_cols :],
        gain_sum,
        grad_q_gain,
        grad_k_gain,
        norm_row_dots,
    )


def solution(mesh):
    placed = (
        P("ctx", None),
        P("ctx", "fsdp"),
        P("ctx", "fsdp"),
        P("ctx", "fsdp"),
        P("ctx", "fsdp"),
        P(),
        P(),
        P(),
        P(),
    )
    return jax.shard_map(
        on_device,
        mesh=mesh,
        in_specs=placed,
        out_specs=(
            P("ctx", "fsdp"),
            P("ctx", "fsdp"),
            P("ctx", "fsdp"),
            P("ctx", "fsdp"),
            P(("fsdp", "ctx")),
            P(),
            P(),
            P("ctx"),
        ),
        check_vma=False,
    )
```

```python
import jax
import jax.numpy as jnp
from jax import lax
from jax.experimental import pallas as pl
from jax.experimental.pallas import tpu as pltpu
from jax.sharding import PartitionSpec as P

WIN = 1024
REACH = 2


epsilon = 1e-06
query_scale = 168.0 ** (-0.5)


F32, BF16 = jnp.float32, jnp.bfloat16
NT = (((1,), (1,)), ((), ()))
TN = (((0,), (0,)), ((), ()))
MESH = pl.DeviceIdType.MESH
LOG2E = 1.4426950408889634


def attention_and_reductions(w_ref, nt_ref, nt_far_ref, q_ref, kv_ref, do_ref, lengths_ref, proj_ref, q_gain_ref, k_mul_ref,
                             x_mine_ref, inv_ref, scale, q_scale):
    tokens, q_cols = q_ref.shape
    cols = proj_ref.shape[1]
    part = w_ref.shape[1] // 16
    wing = cols // 2
    kvs = kv_ref.shape[1] // 2
    head = q_gain_ref.shape[1]
    kv_heads = kvs // head
    segs = lengths_ref.shape[0]
    group = q_cols // kvs
    half = tokens // 2
    span = 5 * half
    reach = kv_ref.shape[0]
    quarter = tokens // 2

    def kernel(w_hbm, nt_hbm, nt_far_hbm, q, kv, do, lengths, proj_hbm, q_gain, k_mul, x_mine_hbm, inv,
               dn_out, wg_out, sum_f, sum_c,
               w, nt, nt_far, proj, x_mine, v_one, e_all, mask, dkey, dval, kvg, kvg_in, own_kv, d, d_far, small,
               slots_f, slots_c, mine_c, far, near, far_in, near_in, cross, cross_in,
               fetch_sem, kvg_s, kvg_r, swap_s, swap_r, few_s, few_r, far_s, far_r, near_s, near_r, cross_s, cross_r):
        c, f = lax.axis_index("ctx"), lax.axis_index("fsdp")
        z, x, core = c // 4, lax.rem(c // 2, 2), lax.rem(c, 2)
        xh, y = f // 4, lax.rem(f, 4)
        ring = (
            lambda k: (c, xh * 4 + lax.rem(y + k, 4)),
            lambda k: (lax.rem(z + k, 4) * 4 + x * 2 + core, f),
        )
        across = ((c, (1 - xh) * 4 + y), (z * 4 + (1 - x) * 2 + core, f))
        twin = (z * 4 + x * 2 + 1 - core, f)
        peers_f = [(c, lax.rem(f + k, 8)) for k in range(1, 8)]
        peers_c = [(lax.rem(c + k, 16), f) for k in range(1, 16)]

        def rows_of(block):
            return pl.ds(pl.multiple_of(block * part, 16), part)

        barrier = pltpu.get_barrier_semaphore()
        partners = peers_f + peers_c
        for partner in partners:
            pl.semaphore_signal(barrier, inc=1, device_id=partner, device_id_type=MESH)
        fetches = [pltpu.make_async_copy(nt_hbm.at[rows_of(j * 2 + core)], nt.at[j], fetch_sem.at[j]) for j in range(8)]
        fetches.append(pltpu.make_async_copy(nt_far_hbm, nt_far, fetch_sem.at[8]))
        fetches.append(pltpu.make_async_copy(w_hbm, w, fetch_sem.at[9]))
        fetches.append(pltpu.make_async_copy(x_mine_hbm, x_mine, fetch_sem.at[10]))
        proj_copy = pltpu.make_async_copy(proj_hbm, proj, fetch_sem.at[11])
        for cp in [proj_copy, *fetches]:
            cp.start()

        def copy(src, dst, ss, rs, to):
            return pltpu.make_async_remote_copy(
                src_ref=src, dst_ref=dst, send_sem=ss, recv_sem=rs, device_id=to, device_id_type=MESH
            )

        sent = []

        def go(*what):
            cp = copy(*what)
            cp.start()
            sent.append(cp)
            return cp

        ones = jnp.ones((reach, head), BF16)
        for g in range(kv_heads):
            v_one[g, :, :head] = kv[:, kvs + g * head : kvs + (g + 1) * head]
            v_one[g, :, head:] = ones
        q_mul = q_gain[...] * q_scale
        first_row = c * tokens
        ends = [lengths[0]]
        for n in range(1, segs):
            ends.append(ends[-1] + lengths[n])
        for t in range(2):
            at = lax.broadcasted_iota(jnp.int32, (half, 1), 0) + (first_row + t * half)
            begun = jnp.zeros((half, 1), jnp.int32)
            for end in ends:
                begun = jnp.where(at >= end, end, begun)
            low = jnp.maximum(at - (WIN - 1), begun) - (first_row - REACH * tokens)
            col = lax.broadcasted_iota(jnp.int32, (half, span), 1) + t * half
            row = lax.broadcasted_iota(jnp.int32, (half, span), 0) + t * half
            seen = (col >= low) & (col <= row + 2 * tokens)
            mask[t] = jnp.where(seen, 1.0, 0.0).astype(BF16)
        lane = lax.broadcasted_iota(jnp.int32, (half, head), 1)

        def norm_back(grad, raw, mul):
            one = lax.rsqrt(jnp.mean(raw * raw, axis=1, keepdims=True) + epsilon)
            hat = raw * one
            up = grad * mul
            back = one * (up - hat * jnp.mean(up * hat, axis=1, keepdims=True))
            return back.astype(BF16), jnp.sum(grad * hat, axis=0, keepdims=True)

        proj_copy.wait()
        q_term = jnp.zeros((1, head), F32)
        kv_first, kv_second = [], []

        def pass_on(g):
            kv_first[g].wait_recv()
            pre = jnp.where(core == 1, kvg_in[g, 0].astype(F32), 0.0)
            kvg[g, 1] = (kvg[g, 1].astype(F32) + pre).astype(BF16)
            kv_second.append(
                go(kvg.at[g, 1], kvg_in.at[g, 1], kvg_s.at[g, 1], kvg_r.at[g, 1], (lax.rem(c + 14, 16), f))
            )

        for g in range(kv_heads):
            dkey[...] = jnp.zeros_like(dkey)
            dval[...] = jnp.zeros_like(dval)
            for r in range(group):
                if g and r == 1:
                    pass_on(g - 1)
                h = g * group + r
                hc = slice(h * head, (h + 1) * head)
                for t in range(2):
                    qs = slice(t * half, (t + 1) * half)
                    ks = slice(t * half, t * half + span)
                    qt = q[qs, hc]
                    keys = kv[ks, g * head : (g + 1) * head]
                    s = lax.dot_general(qt, keys, NT, preferred_element_type=F32)
                    e_all[...] = jnp.exp2(s).astype(BF16) * mask[t]
                    out = jnp.dot(e_all[...], v_one[g, ks, :], preferred_element_type=F32)
                    inv_l = 1.0 / out[:, head:]
                    scaled = do[qs, hc].astype(F32) * inv_l
                    delta = jnp.sum(scaled * (out[:, :head] * inv_l), axis=1, keepdims=True)
                    d_hi = delta.astype(BF16).astype(F32)
                    tail = jnp.where(lane == 0, -d_hi, jnp.where(lane == 1, d_hi - delta, 0.0))
                    scaled16 = scaled.astype(BF16)
                    both = jnp.concatenate([scaled16, tail.astype(BF16)], axis=1)
                    dp = lax.dot_general(both, v_one[g, ks, :], NT, preferred_element_type=F32)
                    ds = dp.astype(BF16) * e_all[...]
                    dq = jnp.dot(ds, keys, preferred_element_type=F32)
                    dkey[ks, :] += lax.dot_general(ds, qt, TN, preferred_element_type=F32)
                    dval[ks, :] += lax.dot_general(e_all[...], scaled16, TN, preferred_element_type=F32)
                    d[qs, hc], term_q = norm_back(dq, proj[qs, hc], q_mul)
                    q_term += term_q
            if g == 0:
                pl.semaphore_wait(barrier, len(partners))
            for n in range(2):
                away = slice((1 - n) * tokens, (2 - n) * tokens)
                kvg[g, n, :, :head] = (dkey[away, :] * (1.0 / LOG2E)).astype(BF16)
                kvg[g, n, :, head:] = dval[away, :].astype(BF16)
            kv_first.append(go(kvg.at[g, 0], kvg_in.at[g, 0], kvg_s.at[g, 0], kvg_r.at[g, 0], twin))
            own_kv[:, g * head : (g + 1) * head] = dkey[2 * tokens :, :] * (1.0 / LOG2E)
            own_kv[:, kvs + g * head : kvs + (g + 1) * head] = dval[2 * tokens :, :]
        swap_q = go(d.at[:, pl.ds(0, wing)], d_far.at[:, pl.ds(0, wing)], swap_s.at[0], swap_r.at[0], twin)

        pass_on(kv_heads - 1)

        def term(m, s, k, h):
            if m == 0:
                block = (xh if s else 1 - xh) * 4 + lax.rem(y + k, 4)
                rows = rows_of(block * 2 + h)
                total = lax.dot_general(w[0, rows, :], d[:, :wing], NT, preferred_element_type=F32)
                total += lax.dot_general(w[1, rows, :], d[:, wing:], NT, preferred_element_type=F32)
                return total
            block = lax.rem(z + k, 4) * 2 + (x if s else 1 - x)
            hs = slice(h * wing, (h + 1) * wing)
            total = jnp.dot(nt[block], d[:, hs], preferred_element_type=F32)
            total += jnp.dot(nt_far[block], d_far[:, hs], preferred_element_type=F32)
            return total * scale

        fars, nears, crossed = {}, {}, {}

        def send_far(m, s, h):
            far[m, s, h] = term(m, s, 2, h).astype(BF16)
            for n, k in enumerate((1, 3)):
                fars[m, s, h, n] = go(
                    far.at[m, s, h, :, pl.ds(n * quarter, quarter)], far_in.at[m, s, h, n],
                    far_s.at[m, s, h, n], far_r.at[m, s, h, n], ring[m](k),
                )

        def make_near(m, s, h):
            for n, k in enumerate((1, 3)):
                near[m, s, n, h] = term(m, s, k, h).astype(BF16)

        def send_near(m, s, h):
            for n, k in enumerate((1, 3)):
                fars[m, s, h, n].wait_recv()
                at = slice(n * quarter, (n + 1) * quarter)
                near[m, s, n, h, :, at] = (
                    near[m, s, n, h, :, at].astype(F32) + far_in[m, s, h, n].astype(F32)
                ).astype(BF16)
                nears[m, s, n, h] = go(
                    near.at[m, s, n, h], near_in.at[m, s, n, h], near_s.at[m, s, n, h], near_r.at[m, s, n, h], ring[m](k)
                )

        def arrived(m, s, h):
            for n in range(2):
                nears[m, s, n, h].wait_recv()
            return near_in[m, s, 0, h].astype(F32) + near_in[m, s, 1, h].astype(F32)

        def send_cross(m, h):
            mine = term(m, 0, 0, h)
            cross[m, h] = (mine + arrived(m, 0, h)).astype(BF16)
            crossed[m, h] = go(cross.at[m, h], cross_in.at[m, h], cross_s.at[m, h], cross_r.at[m, h], across[m])

        for cp in fetches[:9]:
            cp.wait()
        swap_q.wait_recv()
        send_far(1, 0, 0)
        make_near(1, 0, 0)
        send_far(1, 1, 0)
        send_near(1, 0, 0)
        make_near(1, 1, 0)

        k_term = jnp.zeros((1, head), F32)
        for cp in kv_second:
            cp.wait_recv()
        for g in range(kv_heads):
            at = slice(g * head, (g + 1) * head)
            there = slice(wing + g * head, wing + (g + 1) * head)
            grad = own_kv[:, at] + (jnp.where(core == 0, kvg_in[g, 0, :, :head].astype(F32), 0.0) + kvg_in[g, 1, :, :head].astype(F32))
            d[:, there], term_k = norm_back(grad, proj[:, there], k_mul[...])
            k_term += term_k
            at = slice(kvs + g * head, kvs + (g + 1) * head)
            grad = own_kv[:, at] + (jnp.where(core == 0, kvg_in[g, 0, :, head:].astype(F32), 0.0) + kvg_in[g, 1, :, head:].astype(F32))
            d[:, wing + kvs + g * head : wing + kvs + (g + 1) * head] = grad.astype(BF16)
        swap_kv = go(d.at[:, pl.ds(wing, wing)], d_far.at[:, pl.ds(wing, wing)], swap_s.at[1], swap_r.at[1], twin)
        fetches[9].wait()
        fetches[10].wait()
        send_far(0, 0, 0)
        make_near(0, 0, 0)
        send_far(0, 0, 1)
        swap_kv.wait_recv()
        send_far(1, 0, 1)
        send_near(0, 0, 0)
        make_near(1, 0, 1)
        make_near(0, 0, 1)
        send_cross(1, 0)
        send_far(0, 1, 0)
        send_near(0, 0, 1)
        send_near(1, 0, 1)
        send_near(1, 1, 0)
        send_far(1, 1, 1)
        make_near(0, 1, 0)

        product = d[...].astype(F32) * proj[...]
        upper = product.astype(BF16)
        lower = (product - upper.astype(F32)).astype(BF16)
        ones_row = jnp.ones((8, cols), BF16)
        dots = lax.dot_general(ones_row, upper, NT, preferred_element_type=F32)
        dots += lax.dot_general(ones_row, lower, NT, preferred_element_type=F32)
        small[...] = jnp.zeros_like(small)
        for n in range(tokens // 128):
            small[n : n + 1, :] = dots[:1, n * 128 : (n + 1) * 128]
        small[4:5, :] = q_term * (scale * q_scale)
        small[5:6, :] = k_term * scale
        slots_f[f] = small[...]
        few = [go(small, slots_f.at[f], few_s.at[k], few_r.at[k], to) for k, to in enumerate(peers_f)]

        send_cross(0, 0)
        send_far(0, 1, 1)
        send_near(0, 1, 0)
        make_near(1, 1, 1)
        send_cross(1, 1)
        make_near(0, 1, 1)
        send_near(1, 1, 1)
        send_cross(0, 1)
        send_near(0, 1, 1)
        for cp in few:
            cp.wait_recv()
        total_f = slots_f[0]
        for k in range(1, 8):
            total_f = total_f + slots_f[k]
        sum_f[...] = total_f
        for h in range(2):
            dn_out[h] = term(0, 1, 0, h)
        spread = jnp.zeros((128, 128), F32)

        def finish_weights(h):
            own_kv[:part, :] = term(1, 1, 0, h)
            crossed[1, h].wait_recv()
            total = own_kv[:part, :] + cross_in[1, h].astype(F32) + arrived(1, 1, h)
            wg_out[:, h * wing : (h + 1) * wing] = total.astype(BF16)

        finish_weights(0)
        for h in range(2):
            if h == 1:
                for cp in sent:
                    cp.wait_send()
            crossed[0, h].wait_recv()
            total = dn_out[h] + cross_in[0, h].astype(F32) + arrived(0, 1, h)
            dn_out[h] = total
            hat = x_mine[h * part : (h + 1) * part, :].astype(F32) * inv[...]
            sums = scale * jnp.sum(total * hat, axis=1, keepdims=True)
            at = lax.broadcasted_iota(jnp.int32, (part, 128), 0) + h * part
            lanes = lax.broadcasted_iota(jnp.int32, (part, 128), 1)
            to_row = jnp.where(at // 128 == lanes, sums, 0.0)
            to_lane = jnp.where(lax.rem(at, 128) == lanes, 1.0, 0.0)
            spread += lax.dot_general(to_row.astype(BF16), to_lane.astype(BF16), TN, preferred_element_type=F32)
        mine_c[...] = spread[:8]
        mine_c[6:8, :] = total_f[4:6, :]
        slots_c[c] = mine_c[...]
        few_c = [go(mine_c, slots_c.at[c], few_s.at[7 + k], few_r.at[7 + k], to) for k, to in enumerate(peers_c)]
        finish_weights(1)
        for cp in few_c:
            cp.wait_recv()
        total_c = slots_c[0]
        for k in range(1, 16):
            total_c = total_c + slots_c[k]
        sum_c[...] = total_c
        for cp in few_c:
            cp.wait_send()

    vm = pl.BlockSpec(memory_space=pltpu.VMEM)
    anywhere = pl.BlockSpec(memory_space=pl.ANY)
    dma = pltpu.SemaphoreType.DMA
    block = (2, part, tokens)
    return pl.pallas_call(
        kernel,
        out_shape=(
            jax.ShapeDtypeStruct(block, F32),
            jax.ShapeDtypeStruct((part, cols), BF16),
            jax.ShapeDtypeStruct((8, 128), F32),
            jax.ShapeDtypeStruct((8, 128), F32),
        ),
        in_specs=[anywhere] * 3 + [vm] * 3 + [pl.BlockSpec(memory_space=pltpu.SMEM), anywhere, vm, vm, anywhere, vm],
        out_specs=(vm,) * 4,
        scratch_shapes=[
            pltpu.VMEM(w_ref.shape, BF16),
            pltpu.VMEM((8, part, tokens), BF16),
            pltpu.VMEM((8, part, tokens), BF16),
            pltpu.VMEM(proj_ref.shape, F32),
            pltpu.VMEM(x_mine_ref.shape, BF16),
            pltpu.VMEM((kv_heads, reach, 2 * head), BF16),
            pltpu.VMEM((half, span), BF16),
            pltpu.VMEM((2, half, span), BF16),
            pltpu.VMEM((reach, head), F32),
            pltpu.VMEM((reach, head), F32),
            pltpu.VMEM((2, 2, tokens, 2 * head), BF16),
            pltpu.VMEM((2, 2, tokens, 2 * head), BF16),
            pltpu.VMEM((tokens, 2 * kvs), F32),
            pltpu.VMEM((tokens, cols), BF16),
            pltpu.VMEM((tokens, cols), BF16),
            pltpu.VMEM((8, 128), F32),
            pltpu.VMEM((8, 8, 128), F32),
            pltpu.VMEM((16, 8, 128), F32),
            pltpu.VMEM((8, 128), F32),
            pltpu.VMEM((2, 2) + block, BF16),
            pltpu.VMEM((2, 2, 2) + block, BF16),
            pltpu.VMEM((2, 2, 2, 2, part, quarter), BF16),
            pltpu.VMEM((2, 2, 2) + block, BF16),
            pltpu.VMEM((2,) + block, BF16),
            pltpu.VMEM((2,) + block, BF16),
            dma((12,)),
            dma((2, 2)), dma((2, 2)),
            dma((2,)), dma((2,)),
            dma((22,)), dma((22,)),
            dma((2, 2, 2, 2)), dma((2, 2, 2, 2)),
            dma((2, 2, 2, 2)), dma((2, 2, 2, 2)),
            dma((2, 2)), dma((2, 2)),
        ],
        compiler_params=pltpu.CompilerParams(
            collective_id=1, has_side_effects=True, vmem_limit_bytes=60 << 20
        ),
        name="attention_and_reductions",
    )(w_ref, nt_ref, nt_far_ref, q_ref, kv_ref, do_ref, lengths_ref, proj_ref, q_gain_ref, k_mul_ref, x_mine_ref, inv_ref)


def gather_and_project(x_ref, wq_ref, wk_ref, wv_ref, gain_ref, q_gain_ref, k_mul_ref, q_scale):
    tokens, width = x_ref.shape
    deep, q_cols = wq_ref.shape
    kv_cols = wk_ref.shape[1]
    head = q_gain_ref.shape[1]
    wing = q_cols // 2

    def kernel(x_hbm, wq, wk, wv, gain, q_gain, k_mul, w_out, nt_out, nt_far, proj, q16, kv, inv, x_mine,
               x, w_all, nt, normed, one_of, xt, own_s,
               x_s, x_r, near_s, near_r, far_s, far_r, twin_s, twin_r, swap_s, swap_r, kv_s, kv_r):
        c, f = lax.axis_index("ctx"), lax.axis_index("fsdp")
        z, xl, core = c // 4, lax.rem(c // 2, 2), lax.rem(c, 2)
        twin = (z * 4 + xl * 2 + 1 - core, f)
        mate = (z * 4 + (1 - xl) * 2 + core, f)
        along = lambda k: (lax.rem(z + k, 4) * 4 + xl * 2 + core, f)
        later = [(lax.rem(c + k, 16), f) for k in (1, 2)]
        earlier = [(lax.rem(c + 16 - k, 16), f) for k in (1, 2)]

        x_copy = pltpu.make_async_copy(x_hbm, x, own_s.at[0])
        x_copy.start()
        barrier = pltpu.get_barrier_semaphore()
        for to in [twin, mate, along(1), along(3)] + later + earlier:
            pl.semaphore_signal(barrier, inc=1, device_id=to, device_id_type=MESH)
        pl.semaphore_wait(barrier, 8)

        def rows(k, xx, who=None):
            place = lax.rem(z + k, 4) * 4 + (1 - xl if xx else xl) * 2 + (core if who is None else who)
            return pl.ds(pl.multiple_of(place * deep, 16), deep)

        def copy(src, dst, ss, rs, to):
            return pltpu.make_async_remote_copy(
                src_ref=src, dst_ref=dst, send_sem=ss, recv_sem=rs, device_id=to, device_id_type=MESH
            )

        started = []

        def go(ref, ss, rs, to):
            cp = copy(ref, ref, ss, rs, to)
            cp.start()
            started.append(cp)

        def wait_for(ref, ss, rs):
            copy(ref, ref, ss, rs, twin).wait_recv()

        def to_twin(s, k, xx):
            go(w_all.at[s, rows(k, xx)], twin_s.at[s, xx, k], twin_r.at[s, xx, k], twin)

        def to_near(s, xx):
            for n, k in enumerate((1, 3)):
                go(w_all.at[s, rows(0, xx)], near_s.at[s, xx, n], near_r.at[s, xx, n], along(k))

        def near_and_forward(s, xx):
            for n, k in enumerate((3, 1)):
                wait_for(w_all.at[s, rows(k, xx)], near_s.at[s, xx, n], near_r.at[s, xx, n])
                go(w_all.at[s, rows(k, xx), pl.ds(n * wing, wing)], far_s.at[s, xx, n], far_r.at[s, xx, n],
                   along(1 if n == 0 else 3))
                to_twin(s, k, xx)

        def far(s, xx):
            for n in range(2):
                wait_for(w_all.at[s, rows(2, xx), pl.ds(n * wing, wing)], far_s.at[s, xx, n], far_r.at[s, xx, n])
            to_twin(s, 2, xx)

        def to_mate(s):
            go(w_all.at[s, rows(0, 0)], x_s.at[s], x_r.at[s], mate)

        def from_mate(s):
            wait_for(w_all.at[s, rows(0, 1)], x_s.at[s], x_r.at[s])

        def all_from_twin(s, ks):
            for xx in range(2):
                for k in ks:
                    wait_for(w_all.at[s, rows(k, xx, 1 - core)], twin_s.at[s, xx, k], twin_r.at[s, xx, k])

        w_all[1, rows(0, 0), :kv_cols] = wk[...]
        w_all[1, rows(0, 0), kv_cols:] = wv[...]
        to_mate(1)
        to_near(1, 0)
        w_all[0, rows(0, 0), :] = wq[...]
        to_twin(1, 0, 0)

        tile = 32

        def norm_tile(i, carry):
            at = pl.ds(pl.multiple_of(i * tile, tile), tile)
            wide = x[at, :].astype(F32)
            one = lax.rsqrt(jnp.sum(wide * wide, axis=1, keepdims=True) * (1.0 / width) + epsilon)
            one_of[at, :] = jnp.broadcast_to(one, (tile, 128))
            hat = wide * one
            for j in range(width // 128):
                strip_j = slice(j * 128, (j + 1) * 128)
                normed[at, strip_j] = (hat[:, strip_j] * gain[j : j + 1, :]).astype(BF16)
            return carry

        x_copy.wait()
        lax.fori_loop(0, tokens // tile, norm_tile, 0)
        from_mate(1)
        to_near(1, 1)
        to_mate(0)
        to_twin(1, 0, 1)

        strip = 256

        def turn(i, carry):
            at = pl.ds(pl.multiple_of(i * strip, strip), strip)
            nt[at, :] = normed[:, at].T
            xt[at, :] = x[:, at].T
            return carry

        near_and_forward(1, 0)
        lax.fori_loop(0, width // strip, turn, 0)
        outward = [pltpu.make_async_copy(nt, nt_out, own_s.at[1])]
        outward[0].start()
        inv[...] = one_of[...].T[:1]
        x_mine[...] = xt[pl.ds(pl.multiple_of(f * (2 * deep), 16), 2 * deep), :]
        near_and_forward(1, 1)
        to_near(0, 0)
        to_twin(0, 0, 0)
        from_mate(0)
        swaps = []
        for j in range(8):
            src = pl.ds(pl.multiple_of((j * 2 + 1 - core) * deep, 16), deep)
            cp = copy(nt.at[src], nt_far.at[j], swap_s.at[j], swap_r.at[j], twin)
            cp.start()
            swaps.append(cp)
        far(1, 0)
        to_near(0, 1)
        to_twin(0, 0, 1)
        far(1, 1)
        all_from_twin(1, range(4))
        def to_hbm(s, at, n):
            cp = pltpu.make_async_copy(w_all.at[s, at], w_out.at[s, at], own_s.at[n])
            cp.start()
            outward.append(cp)

        to_hbm(1, pl.ds(0, width), 2)
        proj[:, q_cols:] = jnp.dot(normed[...], w_all[1], preferred_element_type=F32)

        def head_norm(raw, mul):
            one = lax.rsqrt(jnp.mean(raw * raw, axis=1, keepdims=True) + epsilon)
            return (raw * one * mul).astype(BF16)

        last = pl.ds(2 * tokens, tokens)
        for g in range(kv_cols // head):
            at = slice(q_cols + g * head, q_cols + (g + 1) * head)
            kv[last, g * head : (g + 1) * head] = head_norm(proj[:, at], k_mul[...])
        kv[last, kv_cols:] = proj[:, q_cols + kv_cols :].astype(BF16)
        passed = []
        for n in range(2):
            cp = copy(kv.at[last], kv.at[pl.ds((1 - n) * tokens, tokens)], kv_s.at[n], kv_r.at[n], later[n])
            cp.start()
            passed.append(cp)
        near_and_forward(0, 0)
        near_and_forward(0, 1)
        all_from_twin(0, (0, 1, 3))
        span = width // 2
        pair = z // 2
        near_half = pl.ds(pl.multiple_of(pair * span, 128), span)
        to_hbm(0, near_half, 3)
        proj[:, :q_cols] = jnp.dot(normed[:, near_half], w_all[0, near_half, :], preferred_element_type=F32)
        far(0, 0)
        far(0, 1)
        all_from_twin(0, (2,))
        far_half = pl.ds(pl.multiple_of((1 - pair) * span, 128), span)
        to_hbm(0, far_half, 4)
        proj[:, :q_cols] += jnp.dot(normed[:, far_half], w_all[0, far_half, :], preferred_element_type=F32)
        for h in range(q_cols // head):
            at = slice(h * head, (h + 1) * head)
            q16[:, at] = head_norm(proj[:, at], q_gain[...] * (q_scale * LOG2E))
        for cp in passed + swaps:
            cp.wait_recv()
        for cp in passed + swaps + started:
            cp.wait_send()
        for cp in outward:
            cp.wait()

    vm = pl.BlockSpec(memory_space=pltpu.VMEM)
    anywhere = pl.BlockSpec(memory_space=pl.ANY)
    dma = pltpu.SemaphoreType.DMA
    return pl.pallas_call(
        kernel,
        out_shape=(
            jax.ShapeDtypeStruct((2, width, q_cols), BF16),
            jax.ShapeDtypeStruct((width, tokens), BF16),
            jax.ShapeDtypeStruct((8, deep, tokens), BF16),
            jax.ShapeDtypeStruct((tokens, 2 * q_cols), F32),
            jax.ShapeDtypeStruct((tokens, q_cols), BF16),
            jax.ShapeDtypeStruct((3 * tokens, 2 * kv_cols), BF16),
            jax.ShapeDtypeStruct((1, tokens), F32),
            jax.ShapeDtypeStruct((2 * deep, tokens), BF16),
        ),
        in_specs=[anywhere] + [vm] * 6,
        out_specs=(anywhere,) * 3 + (vm,) * 5,
        scratch_shapes=[
            pltpu.VMEM((tokens, width), BF16),
            pltpu.VMEM((2, width, q_cols), BF16),
            pltpu.VMEM((width, tokens), BF16),
            pltpu.VMEM((tokens, width), BF16),
            pltpu.VMEM((tokens, 128), F32),
            pltpu.VMEM((width, tokens), BF16),
            dma((5,)),
            dma((2,)), dma((2,)),
            dma((2, 2, 2)), dma((2, 2, 2)),
            dma((2, 2, 2)), dma((2, 2, 2)),
            dma((2, 2, 4)), dma((2, 2, 4)),
            dma((8,)), dma((8,)),
            dma((2,)), dma((2,)),
        ],
        compiler_params=pltpu.CompilerParams(
            collective_id=2, has_side_effects=True, vmem_limit_bytes=60 << 20
        ),
        name="gather_and_project",
    )(x_ref, wq_ref, wk_ref, wv_ref, gain_ref, q_gain_ref, k_mul_ref)


def on_device(
    inputs,
    output_cotangent,
    w_query,
    key_projection,
    value_projection,
    norm_gain,
    q_gain,
    key_norm_gain,
    half_lengths,
):
    tokens = inputs.shape[0]
    model_width = inputs.shape[1]
    head_dim = q_gain.shape[0]
    q_cols = w_query.shape[1]
    kv_cols = key_projection.shape[1]
    ctx_count = lax.axis_size("ctx")
    ctx_index = lax.axis_index("ctx")
    grad_scale = float(tokens * ctx_count) ** (-0.5)
    gathered, normed_t, normed_far, projected, query_rows, kv_span, inv_row, inputs_mine = gather_and_project(
        inputs, w_query, key_projection, value_projection, norm_gain.reshape(model_width // 128, 128),
        q_gain[None], key_norm_gain[None], query_scale,
    )
    fsdp_index = lax.axis_index("fsdp")
    fsdp_count = lax.axis_size("fsdp")
    features = model_width // fsdp_count
    hat_mine = inputs_mine.astype(jnp.float32) * inv_row
    gain_mine = lax.dynamic_slice_in_dim(norm_gain, fsdp_index * features, features, 0)
    d_mine, weight_sum, sum_f, sum_c = attention_and_reductions(
        gathered, normed_t, normed_far, query_rows, kv_span, output_cotangent, half_lengths, projected,
        q_gain[None], key_norm_gain[None], inputs_mine, inv_row, grad_scale, query_scale,
    )
    d_mine = d_mine.reshape(features, tokens)
    row_dot = sum_f[:4].reshape(tokens)
    upstream = d_mine * gain_mine[:, None]
    grad_inputs = (inv_row * (upstream - hat_mine * (row_dot[None, :] / model_width))).astype(jnp.bfloat16).T
    norm_row_dots = row_dot * float(model_width) ** (-0.5)
    own_features = model_width // (fsdp_count * ctx_count)
    gain_sum = lax.dynamic_slice_in_dim(
        sum_c[:6].reshape(6 * 128), ctx_index * own_features, own_features, 0
    )
    grad_q_gain, grad_k_gain = sum_c[6], sum_c[7]
    return (
        grad_inputs,
        weight_sum[:, :q_cols],
        weight_sum[:, q_cols : q_cols + kv_cols],
        weight_sum[:, q_cols + kv_cols :],
        gain_sum,
        grad_q_gain,
        grad_k_gain,
        norm_row_dots,
    )


def solution(mesh):
    placed = (
        P("ctx", None),
        P("ctx", "fsdp"),
        P("ctx", "fsdp"),
        P("ctx", "fsdp"),
        P("ctx", "fsdp"),
        P(),
        P(),
        P(),
        P(),
    )
    return jax.shard_map(
        on_device,
        mesh=mesh,
        in_specs=placed,
        out_specs=(
            P("ctx", "fsdp"),
            P("ctx", "fsdp"),
            P("ctx", "fsdp"),
            P("ctx", "fsdp"),
            P(("fsdp", "ctx")),
            P(),
            P(),
            P("ctx"),
        ),
        check_vma=False,
    )
```
